256 devices in a mesh: tm: 16 (over x, z_lo, core), space: 16 (over z_hi, y).
Axes of the slice: x: 4, y: 4, z: 8 (z_hi: 4, z_lo: 2; z = z_hi * 2 + z_lo), core: 2. Of those that a mesh axis runs over, the one named last changes fastest.
Arguments:
- activations: bfloat16 [32, 32, 192, 512], P('tm', 'space'), may hold values from -6 to 6
- cotangent: bfloat16 [32, 32, 192, 512], P('tm', 'space'), may hold values from -6 to 6
- spatial_kernel: bfloat16 [512, 9, 512], P('space'), may hold values from -0.09375 to 0.09375
- temporal_kernel: bfloat16 [512, 3, 512], P('space'), may hold values from -0.15625 to 0.15625
Outputs:
- grad_input: float32 [32, 32, 192, 512], P('tm', 'space')
- grad_spatial: float32 [512, 9, 512], P('space')
- grad_temporal: float32 [512, 3, 512], P('space')
The draws below stay inside these ranges and needn't reach their ends.
All inputs are finite; a program needn't handle non-finite values.
Results may differ from the reference program's by a relative error of at most 0.0029.
Values may be sent and summed in bfloat16 or wider, within the bound.
No kernel may reach another device: no remote copies, remote signals or barrier semaphores. Data moves between devices by JAX's collectives and lax.ppermute only.
A program may use at most 128 MiB of HBM per device.

```python
import math
import jax
import jax.numpy as jnp
from jax import lax

CHANNELS = 512
WIDTH = 192
FRAMES = 32
HEIGHT = 32


def raised(entries, key, source, target, blocks, factor):
    owner, partner = [(jnp.arange(entries.shape[dim]) // (entries.shape[dim] // blocks)).reshape([-1 if axis == dim else 1 for axis in range(entries.ndim)]) for dim in (source, target)]
    chosen = jax.random.permutation(key, blocks)[partner]
    strong = (owner == chosen) | (owner == (partner + blocks // 2) % blocks)
    return jnp.where(strong, factor * entries, entries)


def level_of(rng, dims, cuts, smallest, top_value):
    loudness, own = 1.0, jax.random.fold_in(rng, 6)
    for axis_at, blocks in cuts:
        draws = jnp.exp(jax.random.uniform(jax.random.fold_in(own, axis_at), (blocks,), jnp.float32, smallest / len(cuts), top_value / len(cuts)))
        loudness = loudness * jnp.repeat(draws, dims[axis_at] // blocks).reshape([-1 if axis == axis_at else 1 for axis in range(len(dims))])
    return loudness


def centred(own_key, dims, scale, bound, cuts=(), held_as=jnp.bfloat16):
    drawn = scale * jax.random.normal(own_key, dims, jnp.float32)
    if cuts:
        drawn = drawn * level_of(own_key, dims, cuts, -0.22, 0.18)
    return jnp.clip(drawn, -bound, bound).astype(held_as)


def bell_draw_with(stream_key, extent, scale, bound, cuts, heavy, kind=jnp.bfloat16):
    values = scale * jax.random.normal(stream_key, extent, jnp.float32)
    if cuts:
        values = values * level_of(stream_key, extent, cuts, -0.22, 0.18)
    return jnp.clip(raised(values, jax.random.fold_in(stream_key, 3), *heavy), -bound, bound).astype(kind)


def setup_inputs(seed: int = 0) -> dict:
    key_of = jax.random.split(jax.random.key(seed), 5)
    return {
        "activations": centred(key_of[0], (FRAMES, HEIGHT, WIDTH, CHANNELS), 1.0, 6.0, ((0, 16), (1, 16))),
        "cotangent": bell_draw_with(key_of[1], (FRAMES, HEIGHT, WIDTH, CHANNELS), 1.0, 6.0, ((0, 16), (1, 16)), (1, 3, 16, 2.0)),
        "spatial_kernel": centred(key_of[2], (CHANNELS, 9, CHANNELS), (9 * CHANNELS) ** -0.5, 0.09375, ((0, 16),)),
        "temporal_kernel": centred(key_of[3], (CHANNELS, 3, CHANNELS), (3 * CHANNELS) ** -0.5, 0.15625, ((0, 16),)),
    }


def frame_taps(frame, lead):
    padded = jnp.pad(frame, ((1, 1), (1, 1), (0, 0)))
    rows = frame.shape[0]
    cols = frame.shape[1]
    pieces = []
    for a in range(3):
        for b in range(3):
            ra = a if lead else 2 - a
            rb = b if lead else 2 - b
            pieces.append(padded[ra:ra + rows, rb:rb + cols, :].reshape(rows * cols, frame.shape[2]))
    return pieces

def conv_forward(frame, kernel):
    pieces = frame_taps(frame, True)
    total = jnp.zeros((pieces[0].shape[0], kernel.shape[0]), jnp.float32)
    for tap in range(9):
        total = total + lax.dot_general(pieces[tap], kernel[:, tap, :], (((1,), (1,)), ((), ())), preferred_element_type=jnp.float32)
    return total.reshape(frame.shape[0], frame.shape[1], kernel.shape[0])

def reference(activations, cotangent, spatial_kernel, temporal_kernel):
    frames, height, width, chans = activations.shape
    pre = lax.map(lambda frame: conv_forward(frame, spatial_kernel), activations)
    hidden = jax.nn.silu(pre).astype(jnp.bfloat16)
    hid_pad = jnp.pad(hidden, ((1, 1), (0, 0), (0, 0), (0, 0)))
    cot_pad = jnp.pad(cotangent, ((1, 1), (0, 0), (0, 0), (0, 0)))
    count = frames * height * width
    cot_flat = cotangent.reshape(count, chans)
    slope_hidden = jnp.zeros((count, chans), jnp.float32)
    temporal_parts = []
    for k in range(3):
        shifted = cot_pad[2 - k:2 - k + frames].reshape(count, chans)
        slope_hidden = slope_hidden + jnp.dot(shifted, temporal_kernel[:, k, :], preferred_element_type=jnp.float32)
        hid_k = hid_pad[k:k + frames].reshape(count, chans)
        temporal_parts.append(lax.dot_general(cot_flat, hid_k, (((0,), (0,)), ((), ())), preferred_element_type=jnp.float32))
    temporal_sum = jnp.stack(temporal_parts, axis=1)
    slope_hidden = slope_hidden.reshape(frames, height, width, chans)
    sigma = jax.nn.sigmoid(pre)
    slope_pre = (slope_hidden * sigma * (1.0 + pre * (1.0 - sigma))).astype(jnp.bfloat16)

    def per_frame(carry, items):
        frame, slope, cot = items
        x_pieces = frame_taps(frame, True)
        s_pieces = frame_taps(slope, False)
        slope_flat = slope.reshape(height * width, chans)
        total = cot.reshape(height * width, chans).astype(jnp.float32)
        parts = []
        for tap in range(9):
            total = total + jnp.dot(s_pieces[tap], spatial_kernel[:, tap, :], preferred_element_type=jnp.float32)
            parts.append(lax.dot_general(slope_flat, x_pieces[tap], (((0,), (0,)), ((), ())), preferred_element_type=jnp.float32))
        carry = carry + jnp.stack(parts, axis=1)
        return (carry, total.reshape(height, width, chans))
    start = jnp.zeros((chans, 9, chans), jnp.float32)
    spatial_sum, grad_input = lax.scan(per_frame, start, (activations, slope_pre, cotangent))
    scale = 1.0 / math.sqrt(FRAMES * HEIGHT * WIDTH)
    return (grad_input, spatial_sum * scale, temporal_sum * scale)
```

```python
import math

import jax
import jax.numpy as jnp
from jax import lax
from jax.sharding import Mesh, PartitionSpec as P

TM = ("x", "zl", "core")
SPACE = ("zh", "y")
PAIR = [(0, 1), (1, 0)]
ORDER = ((1, 3), (3, 1))


def swap(block):
    return lax.ppermute(block, "core", PAIR)


def exchange(block, axis, stage):
    if axis == "x":
        names, number = ("x", "core"), lambda core, p: 2 * p + core
    else:
        names, number = ("core", axis), lambda core, p: 4 * core + p
    pairs = [
        (number(core, p), number(core, p ^ ORDER[core][stage]))
        for core in range(2)
        for p in range(4)
    ]
    return lax.ppermute(block, names, pairs)


def positions(axis):
    p = lax.axis_index(axis)
    core = lax.axis_index("core")
    return p, p ^ (1 + 2 * core), p ^ (3 - 2 * core), p ^ 2


def at(block, index, dim):
    return lax.dynamic_index_in_dim(block, index, dim, keepdims=False)


def ring_scatter(block, axis, dim, kind):
    own, first, second, far = positions(axis)
    sent = jnp.stack([at(block, first, dim), at(block, far, dim)]).astype(kind)
    came = exchange(sent, axis, 0).astype(jnp.float32)
    passed = (at(block, second, dim) + came[1]).astype(kind)
    return at(block, own, dim) + came[0] + exchange(passed, axis, 1).astype(jnp.float32)


def ring_gather(block, axis):
    near = exchange(block, axis, 0)
    rest = exchange(jnp.stack([block, near]), axis, 1)
    return list(zip(positions(axis), (block, near, rest[0], rest[1])))


def placed(target, slots, dim, *fixed):
    for index, block in slots:
        start = [0] * target.ndim
        for where, value in fixed:
            start[where] = value
        start[dim] = index
        target = lax.dynamic_update_slice(target, jnp.expand_dims(block, dim), start)
    return target


def halo(block, axis, dim):
    count = lax.axis_size(axis)
    forward = [(i, i + 1) for i in range(count - 1)]
    backward = [(target, source) for source, target in forward]
    size = block.shape[dim]
    low = lax.ppermute(lax.slice_in_dim(block, size - 1, size, axis=dim), axis, forward)
    high = lax.ppermute(lax.slice_in_dim(block, 0, 1, axis=dim), axis, backward)
    return jnp.concatenate([low, block, high], axis=dim)


def taps_of(padded, frames, rows, width, lead):
    pieces = []
    for a in range(3):
        for b in range(3):
            ra = a if lead else 2 - a
            rb = b if lead else 2 - b
            piece = padded[:, ra : ra + rows, rb : rb + width, :]
            pieces.append(piece.reshape(frames * rows * width, padded.shape[3]))
    return pieces


def kernel_half(spatial_kernel, temporal_kernel, half):
    core = lax.axis_index("core")
    x = lax.axis_index("x")
    own = spatial_kernel.shape[0]
    both = jnp.concatenate(
        [spatial_kernel.transpose(1, 0, 2), temporal_kernel.transpose(1, 0, 2)], axis=0
    )
    unit = lax.dynamic_slice(both, (3 * x, 0, core * half), (3, own, half))
    kind = both.dtype
    unit = placed(jnp.zeros((3, 4, own, half), kind), ring_gather(unit, "zh"), 1)
    lower, upper = unit[:, :2], unit[:, 2:]
    lower = placed(jnp.zeros((3, 2, 4, own, half), kind), ring_gather(lower, "y"), 2)
    upper = placed(jnp.zeros((4, 3, 2, own, half), kind), ring_gather(upper, "x"), 0)
    whole = jnp.zeros((4, 3, 4, 4, own, half), kind)
    whole = placed(whole, ring_gather(lower, "x"), 0)
    whole = placed(whole, ring_gather(upper, "y"), 3, (2, 2))
    return whole.reshape(12, 16 * own, half)


def per_device(activations, cotangent, spatial_kernel, temporal_kernel):
    frames, rows, width, chans = activations.shape
    count = frames * rows * width
    half = chans // 2
    core = lax.axis_index("core")
    own = spatial_kernel.shape[0]

    k_mine = kernel_half(spatial_kernel, temporal_kernel, half)
    k_other = swap(k_mine)

    x_pad = jnp.pad(halo(activations, SPACE, 1), ((0, 0), (0, 0), (1, 1), (0, 0)))
    x_mine = lax.dynamic_slice_in_dim(x_pad, core * half, half, axis=3)
    x_other = lax.dynamic_slice_in_dim(x_pad, (1 - core) * half, half, axis=3)
    x_pair = swap(x_other)
    cot_pad = halo(cotangent, TM, 0)
    cot_pair = swap(cot_pad)

    def shifts(padded):
        return [padded[2 - k : 2 - k + frames].reshape(count, chans) for k in range(3)]

    def in_order(mine, other):
        return jnp.where(
            core == 0,
            jnp.concatenate([mine, other], axis=1),
            jnp.concatenate([other, mine], axis=1),
        )

    shifted = shifts(cot_pad)
    pre = jnp.zeros((count, chans), jnp.float32)
    slope_hidden = []
    for part, kernel in ((x_mine, k_mine), (x_other, k_other)):
        for tap, piece in enumerate(taps_of(part, frames, rows, width, True)):
            pre = pre + lax.dot_general(
                piece, kernel[tap], (((1,), (1,)), ((), ())), preferred_element_type=jnp.float32
            )
        total = jnp.zeros((count, half), jnp.float32)
        for k in range(3):
            total = total + jnp.dot(shifted[k], kernel[9 + k], preferred_element_type=jnp.float32)
        slope_hidden.append(total)
    slope_hidden = in_order(*slope_hidden)
    sigma = jax.nn.sigmoid(pre)
    hidden = (pre * sigma).astype(jnp.bfloat16)
    slope_pre = (slope_hidden * sigma * (1.0 + pre * (1.0 - sigma))).astype(jnp.bfloat16)

    h_mine = lax.dynamic_slice_in_dim(hidden, core * half, half, axis=1)
    h_other = lax.dynamic_slice_in_dim(hidden, (1 - core) * half, half, axis=1)
    h_pair = swap(h_other)
    slope_pair = swap(slope_pre)
    slope_maps = slope_pre.reshape(frames, rows, width, chans)
    slope_pad = jnp.pad(halo(slope_maps, SPACE, 1), ((0, 0), (0, 0), (1, 1), (0, 0)))

    def weight_terms(start):
        terms = []
        for slope, part, cots, hid in (
            (slope_pre, x_mine, shifted, h_mine),
            (slope_pair, x_pair, shifts(cot_pair), h_pair),
        ):
            pieces = [(slope, p) for p in taps_of(part, frames, rows, width, True)]
            pieces += [(cot, hid) for cot in cots]
            terms.append(
                [
                    lax.dot_general(
                        a[:, start : start + half],
                        b,
                        (((0,), (0,)), ((), ())),
                        preferred_element_type=jnp.float32,
                    )
                    for a, b in pieces
                ]
            )
        total = jnp.stack([a + b for a, b in zip(*terms)])
        return total.reshape(4, 3, 2, 4, own, half)

    lower = ring_scatter(weight_terms(0), "x", 0, jnp.bfloat16)
    upper = ring_scatter(weight_terms(half), "y", 3, jnp.bfloat16)
    lower = ring_scatter(lower, "y", 2, jnp.float32)
    upper = ring_scatter(upper, "x", 0, jnp.float32)
    terms = jnp.concatenate([lower, upper], axis=1)
    terms = ring_scatter(terms, "zh", 1, jnp.float32)
    terms = terms + lax.ppermute(terms, "zl", PAIR)
    pixels = count * lax.axis_size(TM) * lax.axis_size(SPACE)
    terms = terms * (1.0 / math.sqrt(pixels))
    terms = placed(jnp.zeros((4, 3, own, half), jnp.float32), ring_gather(terms, "x"), 0)
    terms = terms.reshape(12 * own, half)
    terms = in_order(terms, swap(terms)).reshape(12, own, chans).transpose(1, 0, 2)

    grads = []
    for kernel in (k_mine, k_other):
        total = jnp.zeros((count, half), jnp.float32)
        for tap, piece in enumerate(taps_of(slope_pad, frames, rows, width, False)):
            total = total + jnp.dot(piece, kernel[tap], preferred_element_type=jnp.float32)
        grads.append(total)
    grad = in_order(*grads) + cotangent.reshape(count, chans).astype(jnp.float32)
    return grad.reshape(frames, rows, width, chans), terms[:, :9], terms[:, 9:]


def solution(mesh):
    split = Mesh(mesh.devices.reshape(4, 2, 2, 4, 4), TM + SPACE)
    maps = P(TM, SPACE, None, None)
    kernels = P(SPACE, None, None)
    return jax.shard_map(
        per_device,
        mesh=split,
        in_specs=(maps, maps, kernels, kernels),
        out_specs=(maps, kernels, kernels),
        check_vma=False,
    )
```

```python
import functools
import math

import jax
import jax.numpy as jnp
from jax import lax
from jax.experimental import pallas as pl
from jax.experimental.pallas import tpu as pltpu
from jax.sharding import Mesh, PartitionSpec as P

TM = ("x", "zl", "core")
SPACE = ("zh", "y")
PAIR = [(0, 1), (1, 0)]
ORDER = ((1, 3), (3, 1))
VMEM = pl.BlockSpec(memory_space=pltpu.VMEM)
ANY = pl.BlockSpec(memory_space=pl.ANY)
SMEM = pl.BlockSpec(memory_space=pltpu.SMEM)
PARAMS = pltpu.CompilerParams(vmem_limit_bytes=40 * 1024 * 1024)


def swap(block):
    return lax.ppermute(block, "core", PAIR)


def exchange(block, axis, stage):
    if axis == "x":
        names, number = ("x", "core"), lambda core, p: 2 * p + core
    else:
        names, number = ("core", axis), lambda core, p: 4 * core + p
    pairs = [
        (number(core, p), number(core, p ^ ORDER[core][stage]))
        for core in range(2)
        for p in range(4)
    ]
    return lax.ppermute(block, names, pairs)


def positions(axis):
    p = lax.axis_index(axis)
    core = lax.axis_index("core")
    return p, p ^ (1 + 2 * core), p ^ (3 - 2 * core), p ^ 2


def slots_of(axis):
    own, first, second, far = positions(axis)
    q = jnp.arange(4, dtype=jnp.int32)
    return jnp.where(q == own, 0, jnp.where(q == second, 1, jnp.where(q == first, 2, 3)))


def ring_scatter(terms, sent, axis):
    came = exchange(sent, axis, 0).astype(jnp.float32)
    passed = (terms[1] + came[1]).astype(sent.dtype)
    return terms[0] + came[0] + exchange(passed, axis, 1).astype(jnp.float32)


def ring_first(block, axis):
    return block, exchange(block, axis, 0)


def ring_second(pair, axis):
    rest = exchange(jnp.stack(pair), axis, 1)
    return list(zip(positions(axis), (*pair, rest[0], rest[1])))


def placed(target, slots, dim, *fixed):
    for index, block in slots:
        start = [0] * target.ndim
        for where, value in fixed:
            start[where] = value
        start[dim] = index
        target = lax.dynamic_update_slice(target, jnp.expand_dims(block, dim), start)
    return target


def gathered(block, axis):
    spread = jnp.broadcast_to(block[None], (lax.axis_size(axis),) + block.shape)
    return lax.all_to_all(spread, axis, 0, 0, tiled=True)


def scattered(block, axis):
    return jnp.sum(lax.all_to_all(block, axis, 0, 0, tiled=True).astype(jnp.float32), axis=0)


def halo(block, axis, dim):
    count = lax.axis_size(axis)
    forward = [(i, i + 1) for i in range(count - 1)]
    backward = [(target, source) for source, target in forward]
    size = block.shape[dim]
    low = lax.ppermute(lax.slice_in_dim(block, size - 1, size, axis=dim), axis, forward)
    high = lax.ppermute(lax.slice_in_dim(block, 0, 1, axis=dim), axis, backward)
    return jnp.concatenate([low, block, high], axis=dim)


def column_shifts(maps):
    edge = jnp.zeros_like(maps[:, :, :1])
    return jnp.stack(
        [
            jnp.concatenate([edge, maps[:, :, :-1]], axis=2),
            maps,
            jnp.concatenate([maps[:, :, 1:], edge], axis=2),
        ]
    )


def lanes(index, half):
    return pl.ds(pl.multiple_of(index * half, half), half)


def add_terms(index, x_ref, cot_ref, kernel_hbm, kernel_ref, sems, pre_ref, slope_ref, start_ref):
    frames, block, chans = pre_ref.shape
    half = chans // 2
    copies = []
    for group in range(4):
        taps = pl.ds(3 * group, 3)
        copies.append(
            pltpu.make_async_copy(kernel_hbm.at[taps], kernel_ref.at[taps], sems.at[group])
        )
        copies[group].start()

    def convolve(f, _, a):
        if a > 0:
            total = pre_ref[f]
        elif start_ref is not None:
            total = start_ref[f]
        else:
            total = jnp.zeros((block, chans), jnp.float32)
        for b in range(3):
            piece = x_ref[b, f, a : a + 2, :, lanes(index, half)].reshape(block, half)
            total += lax.dot_general(
                piece,
                kernel_ref[3 * a + b],
                (((1,), (1,)), ((), ())),
                preferred_element_type=jnp.float32,
            )
        pre_ref[f] = total
        return 0

    def blend(f, _):
        total = jnp.zeros((block, half), jnp.float32)
        for k in range(3):
            piece = cot_ref[2 - k + f].reshape(block, chans)
            total += jnp.dot(piece, kernel_ref[9 + k], preferred_element_type=jnp.float32)
        slope_ref[f] = total
        return 0

    for a in range(3):
        copies[a].wait()
        lax.fori_loop(0, frames, functools.partial(convolve, a=a), 0)
    copies[3].wait()
    lax.fori_loop(0, frames, blend, 0)


def first_kernel(core_ref, x_ref, cot_ref, kernel_hbm, pre_ref, slope_ref, kernel_ref, sems):
    add_terms(
        core_ref[0], x_ref, cot_ref, kernel_hbm, kernel_ref, sems, pre_ref, slope_ref, None
    )


def second_kernel(
    core_ref,
    x_ref,
    cot_ref,
    kernel_hbm,
    start_ref,
    mine_ref,
    hid_mine_ref,
    hid_other_ref,
    slope_ref,
    turned_ref,
    pre_ref,
    other_ref,
    work_ref,
    kernel_ref,
    sems,
):
    core = core_ref[0]
    add_terms(
        1 - core, x_ref, cot_ref, kernel_hbm, kernel_ref, sems, pre_ref, other_ref, start_ref
    )
    frames, block, chans = pre_ref.shape
    half = chans // 2
    part = 32
    for hid_ref, source_ref, index in (
        (hid_mine_ref, mine_ref, core),
        (hid_other_ref, other_ref, 1 - core),
    ):

        def finish(step, _, hid_ref=hid_ref, source_ref=source_ref, index=index):
            f, r = step // (block // part), step % (block // part)
            rows = pl.ds(pl.multiple_of(r * part, part), part)
            pre = pre_ref[f, rows, lanes(index, half)]
            sigma = 1.0 / (1.0 + jnp.exp(-pre))
            hid_ref[f, rows] = (pre * sigma).astype(jnp.bfloat16)
            slope = source_ref[f, rows] * sigma * (1.0 + pre * (1.0 - sigma))
            work_ref[f, rows, lanes(index, half)] = slope
            return 0

        lax.fori_loop(0, frames * (block // part), finish, 0)
    for f in range(frames):
        slope = work_ref[f].astype(jnp.bfloat16)
        slope_ref[f] = slope
        turned_ref[:, f * block : (f + 1) * block] = slope.T


def forward(core, shifts, cot_pad, k_mine, k_other):
    frames, _, width, chans = shifts.shape[1:]
    block = 2 * width
    half = chans // 2
    full = jax.ShapeDtypeStruct((frames, block, chans), jnp.float32)
    part = jax.ShapeDtypeStruct((frames, block, half), jnp.float32)
    held = [pltpu.VMEM(k_mine.shape, k_mine.dtype), pltpu.SemaphoreType.DMA((4,))]
    pre, mine = pl.pallas_call(
        first_kernel,
        out_shape=(full, part),
        in_specs=[SMEM, VMEM, VMEM, ANY],
        out_specs=(VMEM, VMEM),
        scratch_shapes=held,
        compiler_params=PARAMS,
        cost_estimate=pl.CostEstimate(flops=3200000000, bytes_accessed=12000000, transcendentals=0),
    )(core, shifts, cot_pad, k_mine)
    hid = jax.ShapeDtypeStruct((frames, block, half), jnp.bfloat16)
    return pl.pallas_call(
        second_kernel,
        out_shape=(
            hid,
            hid,
            jax.ShapeDtypeStruct((frames, block, chans), jnp.bfloat16),
            jax.ShapeDtypeStruct((chans, frames * block), jnp.bfloat16),
        ),
        in_specs=[SMEM, VMEM, VMEM, ANY, VMEM, VMEM],
        out_specs=(VMEM,) * 4,
        scratch_shapes=[
            pltpu.VMEM(full.shape, jnp.float32),
            pltpu.VMEM(part.shape, jnp.float32),
            pltpu.VMEM(full.shape, jnp.float32),
        ]
        + held,
        compiler_params=PARAMS,
        cost_estimate=pl.CostEstimate(flops=3200000000, bytes_accessed=15000000, transcendentals=0),
    )(core, shifts, cot_pad, k_other, pre, mine)


def weight_kernel(
    upper,
    info_ref,
    turned_ref,
    turned_pair_ref,
    x_ref,
    x_pair_ref,
    cot_ref,
    cot_pair_ref,
    hid_ref,
    hid_pair_ref,
    terms_ref,
    sent_ref,
):
    half = x_pair_ref.shape[-1]
    count = turned_ref.shape[1]
    block = count // 2
    own = terms_ref.shape[-2]
    outs = pl.ds(half * upper, half)

    def keep(total, group, b):
        for zh in range(2):
            for y in range(4):
                row = (4 * zh + y) * own
                if upper:
                    terms_ref[info_ref[1 + y], group, b, zh] = total[row : row + own]
                else:
                    terms_ref[info_ref[1 + group], y, b, zh] = total[row : row + own]

    def spatial(a, _):
        for b in range(3):
            piece = x_ref[b, :, pl.ds(a, 2), :, lanes(info_ref[0], half)].reshape(count, half)
            total = jnp.dot(turned_ref[outs], piece, preferred_element_type=jnp.float32)
            piece = x_pair_ref[b, :, pl.ds(a, 2)].reshape(count, half)
            total += jnp.dot(turned_pair_ref[outs], piece, preferred_element_type=jnp.float32)
            keep(total, a, b)
        return 0

    lax.fori_loop(0, 3, spatial, 0)
    for k in range(3):
        piece = cot_ref[outs, (2 - k) * block : (4 - k) * block]
        total = jnp.dot(piece, hid_ref[...], preferred_element_type=jnp.float32)
        piece = cot_pair_ref[outs, (2 - k) * block : (4 - k) * block]
        total += jnp.dot(piece, hid_pair_ref[...], preferred_element_type=jnp.float32)
        keep(total, 3, k)
    for slot in range(2):
        for i in range(4):
            sent_ref[slot, i] = terms_ref[2 + slot, i].astype(jnp.bfloat16)


def weight_terms(upper, own, info, *operands):
    half = operands[-1].shape[-1]
    shape = (4, 4, 3, 2, own, half)
    return pl.pallas_call(
        functools.partial(weight_kernel, upper),
        out_shape=(
            jax.ShapeDtypeStruct(shape, jnp.float32),
            jax.ShapeDtypeStruct((2,) + shape[1:], jnp.bfloat16),
        ),
        in_specs=[SMEM] + [VMEM] * 8,
        out_specs=(VMEM, VMEM),
        compiler_params=PARAMS,
        cost_estimate=pl.CostEstimate(flops=2400000000, bytes_accessed=16000000, transcendentals=0),
    )(info, *operands)


def kernel_unit(spatial_kernel, temporal_kernel, half):
    both = jnp.concatenate(
        [spatial_kernel.transpose(1, 0, 2), temporal_kernel.transpose(1, 0, 2)], axis=0
    )
    start = (3 * lax.axis_index("x"), 0, lax.axis_index("core") * half)
    unit = lax.dynamic_slice(both, start, (3, both.shape[1], half))
    return gathered(unit, "zh").transpose(1, 0, 2, 3)


def kernel_half(unit, waited):
    own, half = unit.shape[-2:]
    lower = gathered(unit[:, :2], "y").transpose(1, 2, 0, 3, 4)
    upper = gathered(unit[:, 2:], "x")
    lower, upper, waited = lax.optimization_barrier(
        (ring_first(lower, "x"), ring_first(upper, "y"), waited)
    )
    whole = jnp.zeros((4, 3, 4, 4, own, half), unit.dtype)
    whole = placed(whole, ring_second(lower, "x"), 0)
    whole = placed(whole, ring_second(upper, "y"), 3, (2, 2))
    return whole.reshape(12, 16 * own, half), waited


def per_device(activations, cotangent, spatial_kernel, temporal_kernel):
    frames, rows, width, chans = activations.shape
    count = frames * rows * width
    half = chans // 2
    core = lax.axis_index("core")
    own = spatial_kernel.shape[0]
    core_info = core.astype(jnp.int32).reshape(1)

    unit = kernel_unit(spatial_kernel, temporal_kernel, half)
    edges = (activations, cotangent)
    edges, unit = lax.optimization_barrier((edges, unit))
    x_wide = halo(edges[0], SPACE, 1)
    cot_pad = halo(edges[1], TM, 0)
    k_mine, (x_wide, cot_pad) = kernel_half(unit, (x_wide, cot_pad))
    x_pair = swap(lax.dynamic_slice_in_dim(x_wide, (1 - core) * half, half, axis=3))
    shifts = column_shifts(x_wide)
    shifts_pair = column_shifts(x_pair)
    cot_turned = cot_pad.reshape((frames + 2) * rows * width, chans).T
    cot_turned_pair = swap(cot_turned)
    k_mine, shifts, cot_turned = lax.optimization_barrier((k_mine, shifts, cot_turned))
    k_other = swap(k_mine)

    hid_mine, hid_other, slope_pre, turned = forward(core_info, shifts, cot_pad, k_mine, k_other)
    turned_pair = swap(turned)
    operands = (
        turned,
        turned_pair,
        shifts,
        shifts_pair,
        cot_turned,
        cot_turned_pair,
        hid_mine.reshape(count, half),
        swap(hid_other).reshape(count, half),
    )
    info = jnp.concatenate([core_info, slots_of("x")])
    lower, sent_lower = weight_terms(0, own, info, *operands)
    info = jnp.concatenate([core_info, slots_of("y")])
    upper, sent_upper = weight_terms(1, own, info, *operands)
    slope_pre, _ = lax.optimization_barrier((slope_pre, sent_upper))

    lower = ring_scatter(lower, sent_lower, "x")
    upper = ring_scatter(upper, sent_upper, "y")
    lower = scattered(lower, "y")
    upper = scattered(upper, "x")
    terms = jnp.concatenate([lower, upper], axis=1)
    terms = terms.reshape(3, 4, 2, own // 2, half).transpose(1, 2, 0, 3, 4)
    terms = scattered(terms.reshape(8, 3, own // 2, half), ("zh", "zl"))
    pixels = count * lax.axis_size(TM) * lax.axis_size(SPACE)
    terms = gathered(terms * (1.0 / math.sqrt(pixels)), TM)
    terms = terms.reshape(4, 2, 2, 3, own // 2, half).transpose(1, 4, 0, 3, 2, 5)
    terms = terms.reshape(own, 12, chans)

    slope_maps = halo(slope_pre.reshape(frames, rows, width, chans), SPACE, 1)
    slope_pad = jnp.pad(slope_maps, ((0, 0), (0, 0), (1, 1), (0, 0)))
    grads = []
    for kernel in (k_mine, k_other):
        total = jnp.zeros((count, half), jnp.float32)
        for tap in range(9):
            a, b = 2 - tap // 3, 2 - tap % 3
            piece = slope_pad[:, a : a + rows, b : b + width].reshape(count, chans)
            total = total + jnp.dot(piece, kernel[tap], preferred_element_type=jnp.float32)
        grads.append(total)
    grad = jnp.where(
        core == 0, jnp.concatenate(grads, axis=1), jnp.concatenate(grads[::-1], axis=1)
    )
    grad = grad + cotangent.reshape(count, chans).astype(jnp.float32)
    return grad.reshape(frames, rows, width, chans), terms[:, :9], terms[:, 9:]


def solution(mesh):
    split = Mesh(mesh.devices.reshape(4, 2, 2, 4, 4), TM + SPACE)
    maps = P(TM, SPACE, None, None)
    kernels = P(SPACE, None, None)
    return jax.shard_map(
        per_device,
        mesh=split,
        in_specs=(maps, maps, kernels, kernels),
        out_specs=(maps, kernels, kernels),
        check_vma=False,
    )
```

```python
import functools
import math

import jax
import jax.numpy as jnp
from jax import lax
from jax.experimental import pallas as pl
from jax.experimental.pallas import tpu as pltpu
from jax.sharding import Mesh, PartitionSpec as P

TM = ("x", "zl", "core")
SPACE = ("zh", "y")
PAIR = [(0, 1), (1, 0)]
ORDER = ((1, 3), (3, 1))
VMEM = pl.BlockSpec(memory_space=pltpu.VMEM)
ANY = pl.BlockSpec(memory_space=pl.ANY)
SMEM = pl.BlockSpec(memory_space=pltpu.SMEM)
PARAMS = pltpu.CompilerParams(vmem_limit_bytes=24 * 1024 * 1024)


def swap(block):
    return lax.ppermute(block, "core", PAIR)


def exchange(block, axis, stage):
    if axis == "x":
        names, number = ("x", "core"), lambda core, p: 2 * p + core
    else:
        names, number = ("core", axis), lambda core, p: 4 * core + p
    pairs = [
        (number(core, p), number(core, p ^ ORDER[core][stage]))
        for core in range(2)
        for p in range(4)
    ]
    return lax.ppermute(block, names, pairs)


def positions(axis):
    p = lax.axis_index(axis)
    core = lax.axis_index("core")
    return p, p ^ (1 + 2 * core), p ^ (3 - 2 * core), p ^ 2


def slots_of(axis):
    own, first, second, far = positions(axis)
    q = jnp.arange(4, dtype=jnp.int32)
    return jnp.where(q == own, 0, jnp.where(q == second, 1, jnp.where(q == first, 2, 3)))


def slots_in(axis, turn):
    p = lax.axis_index(axis)
    core = lax.axis_index("core") ^ turn
    return jnp.stack([p, p ^ (1 + 2 * core), p ^ (3 - 2 * core), p ^ 2]).astype(jnp.int32)


def ring_scatter(terms, sent, axis, waited=None):
    came = exchange(sent, axis, 0)
    if waited is not None:
        came, waited = lax.optimization_barrier((came, waited))
    came = came.astype(jnp.float32)
    passed = (terms[1] + came[1]).astype(sent.dtype)
    return terms[0] + came[0] + exchange(passed, axis, 1).astype(jnp.float32)


def ring_gather(block, axis):
    pair = jnp.stack([block, exchange(block, axis, 0)])
    return pair, exchange(pair, axis, 1)


def gathered(block, axis):
    spread = jnp.broadcast_to(block[None], (lax.axis_size(axis),) + block.shape)
    return lax.all_to_all(spread, axis, 0, 0, tiled=True)


def scattered(block, axis):
    return jnp.sum(lax.all_to_all(block, axis, 0, 0, tiled=True).astype(jnp.float32), axis=0)


def edges_of(block, axis, dim):
    count = lax.axis_size(axis)
    forward = [(i, (i + 1) % count) for i in range(count)]
    backward = [(target, source) for source, target in forward]
    size = block.shape[dim]
    low = lax.ppermute(lax.slice_in_dim(block, size - 1, size, axis=dim), axis, forward)
    high = lax.ppermute(lax.slice_in_dim(block, 0, 1, axis=dim), axis, backward)
    return low, high


def widened(block, edges, axis, dim):
    low, high = edges
    index = lax.axis_index(axis)
    low = jnp.where(index == 0, jnp.zeros_like(low), low)
    high = jnp.where(index == lax.axis_size(axis) - 1, jnp.zeros_like(high), high)
    return jnp.concatenate([low, block, high], axis=dim)


def column_shifts(maps):
    edge = jnp.zeros_like(maps[:, :, :1])
    return jnp.stack(
        [
            jnp.concatenate([edge, maps[:, :, :-1]], axis=2),
            maps,
            jnp.concatenate([maps[:, :, 1:], edge], axis=2),
        ]
    )


def lanes(index, half):
    return pl.ds(pl.multiple_of(index * half, half), half)


def assemble(info_ref, parts, kernel_ref, sems):
    copies = []
    for pair in range(2):
        for j in range(2):
            slot = 2 * pair + j
            for t in range(4):
                x, y = info_ref[1 + slot], info_ref[5 + t]
                target = kernel_ref.at[x, :, pl.ds(0, 2), y]
                copies.append((parts[pair].at[j, t], target))
                x, y = info_ref[1 + t], info_ref[5 + slot]
                target = kernel_ref.at[x, :, pl.ds(2, 2), y]
                copies.append((parts[2 + pair].at[j, t], target))
    copies = [
        pltpu.make_async_copy(source, target, sems.at[i])
        for i, (source, target) in enumerate(copies)
    ]
    for copy in copies:
        copy.start()
    for copy in copies:
        copy.wait()


def add_terms(index, x_ref, cot_ref, kernel_ref, pre_ref, slope_ref, start_ref):
    frames, block, chans = pre_ref.shape
    half = chans // 2

    def convolve(f, _, a):
        if a > 0:
            total = pre_ref[f]
        elif start_ref is not None:
            total = start_ref[f]
        else:
            total = jnp.zeros((block, chans), jnp.float32)
        for b in range(3):
            piece = x_ref[b, f, a : a + 2, :, lanes(index, half)].reshape(block, half)
            total += lax.dot_general(
                piece,
                kernel_ref[a, b].reshape(chans, half),
                (((1,), (1,)), ((), ())),
                preferred_element_type=jnp.float32,
            )
        pre_ref[f] = total
        return 0

    def blend(f, _):
        total = jnp.zeros((block, half), jnp.float32)
        for k in range(3):
            piece = cot_ref[2 - k + f].reshape(block, chans)
            kernel = kernel_ref[3, k].reshape(chans, half)
            total += jnp.dot(piece, kernel, preferred_element_type=jnp.float32)
        slope_ref[f] = total
        return 0

    for a in range(3):
        lax.fori_loop(0, frames, functools.partial(convolve, a=a), 0)
    lax.fori_loop(0, frames, blend, 0)


def first_kernel(info_ref, x_ref, cot_ref, *refs):
    parts, (pre_ref, slope_ref, kernel_ref, sems) = refs[:4], refs[4:]
    assemble(info_ref, parts, kernel_ref, sems)
    add_terms(info_ref[0], x_ref, cot_ref, kernel_ref, pre_ref, slope_ref, None)


def second_kernel(info_ref, x_ref, cot_ref, *refs):
    parts, (start_ref, mine_ref), refs = refs[:4], refs[4:6], refs[6:]
    hid_mine_ref, hid_other_ref, slope_ref, turned_ref, kernel_ref = refs[:5]
    pre_ref, other_ref, work_ref, sems = refs[5:]
    assemble(info_ref, parts, kernel_ref, sems)
    other = info_ref[0]
    add_terms(other, x_ref, cot_ref, kernel_ref, pre_ref, other_ref, start_ref)
    frames, block, chans = pre_ref.shape
    half = chans // 2
    part = 32
    for hid_ref, source_ref, index in (
        (hid_mine_ref, mine_ref, 1 - other),
        (hid_other_ref, other_ref, other),
    ):

        def finish(step, _, hid_ref=hid_ref, source_ref=source_ref, index=index):
            f, r = step // (block // part), step % (block // part)
            rows = pl.ds(pl.multiple_of(r * part, part), part)
            pre = pre_ref[f, rows, lanes(index, half)]
            sigma = 1.0 / (1.0 + jnp.exp(-pre))
            hid_ref[f, rows] = (pre * sigma).astype(jnp.bfloat16)
            slope = source_ref[f, rows] * sigma * (1.0 + pre * (1.0 - sigma))
            work_ref[f, rows, lanes(index, half)] = slope
            return 0

        lax.fori_loop(0, frames * (block // part), finish, 0)
    for f in range(frames):
        slope = work_ref[f].astype(jnp.bfloat16)
        slope_ref[f] = slope
        turned_ref[:, f * block : (f + 1) * block] = slope.T


def forward(infos, shifts, cot_pad, parts, parts_other):
    frames, _, width, chans = shifts.shape[1:]
    block = 2 * width
    half = chans // 2
    full = jax.ShapeDtypeStruct((frames, block, chans), jnp.float32)
    part = jax.ShapeDtypeStruct((frames, block, half), jnp.float32)
    hid = jax.ShapeDtypeStruct((frames, block, half), jnp.bfloat16)
    kernel = jax.ShapeDtypeStruct((4, 3, 4, 4) + parts[0].shape[-2:], parts[0].dtype)
    sems = pltpu.SemaphoreType.DMA((32,))
    pre, mine, k_mine = pl.pallas_call(
        first_kernel,
        out_shape=(full, part, kernel),
        in_specs=[SMEM, VMEM, VMEM] + [ANY] * 4,
        out_specs=(VMEM,) * 3,
        scratch_shapes=[sems],
        compiler_params=PARAMS,
        cost_estimate=pl.CostEstimate(flops=3200000000, bytes_accessed=12000000, transcendentals=0),
    )(infos[0], shifts, cot_pad, *parts)
    results = pl.pallas_call(
        second_kernel,
        out_shape=(
            hid,
            hid,
            jax.ShapeDtypeStruct((frames, block, chans), jnp.bfloat16),
            jax.ShapeDtypeStruct((chans, frames * block), jnp.bfloat16),
            kernel,
        ),
        in_specs=[SMEM, VMEM, VMEM] + [ANY] * 4 + [VMEM] * 2,
        out_specs=(VMEM,) * 5,
        scratch_shapes=[
            pltpu.VMEM(full.shape, jnp.float32),
            pltpu.VMEM(part.shape, jnp.float32),
            pltpu.VMEM(full.shape, jnp.float32),
            sems,
        ],
        compiler_params=PARAMS,
        cost_estimate=pl.CostEstimate(flops=3200000000, bytes_accessed=15000000, transcendentals=0),
    )(infos[1], shifts, cot_pad, *parts_other, pre, mine)
    return k_mine, results


def weight_kernel(
    upper,
    info_ref,
    turned_ref,
    turned_pair_ref,
    x_ref,
    x_pair_ref,
    cot_ref,
    cot_pair_ref,
    hid_ref,
    hid_pair_ref,
    terms_ref,
    sent_ref,
):
    half = x_pair_ref.shape[-1]
    count = turned_ref.shape[1]
    block = count // 2
    own = terms_ref.shape[-2]
    outs = pl.ds(half * upper, half)

    def keep(total, group, b):
        for zh in range(2):
            for y in range(4):
                row = (4 * zh + y) * own
                slots = info_ref[1 + group], info_ref[5 + y]
                slots = slots[::-1] if upper else slots
                terms_ref[slots[0], slots[1], b, zh] = total[row : row + own]

    def spatial(a, _):
        for b in range(3):
            piece = x_ref[b, :, pl.ds(a, 2), :, lanes(info_ref[0], half)].reshape(count, half)
            total = jnp.dot(turned_ref[outs], piece, preferred_element_type=jnp.float32)
            piece = x_pair_ref[b, :, pl.ds(a, 2)].reshape(count, half)
            total += jnp.dot(turned_pair_ref[outs], piece, preferred_element_type=jnp.float32)
            keep(total, a, b)
        return 0

    lax.fori_loop(0, 3, spatial, 0)
    for k in range(3):
        piece = cot_ref[outs, (2 - k) * block : (4 - k) * block]
        total = jnp.dot(piece, hid_ref[...], preferred_element_type=jnp.float32)
        piece = cot_pair_ref[outs, (2 - k) * block : (4 - k) * block]
        total += jnp.dot(piece, hid_pair_ref[...], preferred_element_type=jnp.float32)
        keep(total, 3, k)
    for slot in range(2):
        for i in range(4):
            sent_ref[slot, i] = terms_ref[2 + slot, i].astype(jnp.bfloat16)


def weight_terms(upper, own, info, *operands):
    half = operands[-1].shape[-1]
    shape = (4, 4, 3, 2, own, half)
    return pl.pallas_call(
        functools.partial(weight_kernel, upper),
        out_shape=(
            jax.ShapeDtypeStruct(shape, jnp.float32),
            jax.ShapeDtypeStruct((2,) + shape[1:], jnp.bfloat16),
        ),
        in_specs=[SMEM] + [VMEM] * 8,
        out_specs=(VMEM, VMEM),
        compiler_params=PARAMS,
        cost_estimate=pl.CostEstimate(flops=2400000000, bytes_accessed=16000000, transcendentals=0),
    )(info, *operands)


def grad_kernel(info_ref, x_ref, cot_ref, mine_ref, other_ref, out_ref):
    frames, block, chans = out_ref.shape
    half = chans // 2
    for kernel_ref, index in ((mine_ref, info_ref[0]), (other_ref, 1 - info_ref[0])):
        for a in range(3):

            def convolve(f, _, kernel_ref=kernel_ref, index=index, a=a):
                if a > 0:
                    total = out_ref[f, :, lanes(index, half)]
                else:
                    total = cot_ref[f, :, lanes(index, half)].astype(jnp.float32)
                for b in range(3):
                    piece = x_ref[2 - b, f, 2 - a : 4 - a].reshape(block, chans)
                    kernel = kernel_ref[a, b].reshape(chans, half)
                    total += jnp.dot(piece, kernel, preferred_element_type=jnp.float32)
                out_ref[f, :, lanes(index, half)] = total
                return 0

            lax.fori_loop(0, frames, convolve, 0)


def input_gradient(info, shifts, cotangent, k_mine, k_other):
    frames, rows, width, chans = cotangent.shape
    return pl.pallas_call(
        grad_kernel,
        out_shape=jax.ShapeDtypeStruct((frames, rows * width, chans), jnp.float32),
        in_specs=[SMEM] + [VMEM] * 4,
        out_specs=VMEM,
        compiler_params=PARAMS,
        cost_estimate=pl.CostEstimate(flops=3600000000, bytes_accessed=16000000, transcendentals=0),
    )(info, shifts, cotangent.reshape(frames, rows * width, chans), k_mine, k_other)


def kernel_unit(spatial_kernel, temporal_kernel, half):
    both = jnp.concatenate(
        [spatial_kernel.transpose(1, 0, 2), temporal_kernel.transpose(1, 0, 2)], axis=0
    )
    start = (3 * lax.axis_index("x"), 0, lax.axis_index("core") * half)
    unit = lax.dynamic_slice(both, start, (3, both.shape[1], half))
    return gathered(unit, "zh").transpose(1, 0, 2, 3)


def kernel_parts(unit, waited):
    lower = jnp.concatenate(ring_gather(unit[:, :2], "y"))
    upper = jnp.concatenate(ring_gather(unit[:, 2:], "x"))
    lower, lower_near = lower, exchange(lower, "x", 0)
    upper, upper_near = upper, exchange(upper, "y", 0)
    (lower_near, upper_near), waited = lax.optimization_barrier(((lower_near, upper_near), waited))
    lower = jnp.stack([lower, lower_near])
    upper = jnp.stack([upper, upper_near])
    lower_rest, upper_rest = exchange(lower, "x", 1), exchange(upper, "y", 1)
    mine = (lower, lower_rest, upper, upper_rest)
    return mine, tuple(swap(part) for part in mine), waited


def per_device(activations, cotangent, spatial_kernel, temporal_kernel):
    frames, rows, width, chans = activations.shape
    count = frames * rows * width
    half = chans // 2
    core = lax.axis_index("core").astype(jnp.int32).reshape(1)
    own = spatial_kernel.shape[0]
    infos = [
        jnp.concatenate([core ^ turn, slots_in("x", turn), slots_in("y", turn)])
        for turn in range(2)
    ]

    unit = kernel_unit(spatial_kernel, temporal_kernel, half)
    edges = (activations, cotangent)
    edges, unit = lax.optimization_barrier((edges, unit))
    x_wide = widened(edges[0], edges_of(edges[0], SPACE, 1), SPACE, 1)
    cot_pad = widened(edges[1], edges_of(edges[1], TM, 0), TM, 0)
    parts, parts_other, (x_wide, cot_pad) = kernel_parts(unit, (x_wide, cot_pad))
    x_pair = swap(lax.dynamic_slice_in_dim(x_wide, (1 - core[0]) * half, half, axis=3))
    shifts = column_shifts(x_wide)
    shifts_pair = column_shifts(x_pair)
    cot_turned = cot_pad.reshape((frames + 2) * rows * width, chans).T
    cot_turned_pair = swap(cot_turned)
    (shifts_pair, cot_turned_pair), parts_other = lax.optimization_barrier(
        ((shifts_pair, cot_turned_pair), parts_other)
    )

    k_mine, results = forward(infos, shifts, cot_pad, parts, parts_other)
    hid_mine, hid_other, slope_pre, turned, k_other = results
    turned_pair, hid_pair = swap(turned), swap(hid_other)
    slope_maps = slope_pre.reshape(frames, rows, width, chans)
    slope_edges = edges_of(slope_maps, SPACE, 1)
    operands = (
        turned,
        turned_pair,
        shifts,
        shifts_pair,
        cot_turned,
        cot_turned_pair,
        hid_mine.reshape(count, half),
        hid_pair.reshape(count, half),
    )
    info = jnp.concatenate([core, slots_of("x"), slots_of("y")])
    lower, sent_lower = weight_terms(0, own, info, *operands)
    info, sent_lower, slope_edges = lax.optimization_barrier((info, sent_lower, slope_edges))
    upper, sent_upper = weight_terms(1, own, info, *operands)
    slope_wide = widened(slope_maps, slope_edges, SPACE, 1)
    slope_wide, sent_upper = lax.optimization_barrier((slope_wide, sent_upper))
    grad = input_gradient(core, column_shifts(slope_wide), cotangent, k_mine, k_other)

    lower = ring_scatter(lower, sent_lower, "x", grad)
    upper = ring_scatter(upper, sent_upper, "y", grad)
    lower = ring_scatter(lower, lower[2:], "y")
    upper = ring_scatter(upper, upper[2:], "x")
    terms = jnp.concatenate([lower, upper], axis=1)
    terms = terms.reshape(3, 4, 2, own // 2, half).transpose(1, 2, 0, 3, 4)
    terms = scattered(terms.reshape(8, 3, own // 2, half), ("zh", "zl"))
    pixels = count * lax.axis_size(TM) * lax.axis_size(SPACE)
    terms = gathered(terms * (1.0 / math.sqrt(pixels)), TM)
    terms = terms.reshape(4, 2, 2, 3, own // 2, half).transpose(0, 3, 1, 4, 2, 5)
    spatial = terms[:3].reshape(9, own, chans).transpose(1, 0, 2)
    temporal = terms[3].reshape(3, own, chans).transpose(1, 0, 2)
    return grad.reshape(frames, rows, width, chans), spatial, temporal


def solution(mesh):
    split = Mesh(mesh.devices.reshape(4, 2, 2, 4, 4), TM + SPACE)
    maps = P(TM, SPACE, None, None)
    kernels = P(SPACE, None, None)
    return jax.shard_map(
        per_device,
        mesh=split,
        in_specs=(maps, maps, kernels, kernels),
        out_specs=(maps, kernels, kernels),
        check_vma=False,
    )
```

```python
import functools
import math

import jax
import jax.numpy as jnp
from jax import lax
from jax.experimental import pallas as pl
from jax.experimental.pallas import tpu as pltpu
from jax.sharding import Mesh, PartitionSpec as P

TM = ("x", "zl", "core")
SPACE = ("zh", "y")
PAIR = [(0, 1), (1, 0)]
ORDER = ((1, 3), (3, 1))
VMEM = pl.BlockSpec(memory_space=pltpu.VMEM)
ANY = pl.BlockSpec(memory_space=pl.ANY)
SMEM = pl.BlockSpec(memory_space=pltpu.SMEM)
PARAMS = pltpu.CompilerParams(vmem_limit_bytes=24 * 1024 * 1024)


def swap(block):
    return lax.ppermute(block, "core", PAIR)


def exchange(block, axis, stage):
    if axis == "x":
        names, number = ("x", "core"), lambda core, p: 2 * p + core
    else:
        names, number = ("core", axis), lambda core, p: 4 * core + p
    pairs = [
        (number(core, p), number(core, p ^ ORDER[core][stage]))
        for core in range(2)
        for p in range(4)
    ]
    return lax.ppermute(block, names, pairs)


def positions(axis):
    p = lax.axis_index(axis)
    core = lax.axis_index("core")
    return p, p ^ (1 + 2 * core), p ^ (3 - 2 * core), p ^ 2


def slots_of(axis):
    own, first, second, far = positions(axis)
    q = jnp.arange(4, dtype=jnp.int32)
    return jnp.where(q == own, 0, jnp.where(q == second, 1, jnp.where(q == first, 2, 3)))


def slots_in(axis, turn):
    p = lax.axis_index(axis)
    core = lax.axis_index("core") ^ turn
    return jnp.stack([p, p ^ (1 + 2 * core), p ^ (3 - 2 * core), p ^ 2]).astype(jnp.int32)


def ring_scatter(terms, sent, axis, waited=None):
    came = exchange(sent, axis, 0)
    if waited is not None:
        came, waited = lax.optimization_barrier((came, waited))
    came = came.astype(jnp.float32)
    passed = (terms[1] + came[1]).astype(sent.dtype)
    return terms[0] + came[0] + exchange(passed, axis, 1).astype(jnp.float32)


def ring_gather(block, axis):
    pair = jnp.stack([block, exchange(block, axis, 0)])
    return pair, exchange(pair, axis, 1)


def gathered(block, axis):
    spread = jnp.broadcast_to(block[None], (lax.axis_size(axis),) + block.shape)
    return lax.all_to_all(spread, axis, 0, 0, tiled=True)


def scattered(block, axis):
    return jnp.sum(lax.all_to_all(block, axis, 0, 0, tiled=True).astype(jnp.float32), axis=0)


def edges_of(block, axis, dim):
    count = lax.axis_size(axis)
    forward = [(i, (i + 1) % count) for i in range(count)]
    backward = [(target, source) for source, target in forward]
    size = block.shape[dim]
    low = lax.ppermute(lax.slice_in_dim(block, size - 1, size, axis=dim), axis, forward)
    high = lax.ppermute(lax.slice_in_dim(block, 0, 1, axis=dim), axis, backward)
    return low, high


def widened(block, edges, axis, dim):
    low, high = edges
    index = lax.axis_index(axis)
    low = jnp.where(index == 0, jnp.zeros_like(low), low)
    high = jnp.where(index == lax.axis_size(axis) - 1, jnp.zeros_like(high), high)
    return jnp.concatenate([low, block, high], axis=dim)


def column_shifts(maps):
    edge = jnp.zeros_like(maps[:, :, :1])
    return jnp.stack(
        [
            jnp.concatenate([edge, maps[:, :, :-1]], axis=2),
            maps,
            jnp.concatenate([maps[:, :, 1:], edge], axis=2),
        ]
    )


def lanes(index, half):
    return pl.ds(pl.multiple_of(index * half, half), half)


def assemble(info_ref, parts, kernel_ref, sems):
    copies = []
    for pair in range(2):
        for j in range(2):
            slot = 2 * pair + j
            for t in range(4):
                x, y = info_ref[1 + slot], info_ref[5 + t]
                target = kernel_ref.at[x, :, pl.ds(0, 2), y]
                copies.append((parts[pair].at[j, t], target))
                x, y = info_ref[1 + t], info_ref[5 + slot]
                target = kernel_ref.at[x, :, pl.ds(2, 2), y]
                copies.append((parts[2 + pair].at[j, t], target))
    copies = [
        pltpu.make_async_copy(source, target, sems.at[i])
        for i, (source, target) in enumerate(copies)
    ]
    for copy in copies:
        copy.start()
    for copy in copies:
        copy.wait()


def add_terms(index, x_ref, cot_ref, kernel_ref, pre_ref, slope_ref, start_ref):
    frames, block, chans = pre_ref.shape
    half = chans // 2

    def convolve(f, _, a):
        if a > 0:
            total = pre_ref[f]
        elif start_ref is not None:
            total = start_ref[f]
        else:
            total = jnp.zeros((block, chans), jnp.float32)
        for b in range(3):
            piece = x_ref[b, f, a : a + 2, :, lanes(index, half)].reshape(block, half)
            total += lax.dot_general(
                piece,
                kernel_ref[a, b].reshape(chans, half),
                (((1,), (1,)), ((), ())),
                preferred_element_type=jnp.float32,
            )
        pre_ref[f] = total
        return 0

    def blend(f, _):
        total = jnp.zeros((block, half), jnp.float32)
        for k in range(3):
            piece = cot_ref[2 - k + f].reshape(block, chans)
            kernel = kernel_ref[3, k].reshape(chans, half)
            total += jnp.dot(piece, kernel, preferred_element_type=jnp.float32)
        slope_ref[f] = total
        return 0

    for a in range(3):
        lax.fori_loop(0, frames, functools.partial(convolve, a=a), 0)
    lax.fori_loop(0, frames, blend, 0)


def first_kernel(info_ref, x_ref, cot_ref, *refs):
    parts, (pre_ref, slope_ref, kernel_ref, sems) = refs[:4], refs[4:]
    assemble(info_ref, parts, kernel_ref, sems)
    add_terms(info_ref[0], x_ref, cot_ref, kernel_ref, pre_ref, slope_ref, None)


def second_kernel(info_ref, x_ref, cot_ref, *refs):
    parts, (start_ref, mine_ref), refs = refs[:4], refs[4:6], refs[6:]
    hid_mine_ref, hid_other_ref, slope_ref, turned_ref, kernel_ref = refs[:5]
    pre_ref, other_ref, work_ref, sems = refs[5:]
    assemble(info_ref, parts, kernel_ref, sems)
    other = info_ref[0]
    add_terms(other, x_ref, cot_ref, kernel_ref, pre_ref, other_ref, start_ref)
    frames, block, chans = pre_ref.shape
    half = chans // 2
    part = 32
    for hid_ref, source_ref, index in (
        (hid_mine_ref, mine_ref, 1 - other),
        (hid_other_ref, other_ref, other),
    ):

        def finish(step, _, hid_ref=hid_ref, source_ref=source_ref, index=index):
            f, r = step // (block // part), step % (block // part)
            rows = pl.ds(pl.multiple_of(r * part, part), part)
            pre = pre_ref[f, rows, lanes(index, half)]
            sigma = 1.0 / (1.0 + jnp.exp(-pre))
            hid_ref[f, rows] = (pre * sigma).astype(jnp.bfloat16)
            slope = source_ref[f, rows] * sigma * (1.0 + pre * (1.0 - sigma))
            work_ref[f, rows, lanes(index, half)] = slope
            return 0

        lax.fori_loop(0, frames * (block // part), finish, 0)
    for f in range(frames):
        slope = work_ref[f].astype(jnp.bfloat16)
        slope_ref[f] = slope
        turned_ref[:, f * block : (f + 1) * block] = slope.T


def forward(infos, shifts, cot_pad, parts, parts_other):
    frames, _, width, chans = shifts.shape[1:]
    block = 2 * width
    half = chans // 2
    full = jax.ShapeDtypeStruct((frames, block, chans), jnp.float32)
    part = jax.ShapeDtypeStruct((frames, block, half), jnp.float32)
    hid = jax.ShapeDtypeStruct((frames, block, half), jnp.bfloat16)
    kernel = jax.ShapeDtypeStruct((4, 3, 4, 4) + parts[0].shape[-2:], parts[0].dtype)
    sems = pltpu.SemaphoreType.DMA((32,))
    pre, mine, k_mine = pl.pallas_call(
        first_kernel,
        out_shape=(full, part, kernel),
        in_specs=[SMEM, VMEM, VMEM] + [ANY] * 4,
        out_specs=(VMEM,) * 3,
        scratch_shapes=[sems],
        compiler_params=PARAMS,
        cost_estimate=pl.CostEstimate(flops=3200000000, bytes_accessed=12000000, transcendentals=0),
    )(infos[0], shifts, cot_pad, *parts)
    results = pl.pallas_call(
        second_kernel,
        out_shape=(
            hid,
            hid,
            jax.ShapeDtypeStruct((frames, block, chans), jnp.bfloat16),
            jax.ShapeDtypeStruct((chans, frames * block), jnp.bfloat16),
            kernel,
        ),
        in_specs=[SMEM, VMEM, VMEM] + [ANY] * 4 + [VMEM] * 2,
        out_specs=(VMEM,) * 5,
        scratch_shapes=[
            pltpu.VMEM(full.shape, jnp.float32),
            pltpu.VMEM(part.shape, jnp.float32),
            pltpu.VMEM(full.shape, jnp.float32),
            sems,
        ],
        compiler_params=PARAMS,
        cost_estimate=pl.CostEstimate(flops=3200000000, bytes_accessed=15000000, transcendentals=0),
    )(infos[1], shifts, cot_pad, *parts_other, pre, mine)
    return k_mine, results


def weight_kernel(
    upper,
    info_ref,
    turned_ref,
    turned_pair_ref,
    x_ref,
    x_pair_ref,
    cot_ref,
    cot_pair_ref,
    hid_ref,
    hid_pair_ref,
    terms_ref,
    sent_ref,
):
    half = x_pair_ref.shape[-1]
    count = turned_ref.shape[1]
    block = count // 2
    own = terms_ref.shape[-2]
    outs = pl.ds(half * upper, half)

    def keep(total, group, b):
        for zh in range(2):
            for y in range(4):
                row = (4 * zh + y) * own
                slots = info_ref[1 + group], info_ref[5 + y]
                slots = slots[::-1] if upper else slots
                terms_ref[slots[0], slots[1], b, zh] = total[row : row + own]

    def spatial(a, _):
        for b in range(3):
            piece = x_ref[b, :, pl.ds(a, 2), :, lanes(info_ref[0], half)].reshape(count, half)
            total = jnp.dot(turned_ref[outs], piece, preferred_element_type=jnp.float32)
            piece = x_pair_ref[b, :, pl.ds(a, 2)].reshape(count, half)
            total += jnp.dot(turned_pair_ref[outs], piece, preferred_element_type=jnp.float32)
            keep(total, a, b)
        return 0

    lax.fori_loop(0, 3, spatial, 0)
    for k in range(3):
        piece = cot_ref[outs, (2 - k) * block : (4 - k) * block]
        total = jnp.dot(piece, hid_ref[...], preferred_element_type=jnp.float32)
        piece = cot_pair_ref[outs, (2 - k) * block : (4 - k) * block]
        total += jnp.dot(piece, hid_pair_ref[...], preferred_element_type=jnp.float32)
        keep(total, 3, k)
    for slot in range(2):
        for i in range(4):
            sent_ref[slot, i] = terms_ref[2 + slot, i].astype(jnp.bfloat16)


def weight_terms(upper, own, info, *operands):
    half = operands[-1].shape[-1]
    shape = (4, 4, 3, 2, own, half)
    return pl.pallas_call(
        functools.partial(weight_kernel, upper),
        out_shape=(
            jax.ShapeDtypeStruct(shape, jnp.float32),
            jax.ShapeDtypeStruct((2,) + shape[1:], jnp.bfloat16),
        ),
        in_specs=[SMEM] + [VMEM] * 8,
        out_specs=(VMEM, VMEM),
        compiler_params=PARAMS,
        cost_estimate=pl.CostEstimate(flops=2400000000, bytes_accessed=16000000, transcendentals=0),
    )(info, *operands)


def grad_kernel(info_ref, x_ref, cot_ref, mine_ref, other_ref, out_ref):
    frames, block, chans = out_ref.shape
    half = chans // 2
    for kernel_ref, index in ((mine_ref, info_ref[0]), (other_ref, 1 - info_ref[0])):
        for a in range(3):

            def convolve(f, _, kernel_ref=kernel_ref, index=index, a=a):
                if a > 0:
                    total = out_ref[f, :, lanes(index, half)]
                else:
                    total = cot_ref[f, :, lanes(index, half)].astype(jnp.float32)
                for b in range(3):
                    piece = x_ref[2 - b, f, 2 - a : 4 - a].reshape(block, chans)
                    kernel = kernel_ref[a, b].reshape(chans, half)
                    total += jnp.dot(piece, kernel, preferred_element_type=jnp.float32)
                out_ref[f, :, lanes(index, half)] = total
                return 0

            lax.fori_loop(0, frames, convolve, 0)


def input_gradient(info, shifts, cotangent, k_mine, k_other):
    frames, rows, width, chans = cotangent.shape
    return pl.pallas_call(
        grad_kernel,
        out_shape=jax.ShapeDtypeStruct((frames, rows * width, chans), jnp.float32),
        in_specs=[SMEM] + [VMEM] * 4,
        out_specs=VMEM,
        compiler_params=PARAMS,
        cost_estimate=pl.CostEstimate(flops=3600000000, bytes_accessed=16000000, transcendentals=0),
    )(info, shifts, cotangent.reshape(frames, rows * width, chans), k_mine, k_other)


def kernel_unit(spatial_kernel, temporal_kernel, half):
    both = jnp.concatenate(
        [spatial_kernel.transpose(1, 0, 2), temporal_kernel.transpose(1, 0, 2)], axis=0
    )
    start = (3 * lax.axis_index("x"), 0, lax.axis_index("core") * half)
    unit = lax.dynamic_slice(both, start, (3, both.shape[1], half))
    p = lax.axis_index("zh")
    slots = [unit]
    for k in range(1, 4):
        slots.append(lax.ppermute(unit, "zh", [(i, i ^ k) for i in range(4)]))
    slots = [jnp.where(p & 1, slots[k ^ 1], slots[k]) for k in range(4)]
    slots = [jnp.where(p & 2, slots[k ^ 2], slots[k]) for k in range(4)]
    return jnp.stack(slots, axis=1)


def kernel_parts(unit, waited):
    lower = jnp.concatenate(ring_gather(unit[:, :2], "y"))
    upper = jnp.concatenate(ring_gather(unit[:, 2:], "x"))
    lower, lower_rest = ring_gather(lower, "x")
    upper, upper_rest = ring_gather(upper, "y")
    rest, waited = lax.optimization_barrier(((lower_rest, upper_rest), waited))
    mine = (lower, rest[0], upper, rest[1])
    return mine, tuple(swap(part) for part in mine), waited


def per_device(activations, cotangent, spatial_kernel, temporal_kernel):
    frames, rows, width, chans = activations.shape
    count = frames * rows * width
    half = chans // 2
    core = lax.axis_index("core").astype(jnp.int32).reshape(1)
    own = spatial_kernel.shape[0]
    infos = [
        jnp.concatenate([core ^ turn, slots_in("x", turn), slots_in("y", turn)])
        for turn in range(2)
    ]

    unit = kernel_unit(spatial_kernel, temporal_kernel, half)
    x_wide = widened(activations, edges_of(activations, SPACE, 1), SPACE, 1)
    cot_pad = widened(cotangent, edges_of(cotangent, TM, 0), TM, 0)
    x_pair = swap(lax.dynamic_slice_in_dim(x_wide, (1 - core[0]) * half, half, axis=3))
    shifts = column_shifts(x_wide)
    cot_turned = cot_pad.reshape((frames + 2) * rows * width, chans).T
    waited = (shifts, cot_pad, cot_turned)
    parts, parts_other, (shifts, cot_pad, cot_turned) = kernel_parts(unit, waited)
    shifts_pair = column_shifts(x_pair)
    cot_turned_pair = swap(cot_turned)
    (shifts_pair, cot_turned_pair), parts_other = lax.optimization_barrier(
        ((shifts_pair, cot_turned_pair), parts_other)
    )

    k_mine, results = forward(infos, shifts, cot_pad, parts, parts_other)
    hid_mine, hid_other, slope_pre, turned, k_other = results
    turned_pair, hid_pair = swap(turned), swap(hid_other)
    slope_maps = slope_pre.reshape(frames, rows, width, chans)
    slope_edges = edges_of(slope_maps, SPACE, 1)
    operands = (
        turned,
        turned_pair,
        shifts,
        shifts_pair,
        cot_turned,
        cot_turned_pair,
        hid_mine.reshape(count, half),
        hid_pair.reshape(count, half),
    )
    info = jnp.concatenate([core, slots_of("x"), slots_of("y")])
    lower, sent_lower = weight_terms(0, own, info, *operands)
    upper, sent_upper = weight_terms(1, own, info, *operands)
    slope_edges, _ = lax.optimization_barrier((slope_edges, (sent_lower, sent_upper)))
    slope_wide = widened(slope_maps, slope_edges, SPACE, 1)
    grad = input_gradient(core, column_shifts(slope_wide), cotangent, k_mine, k_other)

    lower = ring_scatter(lower, sent_lower, "x", grad)
    upper = ring_scatter(upper, sent_upper, "y", grad)
    lower = ring_scatter(lower, lower[2:], "y")
    upper = ring_scatter(upper, upper[2:], "x")
    terms = jnp.concatenate([lower, upper], axis=1)
    terms = terms.reshape(3, 4, 2, own // 2, half).transpose(1, 2, 0, 3, 4)
    terms = scattered(terms.reshape(8, 3, own // 2, half), ("zh", "zl"))
    pixels = count * lax.axis_size(TM) * lax.axis_size(SPACE)
    terms = gathered(terms * (1.0 / math.sqrt(pixels)), ("x", "zl"))
    came = swap(terms)
    terms = jnp.concatenate(
        [jnp.where(core[0] == 0, terms, came), jnp.where(core[0] == 0, came, terms)], axis=3
    )
    terms = terms.reshape(4, 2, 3, own // 2, chans).transpose(0, 2, 1, 3, 4)
    spatial = terms[:3].reshape(9, own, chans).transpose(1, 0, 2)
    temporal = terms[3].reshape(3, own, chans).transpose(1, 0, 2)
    return grad.reshape(frames, rows, width, chans), spatial, temporal


def solution(mesh):
    split = Mesh(mesh.devices.reshape(4, 2, 2, 4, 4), TM + SPACE)
    maps = P(TM, SPACE, None, None)
    kernels = P(SPACE, None, None)
    return jax.shard_map(
        per_device,
        mesh=split,
        in_specs=(maps, maps, kernels, kernels),
        out_specs=(maps, kernels, kernels),
        check_vma=False,
    )
```

```python
import functools
import math

import jax
import jax.numpy as jnp
from jax import lax
from jax.experimental import pallas as pl
from jax.experimental.pallas import tpu as pltpu
from jax.sharding import Mesh, PartitionSpec as P

TM = ("x", "zl", "core")
SPACE = ("zh", "y")
PAIR = [(0, 1), (1, 0)]
ORDER = ((1, 3), (3, 1))
VMEM = pl.BlockSpec(memory_space=pltpu.VMEM)
ANY = pl.BlockSpec(memory_space=pl.ANY)
SMEM = pl.BlockSpec(memory_space=pltpu.SMEM)
PARAMS = pltpu.CompilerParams(vmem_limit_bytes=24 * 1024 * 1024)


def swap(block):
    return lax.ppermute(block, "core", PAIR)


def exchange(block, axis, stage):
    if axis == "x":
        names, number = ("x", "core"), lambda core, p: 2 * p + core
    else:
        names, number = ("core", axis), lambda core, p: 4 * core + p
    pairs = [
        (number(core, p), number(core, p ^ ORDER[core][stage]))
        for core in range(2)
        for p in range(4)
    ]
    return lax.ppermute(block, names, pairs)


def positions(axis):
    p = lax.axis_index(axis)
    core = lax.axis_index("core")
    return p, p ^ (1 + 2 * core), p ^ (3 - 2 * core), p ^ 2


def slots_of(axis):
    own, first, second, far = positions(axis)
    q = jnp.arange(4, dtype=jnp.int32)
    return jnp.where(q == own, 0, jnp.where(q == second, 1, jnp.where(q == first, 2, 3)))


def slots_in(axis, turn):
    p = lax.axis_index(axis)
    core = lax.axis_index("core") ^ turn
    return jnp.stack([p, p ^ (1 + 2 * core), p ^ (3 - 2 * core), p ^ 2]).astype(jnp.int32)


def ring_scatter(terms, sent, axis, waited):
    came = exchange(sent, axis, 0)
    came, _ = lax.optimization_barrier((came, waited))
    came = came.astype(jnp.float32)
    passed = (terms[1] + came[1]).astype(sent.dtype)
    return terms[0] + came[0] + exchange(passed, axis, 1).astype(jnp.float32)


def ring_gather(block, axis):
    pair = jnp.stack([block, exchange(block, axis, 0)])
    return pair, exchange(pair, axis, 1)


def turned_by(axis):
    return (lax.axis_index(axis) ^ jnp.arange(4)).astype(jnp.int32)


def direct(blocks, axis):
    came = {
        k: lax.ppermute(blocks[k], axis, [(i, i ^ k) for i in range(4)]) for k in (2, 1, 3)
    }
    return [blocks[0], came[1], came[2], came[3]]


def direct_scatter(terms, axis):
    blocks = [terms[0]] + [terms[k].astype(jnp.bfloat16) for k in range(1, 4)]
    first, *others = direct(blocks, axis)
    return first + sum(block.astype(jnp.float32) for block in others)


def gathered(block, axis):
    spread = jnp.broadcast_to(block[None], (lax.axis_size(axis),) + block.shape)
    return lax.all_to_all(spread, axis, 0, 0, tiled=True)


def scattered(block, axis):
    return jnp.sum(lax.all_to_all(block, axis, 0, 0, tiled=True).astype(jnp.float32), axis=0)


def edges_of(block, axis, dim):
    count = lax.axis_size(axis)
    forward = [(i, (i + 1) % count) for i in range(count)]
    backward = [(target, source) for source, target in forward]
    size = block.shape[dim]
    low = lax.ppermute(lax.slice_in_dim(block, size - 1, size, axis=dim), axis, forward)
    high = lax.ppermute(lax.slice_in_dim(block, 0, 1, axis=dim), axis, backward)
    return low, high


def widened(block, edges, axis, dim):
    low, high = edges
    index = lax.axis_index(axis)
    low = jnp.where(index == 0, jnp.zeros_like(low), low)
    high = jnp.where(index == lax.axis_size(axis) - 1, jnp.zeros_like(high), high)
    return jnp.concatenate([low, block, high], axis=dim)


def column_shifts(maps):
    edge = jnp.zeros_like(maps[:, :, :1])
    return jnp.stack(
        [
            jnp.concatenate([edge, maps[:, :, :-1]], axis=2),
            maps,
            jnp.concatenate([maps[:, :, 1:], edge], axis=2),
        ]
    )


def lanes(index, half):
    return pl.ds(pl.multiple_of(index * half, half), half)


def assemble(info_ref, parts, kernel_ref, sems):
    copies = []
    for pair in range(2):
        for j in range(2):
            slot = 2 * pair + j
            for t in range(4):
                x, y = info_ref[1 + slot], info_ref[13 + t]
                target = kernel_ref.at[x, pl.ds(0, 2), :, y]
                copies.append((parts[pair].at[j, t], target))
                x, y = info_ref[9 + t], info_ref[5 + slot]
                target = kernel_ref.at[x, pl.ds(2, 2), :, y]
                copies.append((parts[2 + pair].at[j, t], target))
    copies = [
        pltpu.make_async_copy(source, target, sems.at[i])
        for i, (source, target) in enumerate(copies)
    ]
    for copy in copies:
        copy.start()
    for copy in copies:
        copy.wait()


def add_terms(index, x_ref, cot_ref, kernel_ref, pre_ref, slope_ref, start_ref):
    frames, block, chans = pre_ref.shape
    half = chans // 2

    def convolve(f, _, a):
        if a > 0:
            total = pre_ref[f]
        elif start_ref is not None:
            total = start_ref[f]
        else:
            total = jnp.zeros((block, chans), jnp.float32)
        pieces = [
            x_ref[b, f, a : a + 2, :, lanes(index, half)].reshape(block, half) for b in range(3)
        ]
        kernels = [kernel_ref[a, :, b].reshape(chans, half) for b in range(3)]
        total += lax.dot_general(
            jnp.concatenate(pieces, axis=1),
            jnp.concatenate(kernels, axis=1),
            (((1,), (1,)), ((), ())),
            preferred_element_type=jnp.float32,
        )
        pre_ref[f] = total
        return 0

    def blend(f, _):
        pieces = [cot_ref[2 - k + f].reshape(block, chans) for k in range(3)]
        kernels = [kernel_ref[3, :, k].reshape(chans, half) for k in range(3)]
        slope_ref[f] = jnp.dot(
            jnp.concatenate(pieces, axis=1),
            jnp.concatenate(kernels, axis=0),
            preferred_element_type=jnp.float32,
        )
        return 0

    for a in range(3):
        lax.fori_loop(0, frames, functools.partial(convolve, a=a), 0)
    lax.fori_loop(0, frames, blend, 0)


def first_kernel(info_ref, x_ref, cot_ref, *refs):
    parts, (pre_ref, slope_ref, kernel_ref, sems) = refs[:4], refs[4:]
    assemble(info_ref, parts, kernel_ref, sems)
    add_terms(info_ref[0], x_ref, cot_ref, kernel_ref, pre_ref, slope_ref, None)


def second_kernel(info_ref, x_ref, cot_ref, *refs):
    parts, (start_ref, mine_ref), refs = refs[:4], refs[4:6], refs[6:]
    hid_mine_ref, hid_other_ref, slope_ref, turned_ref, kernel_ref = refs[:5]
    pre_ref, other_ref, work_ref, sems = refs[5:]
    assemble(info_ref, parts, kernel_ref, sems)
    other = info_ref[0]
    add_terms(other, x_ref, cot_ref, kernel_ref, pre_ref, other_ref, start_ref)
    frames, block, chans = pre_ref.shape
    half = chans // 2
    part = 32
    for hid_ref, source_ref, index in (
        (hid_mine_ref, mine_ref, 1 - other),
        (hid_other_ref, other_ref, other),
    ):

        def finish(step, _, hid_ref=hid_ref, source_ref=source_ref, index=index):
            f, r = step // (block // part), step % (block // part)
            rows = pl.ds(pl.multiple_of(r * part, part), part)
            pre = pre_ref[f, rows, lanes(index, half)]
            sigma = 1.0 / (1.0 + jnp.exp(-pre))
            hid_ref[f, rows] = (pre * sigma).astype(jnp.bfloat16)
            slope = source_ref[f, rows] * sigma * (1.0 + pre * (1.0 - sigma))
            work_ref[f, rows, lanes(index, half)] = slope
            return 0

        lax.fori_loop(0, frames * (block // part), finish, 0)
    for f in range(frames):
        slope = work_ref[f].astype(jnp.bfloat16)
        slope_ref[f] = slope
        turned_ref[:, f * block : (f + 1) * block] = slope.T


def forward(infos, shifts, cot_pad, parts, parts_other):
    frames, _, width, chans = shifts.shape[1:]
    block = 2 * width
    half = chans // 2
    full = jax.ShapeDtypeStruct((frames, block, chans), jnp.float32)
    part = jax.ShapeDtypeStruct((frames, block, half), jnp.float32)
    hid = jax.ShapeDtypeStruct((frames, block, half), jnp.bfloat16)
    kernel = jax.ShapeDtypeStruct((4, 4, 3, 4) + parts[0].shape[-2:], parts[0].dtype)
    sems = pltpu.SemaphoreType.DMA((32,))
    pre, mine, k_mine = pl.pallas_call(
        first_kernel,
        out_shape=(full, part, kernel),
        in_specs=[SMEM, VMEM, VMEM] + [ANY] * 4,
        out_specs=(VMEM,) * 3,
        scratch_shapes=[sems],
        compiler_params=PARAMS,
        cost_estimate=pl.CostEstimate(flops=3200000000, bytes_accessed=12000000, transcendentals=0),
    )(infos[0], shifts, cot_pad, *parts)
    results = pl.pallas_call(
        second_kernel,
        out_shape=(
            hid,
            hid,
            jax.ShapeDtypeStruct((frames, block, chans), jnp.bfloat16),
            jax.ShapeDtypeStruct((chans, frames * block), jnp.bfloat16),
            kernel,
        ),
        in_specs=[SMEM, VMEM, VMEM] + [ANY] * 4 + [VMEM] * 2,
        out_specs=(VMEM,) * 5,
        scratch_shapes=[
            pltpu.VMEM(full.shape, jnp.float32),
            pltpu.VMEM(part.shape, jnp.float32),
            pltpu.VMEM(full.shape, jnp.float32),
            sems,
        ],
        compiler_params=PARAMS,
        cost_estimate=pl.CostEstimate(flops=3200000000, bytes_accessed=15000000, transcendentals=0),
    )(infos[1], shifts, cot_pad, *parts_other, pre, mine)
    return k_mine, results


def weight_kernel(
    upper,
    info_ref,
    turned_ref,
    turned_pair_ref,
    x_ref,
    x_pair_ref,
    cot_ref,
    cot_pair_ref,
    hid_ref,
    hid_pair_ref,
    terms_ref,
    sent_ref,
):
    half = x_pair_ref.shape[-1]
    count = turned_ref.shape[1]
    block = count // 2
    own = terms_ref.shape[-2]
    outs = pl.ds(half * upper, half)

    def keep(total, group, b):
        for zh in range(2):
            for y in range(4):
                row = (4 * zh + y) * own
                if upper:
                    slots = info_ref[5 + y], info_ref[9 + group]
                else:
                    slots = info_ref[1 + group], info_ref[13 + y]
                terms_ref[slots[0], slots[1], b, zh] = total[row : row + own]

    def spatial(a, _):
        for b in range(3):
            mine = x_ref[b, :, pl.ds(a, 2), :, lanes(info_ref[0], half)].reshape(count, half)
            other = x_pair_ref[b, :, pl.ds(a, 2)].reshape(count, half)
            total = jnp.dot(
                jnp.concatenate([turned_ref[outs], turned_pair_ref[outs]], axis=1),
                jnp.concatenate([mine, other], axis=0),
                preferred_element_type=jnp.float32,
            )
            keep(total, a, b)
        return 0

    lax.fori_loop(0, 3, spatial, 0)
    for k in range(3):
        span = slice((2 - k) * block, (4 - k) * block)
        total = jnp.dot(
            jnp.concatenate([cot_ref[outs, span], cot_pair_ref[outs, span]], axis=1),
            jnp.concatenate([hid_ref[...], hid_pair_ref[...]], axis=0),
            preferred_element_type=jnp.float32,
        )
        keep(total, 3, k)
    for slot in range(2):
        for i in range(4):
            sent_ref[slot, i] = terms_ref[2 + slot, i].astype(jnp.bfloat16)


def weight_terms(upper, own, info, *operands):
    half = operands[-1].shape[-1]
    shape = (4, 4, 3, 2, own, half)
    return pl.pallas_call(
        functools.partial(weight_kernel, upper),
        out_shape=(
            jax.ShapeDtypeStruct(shape, jnp.float32),
            jax.ShapeDtypeStruct((2,) + shape[1:], jnp.bfloat16),
        ),
        in_specs=[SMEM] + [VMEM] * 8,
        out_specs=(VMEM, VMEM),
        compiler_params=PARAMS,
        cost_estimate=pl.CostEstimate(flops=2400000000, bytes_accessed=16000000, transcendentals=0),
    )(info, *operands)


def grad_kernel(info_ref, x_ref, cot_ref, mine_ref, other_ref, out_ref):
    frames, block, chans = out_ref.shape
    half = chans // 2
    for kernel_ref, index in ((mine_ref, info_ref[0]), (other_ref, 1 - info_ref[0])):
        for a in range(3):

            def convolve(f, _, kernel_ref=kernel_ref, index=index, a=a):
                if a > 0:
                    total = out_ref[f, :, lanes(index, half)]
                else:
                    total = cot_ref[f, :, lanes(index, half)].astype(jnp.float32)
                pieces = [x_ref[2 - b, f, 2 - a : 4 - a].reshape(block, chans) for b in range(3)]
                kernels = [kernel_ref[a, :, b].reshape(chans, half) for b in range(3)]
                total += jnp.dot(
                    jnp.concatenate(pieces, axis=1),
                    jnp.concatenate(kernels, axis=0),
                    preferred_element_type=jnp.float32,
                )
                out_ref[f, :, lanes(index, half)] = total
                return 0

            lax.fori_loop(0, frames, convolve, 0)


def input_gradient(info, shifts, cotangent, k_mine, k_other):
    frames, rows, width, chans = cotangent.shape
    return pl.pallas_call(
        grad_kernel,
        out_shape=jax.ShapeDtypeStruct((frames, rows * width, chans), jnp.float32),
        in_specs=[SMEM] + [VMEM] * 4,
        out_specs=VMEM,
        compiler_params=PARAMS,
        cost_estimate=pl.CostEstimate(flops=3600000000, bytes_accessed=16000000, transcendentals=0),
    )(info, shifts, cotangent.reshape(frames, rows * width, chans), k_mine, k_other)


def kernel_unit(spatial_kernel, temporal_kernel, half):
    both = jnp.concatenate(
        [spatial_kernel.transpose(1, 0, 2), temporal_kernel.transpose(1, 0, 2)], axis=0
    )
    start = (3 * lax.axis_index("x"), 0, lax.axis_index("core") * half)
    unit = lax.dynamic_slice(both, start, (3, both.shape[1], half))
    p = lax.axis_index("zh")
    slots = direct([unit] * 4, "zh")
    slots = [jnp.where(p & 1, slots[k ^ 1], slots[k]) for k in range(4)]
    slots = [jnp.where(p & 2, slots[k ^ 2], slots[k]) for k in range(4)]
    return jnp.stack(slots[:2]), jnp.stack(slots[2:])


def kernel_parts(unit, waited):
    lower, upper = unit
    lower = jnp.stack(direct([lower] * 4, "y"))
    upper = jnp.stack(direct([upper] * 4, "x"))
    lower, lower_rest = ring_gather(lower, "x")
    upper, upper_rest = ring_gather(upper, "y")
    rest, waited = lax.optimization_barrier(((lower_rest, upper_rest), waited))
    mine = (lower, rest[0], upper, rest[1])
    return mine, tuple(swap(part) for part in mine), waited


def per_device(activations, cotangent, spatial_kernel, temporal_kernel):
    frames, rows, width, chans = activations.shape
    count = frames * rows * width
    half = chans // 2
    core = lax.axis_index("core").astype(jnp.int32).reshape(1)
    own = spatial_kernel.shape[0]
    infos = [
        jnp.concatenate(
            [
                core ^ turn,
                slots_in("x", turn),
                slots_in("y", turn),
                turned_by("x"),
                turned_by("y"),
            ]
        )
        for turn in range(2)
    ]

    unit = kernel_unit(spatial_kernel, temporal_kernel, half)
    x_wide = widened(activations, edges_of(activations, SPACE, 1), SPACE, 1)
    cot_pad = widened(cotangent, edges_of(cotangent, TM, 0), TM, 0)
    x_pair = swap(lax.dynamic_slice_in_dim(x_wide, (1 - core[0]) * half, half, axis=3))
    shifts = column_shifts(x_wide)
    cot_turned = cot_pad.reshape((frames + 2) * rows * width, chans).T
    waited = (shifts, cot_pad, cot_turned)
    parts, parts_other, (shifts, cot_pad, cot_turned) = kernel_parts(unit, waited)
    cot_turned_pair = swap(cot_turned)
    cot_turned_pair, parts_other = lax.optimization_barrier((cot_turned_pair, parts_other))

    k_mine, results = forward(infos, shifts, cot_pad, parts, parts_other)
    hid_mine, hid_other, slope_pre, turned, k_other = results
    turned_pair, hid_pair = swap(turned), swap(hid_other)
    x_pair, _ = lax.optimization_barrier((x_pair, turned))
    shifts_pair = column_shifts(x_pair)
    slope_maps = slope_pre.reshape(frames, rows, width, chans)
    slope_edges = edges_of(slope_maps, SPACE, 1)
    operands = (
        turned,
        turned_pair,
        shifts,
        shifts_pair,
        cot_turned,
        cot_turned_pair,
        hid_mine.reshape(count, half),
        hid_pair.reshape(count, half),
    )
    info = jnp.concatenate(
        [core, slots_of("x"), slots_of("y"), turned_by("x"), turned_by("y")]
    )
    lower, sent_lower = weight_terms(0, own, info, *operands)
    upper, sent_upper = weight_terms(1, own, info, *operands)
    slope_edges, _ = lax.optimization_barrier((slope_edges, (sent_lower, sent_upper)))
    slope_wide = widened(slope_maps, slope_edges, SPACE, 1)
    grad = input_gradient(core, column_shifts(slope_wide), cotangent, k_mine, k_other)

    lower = ring_scatter(lower, sent_lower, "x", grad)
    upper = ring_scatter(upper, sent_upper, "y", grad)
    lower = direct_scatter(lower, "y")
    upper = direct_scatter(upper, "x")
    terms = jnp.concatenate([lower, upper], axis=1)
    terms = terms.reshape(3, 4, 2, own // 2, half).transpose(1, 2, 0, 3, 4)
    terms = scattered(terms.reshape(8, 3, own // 2, half), ("zh", "zl"))
    pixels = count * lax.axis_size(TM) * lax.axis_size(SPACE)
    terms = gathered(terms * (1.0 / math.sqrt(pixels)), ("x", "zl"))
    came = swap(terms)
    terms = jnp.concatenate(
        [jnp.where(core[0] == 0, terms, came), jnp.where(core[0] == 0, came, terms)], axis=3
    )
    terms = terms.reshape(4, 2, 3, own // 2, chans).transpose(0, 2, 1, 3, 4)
    spatial = terms[:3].reshape(9, own, chans).transpose(1, 0, 2)
    temporal = terms[3].reshape(3, own, chans).transpose(1, 0, 2)
    return grad.reshape(frames, rows, width, chans), spatial, temporal


def solution(mesh):
    split = Mesh(mesh.devices.reshape(4, 2, 2, 4, 4), TM + SPACE)
    maps = P(TM, SPACE, None, None)
    kernels = P(SPACE, None, None)
    return jax.shard_map(
        per_device,
        mesh=split,
        in_specs=(maps, maps, kernels, kernels),
        out_specs=(maps, kernels, kernels),
        check_vma=False,
    )
```

```python
import functools
import math

import jax
import jax.numpy as jnp
from jax import lax
from jax.experimental import pallas as pl
from jax.experimental.pallas import tpu as pltpu
from jax.sharding import Mesh, PartitionSpec as P

TM = ("x", "zl", "core")
SPACE = ("zh", "y")
PAIR = [(0, 1), (1, 0)]
ORDER = ((1, 3), (3, 1))
VMEM = pl.BlockSpec(memory_space=pltpu.VMEM)
ANY = pl.BlockSpec(memory_space=pl.ANY)
SMEM = pl.BlockSpec(memory_space=pltpu.SMEM)
PARAMS = pltpu.CompilerParams(vmem_limit_bytes=12 * 1024 * 1024)


def swap(block):
    return lax.ppermute(block, "core", PAIR)


def exchange(block, axis, stage):
    if axis == "x":
        names, number = ("x", "core"), lambda core, p: 2 * p + core
    else:
        names, number = ("core", axis), lambda core, p: 4 * core + p
    pairs = [
        (number(core, p), number(core, p ^ ORDER[core][stage]))
        for core in range(2)
        for p in range(4)
    ]
    return lax.ppermute(block, names, pairs)


def positions(axis):
    p = lax.axis_index(axis)
    core = lax.axis_index("core")
    return p, p ^ (1 + 2 * core), p ^ (3 - 2 * core), p ^ 2


def slots_of(axis):
    own, first, second, far = positions(axis)
    q = jnp.arange(4, dtype=jnp.int32)
    return jnp.where(q == own, 0, jnp.where(q == second, 1, jnp.where(q == first, 2, 3)))


def slots_in(axis, turn):
    p = lax.axis_index(axis)
    core = lax.axis_index("core") ^ turn
    return jnp.stack([p, p ^ (1 + 2 * core), p ^ (3 - 2 * core), p ^ 2]).astype(jnp.int32)


def widen(block):
    return block.astype(jnp.float32)


def ring_scatter(terms, sent, axis):
    came = exchange(sent, axis, 0)
    passed = (terms[1] + widen(came[1])).astype(sent.dtype)
    return terms[0] + widen(came[0]) + widen(exchange(passed, axis, 1))


def ring_gather(block, axis):
    pair = jnp.stack([block, exchange(block, axis, 0)])
    return pair, exchange(pair, axis, 1)


def gathered(block, axis):
    spread = jnp.broadcast_to(block[None], (lax.axis_size(axis),) + block.shape)
    return lax.all_to_all(spread, axis, 0, 0, tiled=True)


def scattered(block, axis):
    return jnp.sum(lax.all_to_all(block, axis, 0, 0, tiled=True).astype(jnp.float32), axis=0)


def edges_of(block, axis, dim):
    count = lax.axis_size(axis)
    forward = [(i, (i + 1) % count) for i in range(count)]
    backward = [(target, source) for source, target in forward]
    size = block.shape[dim]
    low = lax.ppermute(lax.slice_in_dim(block, size - 1, size, axis=dim), axis, forward)
    high = lax.ppermute(lax.slice_in_dim(block, 0, 1, axis=dim), axis, backward)
    return low, high


def widened(block, edges, axis, dim):
    low, high = edges
    index = lax.axis_index(axis)
    low = jnp.where(index == 0, jnp.zeros_like(low), low)
    high = jnp.where(index == lax.axis_size(axis) - 1, jnp.zeros_like(high), high)
    return jnp.concatenate([low, block, high], axis=dim)


def column_shifts(maps):
    edge = jnp.zeros_like(maps[:, :, :1])
    return jnp.stack(
        [
            jnp.concatenate([edge, maps[:, :, :-1]], axis=2),
            maps,
            jnp.concatenate([maps[:, :, 1:], edge], axis=2),
        ]
    )


def lanes(index, half):
    return pl.ds(pl.multiple_of(index * half, half), half)


def assemble(info_ref, parts, kernel_ref, sems):
    copies = []
    for pair in range(2):
        for j in range(2):
            slot = 2 * pair + j
            for t in range(4):
                x, y = info_ref[1 + slot], info_ref[5 + t]
                target = kernel_ref.at[x, pl.ds(0, 2), :, y]
                copies.append((parts[pair].at[j, t], target))
                x, y = info_ref[1 + t], info_ref[5 + slot]
                target = kernel_ref.at[x, pl.ds(2, 2), :, y]
                copies.append((parts[2 + pair].at[j, t], target))
    copies = [
        pltpu.make_async_copy(source, target, sems.at[i])
        for i, (source, target) in enumerate(copies)
    ]
    for copy in copies:
        copy.start()
    for copy in copies:
        copy.wait()


def add_terms(index, x_ref, cot_ref, kernel_ref, pre_ref, slope_ref, start_ref):
    frames, block, chans = pre_ref.shape
    half = chans // 2

    def convolve(f, _, a):
        if a > 0:
            total = pre_ref[f]
        elif start_ref is not None:
            total = start_ref[f]
        else:
            total = jnp.zeros((block, chans), jnp.float32)
        for b in range(3):
            piece = x_ref[b, f, a : a + 2, :, lanes(index, half)].reshape(block, half)
            total += lax.dot_general(
                piece,
                kernel_ref[a, :, b].reshape(chans, half),
                (((1,), (1,)), ((), ())),
                preferred_element_type=jnp.float32,
            )
        pre_ref[f] = total
        return 0

    def blend(f, _):
        total = jnp.zeros((block, half), jnp.float32)
        for k in range(3):
            piece = cot_ref[2 - k + f].reshape(block, chans)
            kernel = kernel_ref[3, :, k].reshape(chans, half)
            total += jnp.dot(piece, kernel, preferred_element_type=jnp.float32)
        slope_ref[f] = total
        return 0

    for a in range(3):
        lax.fori_loop(0, frames, functools.partial(convolve, a=a), 0)
    lax.fori_loop(0, frames, blend, 0)


def first_kernel(info_ref, x_ref, cot_ref, *refs):
    parts, (pre_ref, slope_ref, kernel_ref, sems) = refs[:4], refs[4:]
    assemble(info_ref, parts, kernel_ref, sems)
    add_terms(info_ref[0], x_ref, cot_ref, kernel_ref, pre_ref, slope_ref, None)


def second_kernel(info_ref, x_ref, cot_ref, *refs):
    parts, (start_ref, mine_ref), refs = refs[:4], refs[4:6], refs[6:]
    hid_mine_ref, hid_other_ref, slope_ref, turned_ref, kernel_ref = refs[:5]
    pre_ref, other_ref, work_ref, sems = refs[5:]
    assemble(info_ref, parts, kernel_ref, sems)
    other = info_ref[0]
    add_terms(other, x_ref, cot_ref, kernel_ref, pre_ref, other_ref, start_ref)
    frames, block, chans = pre_ref.shape
    half = chans // 2
    part = 32
    for hid_ref, source_ref, index in (
        (hid_mine_ref, mine_ref, 1 - other),
        (hid_other_ref, other_ref, other),
    ):

        def finish(step, _, hid_ref=hid_ref, source_ref=source_ref, index=index):
            f, r = step // (block // part), step % (block // part)
            rows = pl.ds(pl.multiple_of(r * part, part), part)
            pre = pre_ref[f, rows, lanes(index, half)]
            sigma = 1.0 / (1.0 + jnp.exp(-pre))
            hid_ref[f, rows] = (pre * sigma).astype(jnp.bfloat16)
            slope = source_ref[f, rows] * sigma * (1.0 + pre * (1.0 - sigma))
            work_ref[f, rows, lanes(index, half)] = slope
            return 0

        lax.fori_loop(0, frames * (block // part), finish, 0)
    for f in range(frames):
        slope = work_ref[f].astype(jnp.bfloat16)
        slope_ref[f] = slope
        turned_ref[:, f * block : (f + 1) * block] = slope.T


def forward(infos, shifts, cot_pad, parts, parts_other):
    frames, _, width, chans = shifts.shape[1:]
    block = 2 * width
    half = chans // 2
    full = jax.ShapeDtypeStruct((frames, block, chans), jnp.float32)
    part = jax.ShapeDtypeStruct((frames, block, half), jnp.float32)
    hid = jax.ShapeDtypeStruct((frames, block, half), jnp.bfloat16)
    kernel = jax.ShapeDtypeStruct((4, 4, 3, 4) + parts[0].shape[-2:], parts[0].dtype)
    sems = pltpu.SemaphoreType.DMA((32,))
    pre, mine, k_mine = pl.pallas_call(
        first_kernel,
        out_shape=(full, part, kernel),
        in_specs=[SMEM, VMEM, VMEM] + [ANY] * 4,
        out_specs=(VMEM,) * 3,
        scratch_shapes=[sems],
        compiler_params=PARAMS,
        cost_estimate=pl.CostEstimate(flops=3200000000, bytes_accessed=12000000, transcendentals=0),
    )(infos[0], shifts, cot_pad, *parts)
    results = pl.pallas_call(
        second_kernel,
        out_shape=(
            hid,
            hid,
            jax.ShapeDtypeStruct((frames, block, chans), jnp.bfloat16),
            jax.ShapeDtypeStruct((chans, frames * block), jnp.bfloat16),
            kernel,
        ),
        in_specs=[SMEM, VMEM, VMEM] + [ANY] * 4 + [VMEM] * 2,
        out_specs=(VMEM,) * 5,
        scratch_shapes=[
            pltpu.VMEM(full.shape, jnp.float32),
            pltpu.VMEM(part.shape, jnp.float32),
            pltpu.VMEM(full.shape, jnp.float32),
            sems,
        ],
        compiler_params=PARAMS,
        cost_estimate=pl.CostEstimate(flops=3200000000, bytes_accessed=15000000, transcendentals=0),
    )(infos[1], shifts, cot_pad, *parts_other, pre, mine)
    return k_mine, results


def weight_kernel(
    upper,
    info_ref,
    turned_ref,
    turned_pair_ref,
    x_ref,
    x_pair_ref,
    cot_ref,
    cot_pair_ref,
    hid_ref,
    hid_pair_ref,
    terms_ref,
    sent_ref,
):
    half = x_pair_ref.shape[-1]
    count = turned_ref.shape[1]
    block = count // 2
    own = terms_ref.shape[-2]
    outs = pl.ds(half * upper, half)

    def keep(total, group, b):
        for zh in range(2):
            for y in range(4):
                row = (4 * zh + y) * own
                slots = info_ref[1 + group], info_ref[5 + y]
                slots = slots[::-1] if upper else slots
                terms_ref[slots[0], slots[1], b, zh] = total[row : row + own]

    def spatial(a, _):
        for b in range(3):
            piece = x_ref[b, :, pl.ds(a, 2), :, lanes(info_ref[0], half)].reshape(count, half)
            total = jnp.dot(turned_ref[outs], piece, preferred_element_type=jnp.float32)
            piece = x_pair_ref[b, :, pl.ds(a, 2)].reshape(count, half)
            total += jnp.dot(turned_pair_ref[outs], piece, preferred_element_type=jnp.float32)
            keep(total, a, b)
        return 0

    lax.fori_loop(0, 3, spatial, 0)
    for k in range(3):
        piece = cot_ref[outs, (2 - k) * block : (4 - k) * block]
        total = jnp.dot(piece, hid_ref[...], preferred_element_type=jnp.float32)
        piece = cot_pair_ref[outs, (2 - k) * block : (4 - k) * block]
        total += jnp.dot(piece, hid_pair_ref[...], preferred_element_type=jnp.float32)
        keep(total, 3, k)
    for slot in range(2):
        for i in range(4):
            sent_ref[slot, i] = terms_ref[2 + slot, i].astype(jnp.bfloat16)


def weight_terms(upper, own, info, *operands):
    half = operands[-1].shape[-1]
    shape = (4, 4, 3, 2, own, half)
    return pl.pallas_call(
        functools.partial(weight_kernel, upper),
        out_shape=(
            jax.ShapeDtypeStruct(shape, jnp.float32),
            jax.ShapeDtypeStruct((2,) + shape[1:], jnp.bfloat16),
        ),
        in_specs=[SMEM] + [VMEM] * 8,
        out_specs=(VMEM, VMEM),
        compiler_params=PARAMS,
        cost_estimate=pl.CostEstimate(flops=2400000000, bytes_accessed=16000000, transcendentals=0),
    )(info, *operands)


def grad_kernel(f, info_ref, x_ref, cot_ref, mine_ref, other_ref, *refs):
    out_ref = refs[-1]
    block, chans = out_ref.shape[1:]
    half = chans // 2
    for kernel_ref, index in ((mine_ref, info_ref[0]), (other_ref, 1 - info_ref[0])):

        def convolve(a, _, kernel_ref=kernel_ref, index=index):
            total = out_ref[0, :, lanes(index, half)]
            for b in range(3):
                piece = x_ref[2 - b, f, pl.ds(2 - a, 2)].reshape(block, chans)
                kernel = kernel_ref[a, :, b].reshape(chans, half)
                total += jnp.dot(piece, kernel, preferred_element_type=jnp.float32)
            out_ref[0, :, lanes(index, half)] = total
            return 0

        out_ref[0, :, lanes(index, half)] = cot_ref[f, :, lanes(index, half)].astype(jnp.float32)
        lax.fori_loop(0, 3, convolve, 0)


def input_gradient(f, info, shifts, cotangent, k_mine, k_other, earlier=()):
    frames, rows, width, chans = cotangent.shape
    block = pl.BlockSpec((1, rows * width, chans), lambda i: (f, 0, 0))
    whole = [pl.BlockSpec(memory_space=pltpu.VMEM)] * 4
    return pl.pallas_call(
        functools.partial(grad_kernel, f),
        grid=(1,),
        out_shape=jax.ShapeDtypeStruct((frames, rows * width, chans), jnp.float32),
        in_specs=[SMEM] + whole + [ANY] * len(earlier),
        out_specs=block,
        input_output_aliases={5: 0} if earlier else {},
        compiler_params=PARAMS,
        cost_estimate=pl.CostEstimate(flops=1800000000, bytes_accessed=8000000, transcendentals=0),
    )(info, shifts, cotangent.reshape(frames, rows * width, chans), k_mine, k_other, *earlier)


def kernel_unit(spatial_kernel, temporal_kernel, half):
    both = jnp.concatenate(
        [spatial_kernel.transpose(1, 0, 2), temporal_kernel.transpose(1, 0, 2)], axis=0
    )
    start = (3 * lax.axis_index("x"), 0, lax.axis_index("core") * half)
    unit = lax.dynamic_slice(both, start, (3, both.shape[1], half))
    p = lax.axis_index("zh")
    slots = [unit]
    for k in range(1, 4):
        slots.append(lax.ppermute(unit, "zh", [(i, i ^ k) for i in range(4)]))
    slots = [jnp.where(p & 1, slots[k ^ 1], slots[k]) for k in range(4)]
    slots = [jnp.where(p & 2, slots[k ^ 2], slots[k]) for k in range(4)]
    return jnp.stack(slots[:2]), jnp.stack(slots[2:])


def kernel_parts(unit, waited):
    lower = jnp.concatenate(ring_gather(unit[0], "y"))
    upper = jnp.concatenate(ring_gather(unit[1], "x"))
    lower, lower_rest = ring_gather(lower, "x")
    upper, upper_rest = ring_gather(upper, "y")
    rest, waited = lax.optimization_barrier(((lower_rest, upper_rest), waited))
    mine = (lower, rest[0], upper, rest[1])
    return mine, tuple(swap(part) for part in mine), waited


def per_device(activations, cotangent, spatial_kernel, temporal_kernel):
    frames, rows, width, chans = activations.shape
    count = frames * rows * width
    half = chans // 2
    core = lax.axis_index("core").astype(jnp.int32).reshape(1)
    own = spatial_kernel.shape[0]
    infos = [
        jnp.concatenate([core ^ turn, slots_in("x", turn), slots_in("y", turn)])
        for turn in range(2)
    ]

    unit = kernel_unit(spatial_kernel, temporal_kernel, half)
    x_wide = widened(activations, edges_of(activations, SPACE, 1), SPACE, 1)
    cot_pad = widened(cotangent, edges_of(cotangent, TM, 0), TM, 0)
    x_pair = swap(lax.dynamic_slice_in_dim(x_wide, (1 - core[0]) * half, half, axis=3))
    shifts = column_shifts(x_wide)
    cot_turned = cot_pad.reshape((frames + 2) * rows * width, chans).T
    waited = (shifts, cot_pad, cot_turned)
    parts, parts_other, (shifts, cot_pad, cot_turned) = kernel_parts(unit, waited)
    cot_turned_pair = swap(cot_turned)
    cot_turned_pair, parts_other = lax.optimization_barrier((cot_turned_pair, parts_other))

    k_mine, results = forward(infos, shifts, cot_pad, parts, parts_other)
    hid_mine, hid_other, slope_pre, turned, k_other = results
    turned_pair, hid_pair = swap(turned), swap(hid_other)
    x_pair, _ = lax.optimization_barrier((x_pair, turned))
    shifts_pair = column_shifts(x_pair)
    slope_maps = slope_pre.reshape(frames, rows, width, chans)
    slope_edges = edges_of(slope_maps, SPACE, 1)
    operands = (
        turned,
        turned_pair,
        shifts,
        shifts_pair,
        cot_turned,
        cot_turned_pair,
        hid_mine.reshape(count, half),
        hid_pair.reshape(count, half),
    )
    info = jnp.concatenate([core, slots_of("x"), slots_of("y")])
    lower, sent_lower = weight_terms(0, own, info, *operands)
    upper, sent_upper = weight_terms(1, own, info, *operands)
    slope_edges, _ = lax.optimization_barrier((slope_edges, (sent_lower, sent_upper)))
    slope_wide = widened(slope_maps, slope_edges, SPACE, 1)
    shifts_slope = column_shifts(slope_wide)
    grad = input_gradient(0, core, shifts_slope, cotangent, k_mine, k_other)

    came_lower = exchange(sent_lower, "x", 0)
    came_upper = exchange(sent_upper, "y", 0)
    came_lower, grad = lax.optimization_barrier((came_lower, grad))
    passed = (lower[1] + widen(came_lower[1])).astype(jnp.bfloat16)
    info, _ = lax.optimization_barrier((core, passed))
    grad = input_gradient(1, info, shifts_slope, cotangent, k_mine, k_other, (grad,))
    last_lower = exchange(passed, "x", 1)
    came_upper, grad = lax.optimization_barrier((came_upper, grad))
    passed = (upper[1] + widen(came_upper[1])).astype(jnp.bfloat16)
    last_upper = exchange(passed, "y", 1)

    def total(terms, came, last, slots):
        return terms[0, slots] + widen(came[0, slots]) + widen(last[slots])

    keep, send = slice(0, 2), slice(2, 4)
    sent_lower = total(lower, came_lower, last_lower, send)
    sent_upper = total(upper, came_upper, last_upper, send)
    lower = ring_scatter(total(lower, came_lower, last_lower, keep), sent_lower, "y")
    upper = ring_scatter(total(upper, came_upper, last_upper, keep), sent_upper, "x")
    terms = jnp.concatenate([lower, upper], axis=1)
    terms = terms.reshape(3, 4, 2, own // 2, half).transpose(1, 2, 0, 3, 4)
    terms = terms.reshape(8, 3, own // 2, half).astype(jnp.bfloat16)
    terms = scattered(terms, ("zh", "zl"))
    pixels = count * lax.axis_size(TM) * lax.axis_size(SPACE)
    terms = gathered(terms * (1.0 / math.sqrt(pixels)), ("x", "zl"))
    came = swap(terms)
    terms = jnp.concatenate(
        [jnp.where(core[0] == 0, terms, came), jnp.where(core[0] == 0, came, terms)], axis=3
    )
    terms = terms.reshape(4, 2, 3, own // 2, chans).transpose(0, 2, 1, 3, 4)
    spatial = terms[:3].reshape(9, own, chans).transpose(1, 0, 2)
    temporal = terms[3].reshape(3, own, chans).transpose(1, 0, 2)
    return grad.reshape(frames, rows, width, chans), spatial, temporal


def solution(mesh):
    split = Mesh(mesh.devices.reshape(4, 2, 2, 4, 4), TM + SPACE)
    maps = P(TM, SPACE, None, None)
    kernels = P(SPACE, None, None)
    return jax.shard_map(
        per_device,
        mesh=split,
        in_specs=(maps, maps, kernels, kernels),
        out_specs=(maps, kernels, kernels),
        check_vma=False,
    )
```

```python
import functools
import math

import jax
import jax.numpy as jnp
from jax import lax
from jax.experimental import pallas as pl
from jax.experimental.pallas import tpu as pltpu
from jax.sharding import Mesh, PartitionSpec as P

TM = ("x", "zl", "core")
SPACE = ("zh", "y")
PAIR = [(0, 1), (1, 0)]
ORDER = ((1, 3), (3, 1))
VMEM = pl.BlockSpec(memory_space=pltpu.VMEM)
ANY = pl.BlockSpec(memory_space=pl.ANY)
SMEM = pl.BlockSpec(memory_space=pltpu.SMEM)
PARAMS = pltpu.CompilerParams(vmem_limit_bytes=12 * 1024 * 1024)


def swap(block):
    return lax.ppermute(block, "core", PAIR)


def exchange(block, axis, stage):
    if axis == "x":
        names, number = ("x", "core"), lambda core, p: 2 * p + core
    else:
        names, number = ("core", axis), lambda core, p: 4 * core + p
    pairs = [
        (number(core, p), number(core, p ^ ORDER[core][stage]))
        for core in range(2)
        for p in range(4)
    ]
    return lax.ppermute(block, names, pairs)


def positions(axis):
    p = lax.axis_index(axis)
    core = lax.axis_index("core")
    return p, p ^ (1 + 2 * core), p ^ (3 - 2 * core), p ^ 2


def slots_of(axis):
    own, first, second, far = positions(axis)
    q = jnp.arange(4, dtype=jnp.int32)
    return jnp.where(q == own, 0, jnp.where(q == second, 1, jnp.where(q == first, 2, 3)))


def slots_in(axis, turn):
    p = lax.axis_index(axis)
    core = lax.axis_index("core") ^ turn
    return jnp.stack([p, p ^ (1 + 2 * core), p ^ (3 - 2 * core), p ^ 2]).astype(jnp.int32)


def widen(block):
    return block.astype(jnp.float32)


def ring_scatter(terms, sent, axis):
    came = exchange(sent, axis, 0)
    passed = (terms[1] + widen(came[1])).astype(sent.dtype)
    return terms[0] + widen(came[0]) + widen(exchange(passed, axis, 1))


def ring_gather(block, axis):
    pair = jnp.stack([block, exchange(block, axis, 0)])
    return pair, exchange(pair, axis, 1)


def gathered(block, axis):
    spread = jnp.broadcast_to(block[None], (lax.axis_size(axis),) + block.shape)
    return lax.all_to_all(spread, axis, 0, 0, tiled=True)


def scattered(block, axis):
    return jnp.sum(lax.all_to_all(block, axis, 0, 0, tiled=True).astype(jnp.float32), axis=0)


def edges_of(block, axis, dim):
    count = lax.axis_size(axis)
    forward = [(i, (i + 1) % count) for i in range(count)]
    backward = [(target, source) for source, target in forward]
    size = block.shape[dim]
    low = lax.ppermute(lax.slice_in_dim(block, size - 1, size, axis=dim), axis, forward)
    high = lax.ppermute(lax.slice_in_dim(block, 0, 1, axis=dim), axis, backward)
    return low, high


def widened(block, edges, axis, dim):
    low, high = edges
    index = lax.axis_index(axis)
    low = jnp.where(index == 0, jnp.zeros_like(low), low)
    high = jnp.where(index == lax.axis_size(axis) - 1, jnp.zeros_like(high), high)
    return jnp.concatenate([low, block, high], axis=dim)


def column_shifts(maps):
    edge = jnp.zeros_like(maps[:, :, :1])
    left = jnp.concatenate([edge, maps[:, :, :-1]], axis=2)
    right = jnp.concatenate([maps[:, :, 1:], edge], axis=2)
    return left, maps, right


def lanes(index, half):
    return pl.ds(pl.multiple_of(index * half, half), half)


def assemble(info_ref, parts, kernel_ref, sems):
    copies = []
    for slot in range(4):
        for t in range(4):
            x, y = info_ref[1 + slot], info_ref[5 + t]
            copies.append((parts[slot].at[t], kernel_ref.at[x, pl.ds(0, 2), :, y]))
            x, y = info_ref[1 + t], info_ref[5 + slot]
            copies.append((parts[4 + slot].at[t], kernel_ref.at[x, pl.ds(2, 2), :, y]))
    copies = [
        pltpu.make_async_copy(source, target, sems.at[i])
        for i, (source, target) in enumerate(copies)
    ]
    for copy in copies:
        copy.start()
    for copy in copies:
        copy.wait()


def add_terms(index, x_refs, cot_ref, kernel_ref, pre_ref, slope_ref, start_ref):
    frames, block, chans = pre_ref.shape
    half = chans // 2

    def convolve(f, _, a):
        if a > 0:
            total = pre_ref[f]
        elif start_ref is not None:
            total = start_ref[f]
        else:
            total = jnp.zeros((block, chans), jnp.float32)
        for b in range(3):
            piece = x_refs[b][f, a : a + 2, :, lanes(index, half)].reshape(block, half)
            total += lax.dot_general(
                piece,
                kernel_ref[a, :, b].reshape(chans, half),
                (((1,), (1,)), ((), ())),
                preferred_element_type=jnp.float32,
            )
        pre_ref[f] = total
        return 0

    def blend(f, _):
        total = jnp.zeros((block, half), jnp.float32)
        for k in range(3):
            piece = cot_ref[2 - k + f].reshape(block, chans)
            kernel = kernel_ref[3, :, k].reshape(chans, half)
            total += jnp.dot(piece, kernel, preferred_element_type=jnp.float32)
        slope_ref[f] = total
        return 0

    for a in range(3):
        lax.fori_loop(0, frames, functools.partial(convolve, a=a), 0)
    lax.fori_loop(0, frames, blend, 0)


def first_kernel(info_ref, *refs):
    x_refs, cot_ref, parts, refs = refs[:3], refs[3], refs[4:12], refs[12:]
    pre_ref, slope_ref, kernel_ref, sems = refs
    assemble(info_ref, parts, kernel_ref, sems)
    add_terms(info_ref[0], x_refs, cot_ref, kernel_ref, pre_ref, slope_ref, None)


def second_kernel(info_ref, *refs):
    x_refs, cot_ref, parts, refs = refs[:3], refs[3], refs[4:12], refs[12:]
    start_ref, mine_ref, hid_mine_ref, hid_other_ref, slope_ref, turned_ref = refs[:6]
    kernel_ref, pre_ref, other_ref, work_ref, sems = refs[6:]
    assemble(info_ref, parts, kernel_ref, sems)
    other = info_ref[0]
    add_terms(other, x_refs, cot_ref, kernel_ref, pre_ref, other_ref, start_ref)
    frames, block, chans = pre_ref.shape
    half = chans // 2
    part = 32
    for hid_ref, source_ref, index in (
        (hid_mine_ref, mine_ref, 1 - other),
        (hid_other_ref, other_ref, other),
    ):

        def finish(step, _, hid_ref=hid_ref, source_ref=source_ref, index=index):
            f, r = step // (block // part), step % (block // part)
            rows = pl.ds(pl.multiple_of(r * part, part), part)
            pre = pre_ref[f, rows, lanes(index, half)]
            sigma = 1.0 / (1.0 + jnp.exp(-pre))
            hid_ref[f, rows] = (pre * sigma).astype(jnp.bfloat16)
            slope = source_ref[f, rows] * sigma * (1.0 + pre * (1.0 - sigma))
            work_ref[f, rows, lanes(index, half)] = slope
            return 0

        lax.fori_loop(0, frames * (block // part), finish, 0)
    for f in range(frames):
        slope = work_ref[f].astype(jnp.bfloat16)
        slope_ref[f] = slope
        turned_ref[:, f * block : (f + 1) * block] = slope.T


def forward(infos, shifts, cot_pad, parts, parts_other):
    frames, _, width, chans = shifts[0].shape
    block = 2 * width
    half = chans // 2
    full = jax.ShapeDtypeStruct((frames, block, chans), jnp.float32)
    part = jax.ShapeDtypeStruct((frames, block, half), jnp.float32)
    hid = jax.ShapeDtypeStruct((frames, block, half), jnp.bfloat16)
    kernel = jax.ShapeDtypeStruct((4, 4, 3, 4) + parts[0].shape[-2:], parts[0].dtype)
    sems = pltpu.SemaphoreType.DMA((32,))
    pre, mine, k_mine = pl.pallas_call(
        first_kernel,
        out_shape=(full, part, kernel),
        in_specs=[SMEM] + [VMEM] * 4 + [ANY] * 8,
        out_specs=(VMEM,) * 3,
        scratch_shapes=[sems],
        compiler_params=PARAMS,
        cost_estimate=pl.CostEstimate(flops=3200000000, bytes_accessed=12000000, transcendentals=0),
    )(infos[0], *shifts, cot_pad, *parts)
    results = pl.pallas_call(
        second_kernel,
        out_shape=(
            hid,
            hid,
            jax.ShapeDtypeStruct((frames, block, chans), jnp.bfloat16),
            jax.ShapeDtypeStruct((chans, frames * block), jnp.bfloat16),
            kernel,
        ),
        in_specs=[SMEM] + [VMEM] * 4 + [ANY] * 8 + [VMEM] * 2,
        out_specs=(VMEM,) * 5,
        scratch_shapes=[
            pltpu.VMEM(full.shape, jnp.float32),
            pltpu.VMEM(part.shape, jnp.float32),
            pltpu.VMEM(full.shape, jnp.float32),
            sems,
        ],
        compiler_params=PARAMS,
        cost_estimate=pl.CostEstimate(flops=3200000000, bytes_accessed=15000000, transcendentals=0),
    )(infos[1], *shifts, cot_pad, *parts_other, pre, mine)
    return k_mine, results


def weight_kernel(upper, info_ref, turned_ref, turned_pair_ref, *refs):
    x_refs, x_pair_refs, refs = refs[:3], refs[3:6], refs[6:]
    cot_ref, cot_pair_ref, hid_ref, hid_pair_ref, terms_ref, sent_ref = refs
    half = hid_ref.shape[-1]
    count = turned_ref.shape[1]
    block = count // 2
    own = terms_ref.shape[-2]
    outs = pl.ds(half * upper, half)

    def keep(total, group, b):
        for zh in range(2):
            for y in range(4):
                row = (4 * zh + y) * own
                slots = info_ref[1 + group], info_ref[5 + y]
                slots = slots[::-1] if upper else slots
                terms_ref[slots[0], slots[1], b, zh] = total[row : row + own]

    def spatial(a, _):
        for b in range(3):
            piece = x_refs[b][:, pl.ds(a, 2), :, lanes(info_ref[0], half)].reshape(count, half)
            total = jnp.dot(turned_ref[outs], piece, preferred_element_type=jnp.float32)
            piece = x_pair_refs[b][:, pl.ds(a, 2)].reshape(count, half)
            total += jnp.dot(turned_pair_ref[outs], piece, preferred_element_type=jnp.float32)
            keep(total, a, b)
        return 0

    lax.fori_loop(0, 3, spatial, 0)
    for k in range(3):
        piece = cot_ref[outs, (2 - k) * block : (4 - k) * block]
        total = jnp.dot(piece, hid_ref[...], preferred_element_type=jnp.float32)
        piece = cot_pair_ref[outs, (2 - k) * block : (4 - k) * block]
        total += jnp.dot(piece, hid_pair_ref[...], preferred_element_type=jnp.float32)
        keep(total, 3, k)
    for slot in range(2):
        for i in range(4):
            sent_ref[slot, i] = terms_ref[2 + slot, i].astype(jnp.bfloat16)


def weight_terms(upper, own, info, *operands):
    half = operands[-1].shape[-1]
    shape = (4, 4, 3, 2, own, half)
    return pl.pallas_call(
        functools.partial(weight_kernel, upper),
        out_shape=(
            jax.ShapeDtypeStruct(shape, jnp.float32),
            jax.ShapeDtypeStruct((2,) + shape[1:], jnp.bfloat16),
        ),
        in_specs=[SMEM] + [VMEM] * 12,
        out_specs=(VMEM, VMEM),
        compiler_params=PARAMS,
        cost_estimate=pl.CostEstimate(flops=2400000000, bytes_accessed=16000000, transcendentals=0),
    )(info, *operands)


def grad_kernel(f, info_ref, *refs):
    x_refs, cot_ref, mine_ref, other_ref, out_ref = refs[:3], *refs[3:6], refs[-1]
    block, chans = out_ref.shape[1:]
    half = chans // 2
    for kernel_ref, index in ((mine_ref, info_ref[0]), (other_ref, 1 - info_ref[0])):

        def convolve(a, _, kernel_ref=kernel_ref, index=index):
            total = out_ref[0, :, lanes(index, half)]
            for b in range(3):
                piece = x_refs[2 - b][f, pl.ds(2 - a, 2)].reshape(block, chans)
                kernel = kernel_ref[a, :, b].reshape(chans, half)
                total += jnp.dot(piece, kernel, preferred_element_type=jnp.float32)
            out_ref[0, :, lanes(index, half)] = total
            return 0

        out_ref[0, :, lanes(index, half)] = cot_ref[f, :, lanes(index, half)].astype(jnp.float32)
        lax.fori_loop(0, 3, convolve, 0)


def input_gradient(f, info, shifts, cotangent, k_mine, k_other, earlier=()):
    frames, rows, width, chans = cotangent.shape
    block = pl.BlockSpec((1, rows * width, chans), lambda i: (f, 0, 0))
    whole = [pl.BlockSpec(memory_space=pltpu.VMEM)] * 6
    return pl.pallas_call(
        functools.partial(grad_kernel, f),
        grid=(1,),
        out_shape=jax.ShapeDtypeStruct((frames, rows * width, chans), jnp.float32),
        in_specs=[SMEM] + whole + [ANY] * len(earlier),
        out_specs=block,
        input_output_aliases={7: 0} if earlier else {},
        compiler_params=PARAMS,
        cost_estimate=pl.CostEstimate(flops=1800000000, bytes_accessed=8000000, transcendentals=0),
    )(info, *shifts, cotangent.reshape(frames, rows * width, chans), k_mine, k_other, *earlier)


def kernel_unit(spatial_kernel, temporal_kernel, half):
    both = jnp.concatenate(
        [spatial_kernel.transpose(1, 0, 2), temporal_kernel.transpose(1, 0, 2)], axis=0
    )
    start = (3 * lax.axis_index("x"), 0, lax.axis_index("core") * half)
    unit = lax.dynamic_slice(both, start, (3, both.shape[1], half))
    p = lax.axis_index("zh")
    slots = [unit]
    for k in range(1, 4):
        slots.append(lax.ppermute(unit, "zh", [(i, i ^ k) for i in range(4)]))
    slots = [jnp.where(p & 1, slots[k ^ 1], slots[k]) for k in range(4)]
    slots = [jnp.where(p & 2, slots[k ^ 2], slots[k]) for k in range(4)]
    return jnp.stack(slots[:2]), jnp.stack(slots[2:])


def kernel_parts(unit, ready):
    lower = jnp.concatenate(ring_gather(unit[0], "y"))
    upper = jnp.concatenate(ring_gather(unit[1], "x"))
    near = exchange(lower, "x", 0), exchange(upper, "y", 0)
    second = exchange(lower, "x", 1), exchange(upper, "y", 1)
    near, second, ready = lax.optimization_barrier((near, second, ready))
    far = exchange(near[0], "x", 1), exchange(near[1], "y", 1)
    parts = (lower, near[0], second[0], far[0], upper, near[1], second[1], far[1])
    return parts, ready


def per_device(activations, cotangent, spatial_kernel, temporal_kernel):
    frames, rows, width, chans = activations.shape
    count = frames * rows * width
    half = chans // 2
    core = lax.axis_index("core").astype(jnp.int32).reshape(1)
    own = spatial_kernel.shape[0]
    infos = [
        jnp.concatenate([core ^ turn, slots_in("x", turn), slots_in("y", turn)])
        for turn in range(2)
    ]

    unit = kernel_unit(spatial_kernel, temporal_kernel, half)
    edges = edges_of(activations, SPACE, 1), edges_of(cotangent, TM, 0)
    x_wide = widened(activations, edges[0], SPACE, 1)
    x_other = lax.dynamic_slice_in_dim(x_wide, (1 - core[0]) * half, half, axis=3)
    shifts = column_shifts(x_wide)
    cot_pad = widened(cotangent, edges[1], TM, 0)
    cot_turned = cot_pad.reshape((frames + 2) * rows * width, chans).T
    ready = (shifts, cot_pad, cot_turned, x_other)
    parts, ready = kernel_parts(unit, ready)
    shifts, cot_pad, cot_turned, x_other = ready
    parts_other = tuple(swap(part) for part in parts)
    x_pair = swap(x_other)
    cot_turned_pair = swap(cot_turned)
    cot_turned_pair, parts_other = lax.optimization_barrier((cot_turned_pair, parts_other))

    k_mine, results = forward(infos, shifts, cot_pad, parts, parts_other)
    hid_mine, hid_other, slope_pre, turned, k_other = results
    turned_pair, hid_pair = swap(turned), swap(hid_other)
    x_pair, _ = lax.optimization_barrier((x_pair, turned))
    shifts_pair = column_shifts(x_pair)
    slope_maps = slope_pre.reshape(frames, rows, width, chans)
    slope_edges = edges_of(slope_maps, SPACE, 1)
    operands = (
        turned,
        turned_pair,
        *shifts,
        *shifts_pair,
        cot_turned,
        cot_turned_pair,
        hid_mine.reshape(count, half),
        hid_pair.reshape(count, half),
    )
    info = jnp.concatenate([core, slots_of("x"), slots_of("y")])
    lower, sent_lower = weight_terms(0, own, info, *operands)
    upper, sent_upper = weight_terms(1, own, info, *operands)
    slope_edges, _ = lax.optimization_barrier((slope_edges, (sent_lower, sent_upper)))
    slope_wide = widened(slope_maps, slope_edges, SPACE, 1)
    shifts_slope = column_shifts(slope_wide)
    grad = input_gradient(0, core, shifts_slope, cotangent, k_mine, k_other)

    came_lower = exchange(sent_lower, "x", 0)
    came_upper = exchange(sent_upper, "y", 0)
    came_lower, grad = lax.optimization_barrier((came_lower, grad))
    passed = (lower[1] + widen(came_lower[1])).astype(jnp.bfloat16)
    info, _ = lax.optimization_barrier((core, passed))
    grad = input_gradient(1, info, shifts_slope, cotangent, k_mine, k_other, (grad,))
    last_lower = exchange(passed, "x", 1)
    came_upper, grad = lax.optimization_barrier((came_upper, grad))
    passed = (upper[1] + widen(came_upper[1])).astype(jnp.bfloat16)
    last_upper = exchange(passed, "y", 1)

    def total(terms, came, last, slots):
        return terms[0, slots] + widen(came[0, slots]) + widen(last[slots])

    keep, send = slice(0, 2), slice(2, 4)
    sent_lower = total(lower, came_lower, last_lower, send)
    sent_upper = total(upper, came_upper, last_upper, send)
    lower = ring_scatter(total(lower, came_lower, last_lower, keep), sent_lower, "y")
    upper = ring_scatter(total(upper, came_upper, last_upper, keep), sent_upper, "x")
    terms = jnp.concatenate([lower, upper], axis=1)
    terms = terms.reshape(3, 4, 2, own // 2, half).transpose(1, 2, 0, 3, 4)
    terms = terms.reshape(8, 3, own // 2, half).astype(jnp.bfloat16)
    terms = scattered(terms, ("zh", "zl"))
    pixels = count * lax.axis_size(TM) * lax.axis_size(SPACE)
    terms = gathered(terms * (1.0 / math.sqrt(pixels)), ("x", "zl"))
    came = swap(terms)
    terms = jnp.concatenate(
        [jnp.where(core[0] == 0, terms, came), jnp.where(core[0] == 0, came, terms)], axis=3
    )
    terms = terms.reshape(4, 2, 3, own // 2, chans).transpose(0, 2, 1, 3, 4)
    spatial = terms[:3].reshape(9, own, chans).transpose(1, 0, 2)
    temporal = terms[3].reshape(3, own, chans).transpose(1, 0, 2)
    return grad.reshape(frames, rows, width, chans), spatial, temporal


def solution(mesh):
    split = Mesh(mesh.devices.reshape(4, 2, 2, 4, 4), TM + SPACE)
    maps = P(TM, SPACE, None, None)
    kernels = P(SPACE, None, None)
    return jax.shard_map(
        per_device,
        mesh=split,
        in_specs=(maps, maps, kernels, kernels),
        out_specs=(maps, kernels, kernels),
        check_vma=False,
    )
```

```python
import functools
import math

import jax
import jax.numpy as jnp
from jax import lax
from jax.experimental import pallas as pl
from jax.experimental.pallas import tpu as pltpu
from jax.sharding import Mesh, PartitionSpec as P

TM = ("x", "zl", "core")
SPACE = ("zh", "y")
PAIR = [(0, 1), (1, 0)]
ORDER = ((1, 3), (3, 1))
VMEM = pl.BlockSpec(memory_space=pltpu.VMEM)
ANY = pl.BlockSpec(memory_space=pl.ANY)
SMEM = pl.BlockSpec(memory_space=pltpu.SMEM)
PARAMS = pltpu.CompilerParams(vmem_limit_bytes=12 * 1024 * 1024)


def swap(block):
    return lax.ppermute(block, "core", PAIR)


def exchange(block, axis, stage):
    if axis == "x":
        names, number = ("x", "core"), lambda core, p: 2 * p + core
    else:
        names, number = ("core", axis), lambda core, p: 4 * core + p
    pairs = [
        (number(core, p), number(core, p ^ ORDER[core][stage]))
        for core in range(2)
        for p in range(4)
    ]
    return lax.ppermute(block, names, pairs)


def positions(axis):
    p = lax.axis_index(axis)
    core = lax.axis_index("core")
    return p, p ^ (1 + 2 * core), p ^ (3 - 2 * core), p ^ 2


def slots_of(axis):
    own, first, second, far = positions(axis)
    q = jnp.arange(4, dtype=jnp.int32)
    return jnp.where(q == own, 0, jnp.where(q == second, 1, jnp.where(q == first, 2, 3)))


def slots_in(axis, turn):
    p = lax.axis_index(axis)
    core = lax.axis_index("core") ^ turn
    return jnp.stack([p, p ^ (1 + 2 * core), p ^ (3 - 2 * core), p ^ 2]).astype(jnp.int32)


def widen(block):
    return block.astype(jnp.float32)


def ring_scatter(terms, sent, axis):
    came = exchange(sent, axis, 0)
    passed = (terms[1] + widen(came[1])).astype(sent.dtype)
    return terms[0] + widen(came[0]) + widen(exchange(passed, axis, 1))


def ring_gather(block, axis):
    pair = jnp.stack([block, exchange(block, axis, 0)])
    return pair, exchange(pair, axis, 1)


def gathered(block, axis):
    spread = jnp.broadcast_to(block[None], (lax.axis_size(axis),) + block.shape)
    return lax.all_to_all(spread, axis, 0, 0, tiled=True)


def scattered(block, axis):
    return jnp.sum(lax.all_to_all(block, axis, 0, 0, tiled=True).astype(jnp.float32), axis=0)


def edges_of(block, axis, dim):
    count = lax.axis_size(axis)
    forward = [(i, (i + 1) % count) for i in range(count)]
    backward = [(target, source) for source, target in forward]
    size = block.shape[dim]
    low = lax.ppermute(lax.slice_in_dim(block, size - 1, size, axis=dim), axis, forward)
    high = lax.ppermute(lax.slice_in_dim(block, 0, 1, axis=dim), axis, backward)
    return low, high


def widened(block, edges, axis, dim):
    low, high = edges
    index = lax.axis_index(axis)
    low = jnp.where(index == 0, jnp.zeros_like(low), low)
    high = jnp.where(index == lax.axis_size(axis) - 1, jnp.zeros_like(high), high)
    return jnp.concatenate([low, block, high], axis=dim)


def column_shifts(maps):
    edge = jnp.zeros_like(maps[:, :, :1])
    left = jnp.concatenate([edge, maps[:, :, :-1]], axis=2)
    right = jnp.concatenate([maps[:, :, 1:], edge], axis=2)
    return left, maps, right


def lanes(index, half):
    return pl.ds(pl.multiple_of(index * half, half), half)


def assemble(info_ref, parts, kernel_ref, sems):
    copies = []
    for slot in range(4):
        for t in range(4):
            x, y = info_ref[1 + slot], info_ref[5 + t]
            source = parts[slot // 2].at[slot % 2, t]
            copies.append((source, kernel_ref.at[x, pl.ds(0, 2), :, y]))
            x, y = info_ref[1 + t], info_ref[5 + slot]
            source = parts[2 + slot // 2].at[slot % 2, t]
            copies.append((source, kernel_ref.at[x, pl.ds(2, 2), :, y]))
    copies = [
        pltpu.make_async_copy(source, target, sems.at[i])
        for i, (source, target) in enumerate(copies)
    ]
    for copy in copies:
        copy.start()
    for copy in copies:
        copy.wait()


def add_terms(index, x_refs, cot_ref, kernel_ref, pre_ref, slope_ref, start_ref):
    frames, block, chans = pre_ref.shape
    half = chans // 2

    def convolve(f, _, a):
        if a > 0:
            total = pre_ref[f]
        elif start_ref is not None:
            total = start_ref[f]
        else:
            total = jnp.zeros((block, chans), jnp.float32)
        for b in range(3):
            piece = x_refs[b][f, a : a + 2, :, lanes(index, half)].reshape(block, half)
            total += lax.dot_general(
                piece,
                kernel_ref[a, :, b].reshape(chans, half),
                (((1,), (1,)), ((), ())),
                preferred_element_type=jnp.float32,
            )
        pre_ref[f] = total
        return 0

    def blend(f, _):
        total = jnp.zeros((block, half), jnp.float32)
        for k in range(3):
            piece = cot_ref[2 - k + f].reshape(block, chans)
            kernel = kernel_ref[3, :, k].reshape(chans, half)
            total += jnp.dot(piece, kernel, preferred_element_type=jnp.float32)
        slope_ref[f] = total
        return 0

    for a in range(3):
        lax.fori_loop(0, frames, functools.partial(convolve, a=a), 0)
    lax.fori_loop(0, frames, blend, 0)


def first_kernel(info_ref, *refs):
    x_refs, cot_ref, parts, refs = refs[:3], refs[3], refs[4:8], refs[8:]
    pre_ref, slope_ref, kernel_ref, turned_ref, part_ref, sems = refs
    assemble(info_ref, parts, kernel_ref, sems)
    add_terms(info_ref[0], x_refs, cot_ref, kernel_ref, pre_ref, slope_ref, None)
    block, chans = pre_ref.shape[1:]
    for i in range(cot_ref.shape[0]):
        turned_ref[:, i * block : (i + 1) * block] = cot_ref[i].reshape(block, chans).T
    for f in range(part_ref.shape[0]):
        part_ref[f] = x_refs[1][f, :, :, lanes(1 - info_ref[0], chans // 2)]


def second_kernel(info_ref, *refs):
    x_refs, cot_ref, parts, refs = refs[:3], refs[3], refs[4:8], refs[8:]
    start_ref, mine_ref, hid_mine_ref, hid_other_ref, slope_ref, turned_ref = refs[:6]
    kernel_ref, pre_ref, other_ref, work_ref, sems = refs[6:]
    assemble(info_ref, parts, kernel_ref, sems)
    other = info_ref[0]
    add_terms(other, x_refs, cot_ref, kernel_ref, pre_ref, other_ref, start_ref)
    frames, block, chans = pre_ref.shape
    half = chans // 2
    part = 32
    for hid_ref, source_ref, index in (
        (hid_mine_ref, mine_ref, 1 - other),
        (hid_other_ref, other_ref, other),
    ):

        def finish(step, _, hid_ref=hid_ref, source_ref=source_ref, index=index):
            f, r = step // (block // part), step % (block // part)
            rows = pl.ds(pl.multiple_of(r * part, part), part)
            pre = pre_ref[f, rows, lanes(index, half)]
            sigma = 1.0 / (1.0 + jnp.exp(-pre))
            hid_ref[f, rows] = (pre * sigma).astype(jnp.bfloat16)
            slope = source_ref[f, rows] * sigma * (1.0 + pre * (1.0 - sigma))
            work_ref[f, rows, lanes(index, half)] = slope
            return 0

        lax.fori_loop(0, frames * (block // part), finish, 0)
    for f in range(frames):
        slope = work_ref[f].astype(jnp.bfloat16)
        slope_ref[f] = slope
        turned_ref[:, f * block : (f + 1) * block] = slope.T


def forward(infos, shifts, cot_pad, parts, parts_other):
    frames, _, width, chans = shifts[0].shape
    block = 2 * width
    half = chans // 2
    full = jax.ShapeDtypeStruct((frames, block, chans), jnp.float32)
    part = jax.ShapeDtypeStruct((frames, block, half), jnp.float32)
    hid = jax.ShapeDtypeStruct((frames, block, half), jnp.bfloat16)
    kernel = jax.ShapeDtypeStruct((4, 4, 3, 4) + parts[0].shape[-2:], parts[0].dtype)
    sems = pltpu.SemaphoreType.DMA((32,))
    turned = jax.ShapeDtypeStruct((chans, (frames + 2) * block), jnp.bfloat16)
    x_half = jax.ShapeDtypeStruct(shifts[0].shape[:3] + (half,), jnp.bfloat16)
    pre, mine, k_mine, cot_turned, x_other = pl.pallas_call(
        first_kernel,
        out_shape=(full, part, kernel, turned, x_half),
        in_specs=[SMEM] + [VMEM] * 4 + [ANY] * 4,
        out_specs=(VMEM,) * 5,
        scratch_shapes=[sems],
        compiler_params=PARAMS,
        cost_estimate=pl.CostEstimate(flops=3200000000, bytes_accessed=12000000, transcendentals=0),
    )(infos[0], *shifts, cot_pad, *parts)
    cot_turned_pair, x_pair = swap(cot_turned), swap(x_other)
    results = pl.pallas_call(
        second_kernel,
        out_shape=(
            hid,
            hid,
            jax.ShapeDtypeStruct((frames, block, chans), jnp.bfloat16),
            jax.ShapeDtypeStruct((chans, frames * block), jnp.bfloat16),
            kernel,
        ),
        in_specs=[SMEM] + [VMEM] * 4 + [ANY] * 4 + [VMEM] * 2,
        out_specs=(VMEM,) * 5,
        scratch_shapes=[
            pltpu.VMEM(full.shape, jnp.float32),
            pltpu.VMEM(part.shape, jnp.float32),
            pltpu.VMEM(full.shape, jnp.float32),
            sems,
        ],
        compiler_params=PARAMS,
        cost_estimate=pl.CostEstimate(flops=3200000000, bytes_accessed=15000000, transcendentals=0),
    )(infos[1], *shifts, cot_pad, *parts_other, pre, mine)
    return k_mine, (cot_turned, cot_turned_pair, x_pair), results


def weight_kernel(upper, info_ref, turned_ref, turned_pair_ref, *refs):
    x_refs, x_pair_refs, refs = refs[:3], refs[3:6], refs[6:]
    cot_ref, cot_pair_ref, hid_ref, hid_pair_ref, terms_ref, sent_ref = refs
    half = hid_ref.shape[-1]
    count = turned_ref.shape[1]
    block = count // 2
    own = terms_ref.shape[-2]
    outs = pl.ds(half * upper, half)

    def keep(total, group, b):
        for zh in range(2):
            for y in range(4):
                row = (4 * zh + y) * own
                slots = info_ref[1 + group], info_ref[5 + y]
                slots = slots[::-1] if upper else slots
                terms_ref[slots[0], slots[1], b, zh] = total[row : row + own]

    def spatial(a, _):
        for b in range(3):
            piece = x_refs[b][:, pl.ds(a, 2), :, lanes(info_ref[0], half)].reshape(count, half)
            total = jnp.dot(turned_ref[outs], piece, preferred_element_type=jnp.float32)
            piece = x_pair_refs[b][:, pl.ds(a, 2)].reshape(count, half)
            total += jnp.dot(turned_pair_ref[outs], piece, preferred_element_type=jnp.float32)
            keep(total, a, b)
        return 0

    lax.fori_loop(0, 3, spatial, 0)
    for k in range(3):
        piece = cot_ref[outs, (2 - k) * block : (4 - k) * block]
        total = jnp.dot(piece, hid_ref[...], preferred_element_type=jnp.float32)
        piece = cot_pair_ref[outs, (2 - k) * block : (4 - k) * block]
        total += jnp.dot(piece, hid_pair_ref[...], preferred_element_type=jnp.float32)
        keep(total, 3, k)
    for slot in range(2):
        for i in range(4):
            sent_ref[slot, i] = terms_ref[2 + slot, i].astype(jnp.bfloat16)


def weight_terms(upper, own, info, *operands):
    half = operands[-1].shape[-1]
    shape = (4, 4, 3, 2, own, half)
    return pl.pallas_call(
        functools.partial(weight_kernel, upper),
        out_shape=(
            jax.ShapeDtypeStruct(shape, jnp.float32),
            jax.ShapeDtypeStruct((2,) + shape[1:], jnp.bfloat16),
        ),
        in_specs=[SMEM] + [VMEM] * 12,
        out_specs=(VMEM, VMEM),
        compiler_params=PARAMS,
        cost_estimate=pl.CostEstimate(flops=2400000000, bytes_accessed=16000000, transcendentals=0),
    )(info, *operands)


def grad_kernel(f, info_ref, *refs):
    x_refs, cot_ref, mine_ref, other_ref, out_ref = refs[:3], *refs[3:6], refs[-1]
    block, chans = out_ref.shape[1:]
    half = chans // 2
    for kernel_ref, index in ((mine_ref, info_ref[0]), (other_ref, 1 - info_ref[0])):

        def convolve(a, _, kernel_ref=kernel_ref, index=index):
            total = out_ref[0, :, lanes(index, half)]
            for b in range(3):
                piece = x_refs[2 - b][f, pl.ds(2 - a, 2)].reshape(block, chans)
                kernel = kernel_ref[a, :, b].reshape(chans, half)
                total += jnp.dot(piece, kernel, preferred_element_type=jnp.float32)
            out_ref[0, :, lanes(index, half)] = total
            return 0

        out_ref[0, :, lanes(index, half)] = cot_ref[f, :, lanes(index, half)].astype(jnp.float32)
        lax.fori_loop(0, 3, convolve, 0)


def input_gradient(f, info, shifts, cotangent, k_mine, k_other, earlier=()):
    frames, rows, width, chans = cotangent.shape
    block = pl.BlockSpec((1, rows * width, chans), lambda i: (f, 0, 0))
    whole = [pl.BlockSpec(memory_space=pltpu.VMEM)] * 6
    return pl.pallas_call(
        functools.partial(grad_kernel, f),
        grid=(1,),
        out_shape=jax.ShapeDtypeStruct((frames, rows * width, chans), jnp.float32),
        in_specs=[SMEM] + whole + [ANY] * len(earlier),
        out_specs=block,
        input_output_aliases={7: 0} if earlier else {},
        compiler_params=PARAMS,
        cost_estimate=pl.CostEstimate(flops=1800000000, bytes_accessed=8000000, transcendentals=0),
    )(info, *shifts, cotangent.reshape(frames, rows * width, chans), k_mine, k_other, *earlier)


def kernel_unit(spatial_kernel, temporal_kernel, half):
    both = jnp.concatenate(
        [spatial_kernel.transpose(1, 0, 2), temporal_kernel.transpose(1, 0, 2)], axis=0
    )
    start = (3 * lax.axis_index("x"), 0, lax.axis_index("core") * half)
    unit = lax.dynamic_slice(both, start, (3, both.shape[1], half))
    p = lax.axis_index("zh")
    slots = [unit]
    for k in range(1, 4):
        slots.append(lax.ppermute(unit, "zh", [(i, i ^ k) for i in range(4)]))
    slots = [jnp.where(p & 1, slots[k ^ 1], slots[k]) for k in range(4)]
    slots = [jnp.where(p & 2, slots[k ^ 2], slots[k]) for k in range(4)]
    return jnp.stack(slots[:2]), jnp.stack(slots[2:])


def kernel_parts(unit, ready):
    lower = jnp.concatenate(ring_gather(unit[0], "y"))
    upper = jnp.concatenate(ring_gather(unit[1], "x"))
    lower, lower_rest = ring_gather(lower, "x")
    upper, upper_rest = ring_gather(upper, "y")
    rest, ready = lax.optimization_barrier(((lower_rest, upper_rest), ready))
    return (lower, rest[0], upper, rest[1]), ready


def per_device(activations, cotangent, spatial_kernel, temporal_kernel):
    frames, rows, width, chans = activations.shape
    count = frames * rows * width
    half = chans // 2
    core = lax.axis_index("core").astype(jnp.int32).reshape(1)
    own = spatial_kernel.shape[0]
    infos = [
        jnp.concatenate([core ^ turn, slots_in("x", turn), slots_in("y", turn)])
        for turn in range(2)
    ]

    unit = kernel_unit(spatial_kernel, temporal_kernel, half)
    edges = edges_of(activations, SPACE, 1), edges_of(cotangent, TM, 0)
    x_wide = widened(activations, edges[0], SPACE, 1)
    shifts = column_shifts(x_wide)
    cot_pad = widened(cotangent, edges[1], TM, 0)
    parts, (shifts, cot_pad) = kernel_parts(unit, (shifts, cot_pad))
    parts_other = tuple(swap(part) for part in parts)
    k_mine, swapped, results = forward(infos, shifts, cot_pad, parts, parts_other)
    cot_turned, cot_turned_pair, x_pair = swapped
    hid_mine, hid_other, slope_pre, turned, k_other = results
    turned_pair, hid_pair = swap(turned), swap(hid_other)
    x_pair, _ = lax.optimization_barrier((x_pair, turned))
    shifts_pair = column_shifts(x_pair)
    slope_maps = slope_pre.reshape(frames, rows, width, chans)
    slope_edges = edges_of(slope_maps, SPACE, 1)
    operands = (
        turned,
        turned_pair,
        *shifts,
        *shifts_pair,
        cot_turned,
        cot_turned_pair,
        hid_mine.reshape(count, half),
        hid_pair.reshape(count, half),
    )
    info = jnp.concatenate([core, slots_of("x"), slots_of("y")])
    lower, sent_lower = weight_terms(0, own, info, *operands)
    upper, sent_upper = weight_terms(1, own, info, *operands)
    slope_edges, _ = lax.optimization_barrier((slope_edges, (sent_lower, sent_upper)))
    slope_wide = widened(slope_maps, slope_edges, SPACE, 1)
    shifts_slope = column_shifts(slope_wide)
    grad = input_gradient(0, core, shifts_slope, cotangent, k_mine, k_other)

    came_lower = exchange(sent_lower, "x", 0)
    came_upper = exchange(sent_upper, "y", 0)
    came_lower, grad = lax.optimization_barrier((came_lower, grad))
    passed = (lower[1] + widen(came_lower[1])).astype(jnp.bfloat16)
    info, _ = lax.optimization_barrier((core, passed))
    grad = input_gradient(1, info, shifts_slope, cotangent, k_mine, k_other, (grad,))
    last_lower = exchange(passed, "x", 1)
    came_upper, grad = lax.optimization_barrier((came_upper, grad))
    passed = (upper[1] + widen(came_upper[1])).astype(jnp.bfloat16)
    last_upper = exchange(passed, "y", 1)

    def total(terms, came, last, slots):
        return terms[0, slots] + widen(came[0, slots]) + widen(last[slots])

    keep, send = slice(0, 2), slice(2, 4)
    sent_lower = total(lower, came_lower, last_lower, send)
    sent_upper = total(upper, came_upper, last_upper, send)
    lower = ring_scatter(total(lower, came_lower, last_lower, keep), sent_lower, "y")
    upper = ring_scatter(total(upper, came_upper, last_upper, keep), sent_upper, "x")
    terms = jnp.concatenate([lower, upper], axis=1)
    terms = terms.reshape(3, 4, 2, own // 2, half).transpose(1, 2, 0, 3, 4)
    terms = terms.reshape(8, 3, own // 2, half).astype(jnp.bfloat16)
    terms = scattered(terms, ("zh", "zl"))
    pixels = count * lax.axis_size(TM) * lax.axis_size(SPACE)
    terms = gathered(terms * (1.0 / math.sqrt(pixels)), ("x", "zl"))
    came = swap(terms)
    terms = jnp.concatenate(
        [jnp.where(core[0] == 0, terms, came), jnp.where(core[0] == 0, came, terms)], axis=3
    )
    terms = terms.reshape(4, 2, 3, own // 2, chans).transpose(0, 2, 1, 3, 4)
    spatial = terms[:3].reshape(9, own, chans).transpose(1, 0, 2)
    temporal = terms[3].reshape(3, own, chans).transpose(1, 0, 2)
    return grad.reshape(frames, rows, width, chans), spatial, temporal


def solution(mesh):
    split = Mesh(mesh.devices.reshape(4, 2, 2, 4, 4), TM + SPACE)
    maps = P(TM, SPACE, None, None)
    kernels = P(SPACE, None, None)
    return jax.shard_map(
        per_device,
        mesh=split,
        in_specs=(maps, maps, kernels, kernels),
        out_specs=(maps, kernels, kernels),
        check_vma=False,
    )
```

```python
import functools
import math

import jax
import jax.numpy as jnp
from jax import lax
from jax.experimental import pallas as pl
from jax.experimental.pallas import tpu as pltpu
from jax.sharding import Mesh, PartitionSpec as P

TM = ("x", "zl", "core")
SPACE = ("zh", "y")
PAIR = [(0, 1), (1, 0)]
ORDER = ((1, 3), (3, 1))
VMEM = pl.BlockSpec(memory_space=pltpu.VMEM)
ANY = pl.BlockSpec(memory_space=pl.ANY)
SMEM = pl.BlockSpec(memory_space=pltpu.SMEM)
PARAMS = pltpu.CompilerParams(vmem_limit_bytes=24 * 1024 * 1024)


def swap(block):
    return lax.ppermute(block, "core", PAIR)


def exchange(block, axis, stage):
    if axis == "x":
        names, number = ("x", "core"), lambda core, p: 2 * p + core
    else:
        names, number = ("core", axis), lambda core, p: 4 * core + p
    pairs = [
        (number(core, p), number(core, p ^ ORDER[core][stage]))
        for core in range(2)
        for p in range(4)
    ]
    return lax.ppermute(block, names, pairs)


def positions(axis):
    p = lax.axis_index(axis)
    core = lax.axis_index("core")
    return p, p ^ (1 + 2 * core), p ^ (3 - 2 * core), p ^ 2


def slots_of(axis):
    own, first, second, far = positions(axis)
    q = jnp.arange(4, dtype=jnp.int32)
    return jnp.where(q == own, 0, jnp.where(q == second, 1, jnp.where(q == first, 2, 3)))


def slots_in(axis, turn):
    p = lax.axis_index(axis)
    core = lax.axis_index("core") ^ turn
    return jnp.stack([p, p ^ (1 + 2 * core), p ^ (3 - 2 * core), p ^ 2]).astype(jnp.int32)


def widen(block):
    return block.astype(jnp.float32)


def ring_scatter(terms, sent, axis):
    came = exchange(sent, axis, 0)
    passed = (terms[1] + widen(came[1])).astype(sent.dtype)
    return terms[0] + widen(came[0]) + widen(exchange(passed, axis, 1))


def ring_gather(block, axis):
    pair = jnp.stack([block, exchange(block, axis, 0)])
    return pair, exchange(pair, axis, 1)


def gathered(block, axis):
    spread = jnp.broadcast_to(block[None], (lax.axis_size(axis),) + block.shape)
    return lax.all_to_all(spread, axis, 0, 0, tiled=True)


def scattered(block, axis):
    return jnp.sum(lax.all_to_all(block, axis, 0, 0, tiled=True).astype(jnp.float32), axis=0)


def edges_of(block, axis, dim):
    count = lax.axis_size(axis)
    forward = [(i, (i + 1) % count) for i in range(count)]
    backward = [(target, source) for source, target in forward]
    size = block.shape[dim]
    low = lax.ppermute(lax.slice_in_dim(block, size - 1, size, axis=dim), axis, forward)
    high = lax.ppermute(lax.slice_in_dim(block, 0, 1, axis=dim), axis, backward)
    return low, high


def widened(block, edges, axis, dim):
    low, high = edges
    index = lax.axis_index(axis)
    low = jnp.where(index == 0, jnp.zeros_like(low), low)
    high = jnp.where(index == lax.axis_size(axis) - 1, jnp.zeros_like(high), high)
    return jnp.concatenate([low, block, high], axis=dim)


def column_shifts(maps):
    edge = jnp.zeros_like(maps[:, :, :1])
    return jnp.stack(
        [
            jnp.concatenate([edge, maps[:, :, :-1]], axis=2),
            maps,
            jnp.concatenate([maps[:, :, 1:], edge], axis=2),
        ]
    )


def lanes(index, half):
    return pl.ds(pl.multiple_of(index * half, half), half)


def assemble(info_ref, parts, kernel_ref, sems):
    copies = []
    for pair in range(2):
        for j in range(2):
            slot = 2 * pair + j
            for t in range(4):
                x, y = info_ref[1 + slot], info_ref[5 + t]
                target = kernel_ref.at[x, pl.ds(0, 2), :, y]
                copies.append((parts[pair].at[j, t], target))
                x, y = info_ref[1 + t], info_ref[5 + slot]
                target = kernel_ref.at[x, pl.ds(2, 2), :, y]
                copies.append((parts[2 + pair].at[j, t], target))
    copies = [
        pltpu.make_async_copy(source, target, sems.at[i])
        for i, (source, target) in enumerate(copies)
    ]
    for copy in copies:
        copy.start()
    for copy in copies:
        copy.wait()


def add_terms(index, x_ref, cot_ref, kernel_ref, pre_ref, slope_ref, start_ref):
    frames, block, chans = pre_ref.shape
    half = chans // 2

    def convolve(f, _, a):
        if a > 0:
            total = pre_ref[f]
        elif start_ref is not None:
            total = start_ref[f]
        else:
            total = jnp.zeros((block, chans), jnp.float32)
        for b in range(3):
            piece = x_ref[b, f, a : a + 2, :, lanes(index, half)].reshape(block, half)
            total += lax.dot_general(
                piece,
                kernel_ref[a, :, b].reshape(chans, half),
                (((1,), (1,)), ((), ())),
                preferred_element_type=jnp.float32,
            )
        pre_ref[f] = total
        return 0

    def blend(f, _):
        total = jnp.zeros((block, half), jnp.float32)
        for k in range(3):
            piece = cot_ref[2 - k + f].reshape(block, chans)
            kernel = kernel_ref[3, :, k].reshape(chans, half)
            total += jnp.dot(piece, kernel, preferred_element_type=jnp.float32)
        slope_ref[f] = total
        return 0

    for a in range(3):
        lax.fori_loop(0, frames, functools.partial(convolve, a=a), 0)
    lax.fori_loop(0, frames, blend, 0)


def first_kernel(info_ref, x_ref, cot_ref, *refs):
    parts, (pre_ref, slope_ref, kernel_ref, sems) = refs[:4], refs[4:]
    assemble(info_ref, parts, kernel_ref, sems)
    add_terms(info_ref[0], x_ref, cot_ref, kernel_ref, pre_ref, slope_ref, None)


def second_kernel(info_ref, x_ref, cot_ref, *refs):
    parts, (start_ref, mine_ref), refs = refs[:4], refs[4:6], refs[6:]
    hid_mine_ref, hid_other_ref, slope_ref, turned_ref, kernel_ref = refs[:5]
    pre_ref, other_ref, work_ref, sems = refs[5:]
    assemble(info_ref, parts, kernel_ref, sems)
    other = info_ref[0]
    add_terms(other, x_ref, cot_ref, kernel_ref, pre_ref, other_ref, start_ref)
    frames, block, chans = pre_ref.shape
    half = chans // 2
    part = 32
    for hid_ref, source_ref, index in (
        (hid_mine_ref, mine_ref, 1 - other),
        (hid_other_ref, other_ref, other),
    ):

        def finish(step, _, hid_ref=hid_ref, source_ref=source_ref, index=index):
            f, r = step // (block // part), step % (block // part)
            rows = pl.ds(pl.multiple_of(r * part, part), part)
            pre = pre_ref[f, rows, lanes(index, half)]
            sigma = 1.0 / (1.0 + jnp.exp(-pre))
            hid_ref[f, rows] = (pre * sigma).astype(jnp.bfloat16)
            slope = source_ref[f, rows] * sigma * (1.0 + pre * (1.0 - sigma))
            work_ref[f, rows, lanes(index, half)] = slope
            return 0

        lax.fori_loop(0, frames * (block // part), finish, 0)
    for f in range(frames):
        slope = work_ref[f].astype(jnp.bfloat16)
        slope_ref[f] = slope
        turned_ref[:, f * block : (f + 1) * block] = slope.T


def forward(infos, shifts, cot_pad, parts, parts_other):
    frames, _, width, chans = shifts.shape[1:]
    block = 2 * width
    half = chans // 2
    full = jax.ShapeDtypeStruct((frames, block, chans), jnp.float32)
    part = jax.ShapeDtypeStruct((frames, block, half), jnp.float32)
    hid = jax.ShapeDtypeStruct((frames, block, half), jnp.bfloat16)
    kernel = jax.ShapeDtypeStruct((4, 4, 3, 4) + parts[0].shape[-2:], parts[0].dtype)
    sems = pltpu.SemaphoreType.DMA((32,))
    pre, mine, k_mine = pl.pallas_call(
        first_kernel,
        out_shape=(full, part, kernel),
        in_specs=[SMEM, VMEM, VMEM] + [ANY] * 4,
        out_specs=(VMEM,) * 3,
        scratch_shapes=[sems],
        compiler_params=PARAMS,
        cost_estimate=pl.CostEstimate(flops=3200000000, bytes_accessed=12000000, transcendentals=0),
    )(infos[0], shifts, cot_pad, *parts)
    results = pl.pallas_call(
        second_kernel,
        out_shape=(
            hid,
            hid,
            jax.ShapeDtypeStruct((frames, block, chans), jnp.bfloat16),
            jax.ShapeDtypeStruct((chans, frames * block), jnp.bfloat16),
            kernel,
        ),
        in_specs=[SMEM, VMEM, VMEM] + [ANY] * 4 + [VMEM] * 2,
        out_specs=(VMEM,) * 5,
        scratch_shapes=[
            pltpu.VMEM(full.shape, jnp.float32),
            pltpu.VMEM(part.shape, jnp.float32),
            pltpu.VMEM(full.shape, jnp.float32),
            sems,
        ],
        compiler_params=PARAMS,
        cost_estimate=pl.CostEstimate(flops=3200000000, bytes_accessed=15000000, transcendentals=0),
    )(infos[1], shifts, cot_pad, *parts_other, pre, mine)
    return k_mine, results


def weight_kernel(
    upper,
    info_ref,
    turned_ref,
    turned_pair_ref,
    x_ref,
    x_pair_ref,
    cot_ref,
    cot_pair_ref,
    hid_ref,
    hid_pair_ref,
    terms_ref,
    sent_ref,
):
    half = x_pair_ref.shape[-1]
    count = turned_ref.shape[1]
    block = count // 2
    own = terms_ref.shape[-2]
    outs = pl.ds(half * upper, half)

    def keep(total, group, b):
        for zh in range(2):
            for y in range(4):
                row = (4 * zh + y) * own
                slots = info_ref[1 + group], info_ref[5 + y]
                slots = slots[::-1] if upper else slots
                terms_ref[slots[0], slots[1], b, zh] = total[row : row + own]

    def spatial(a, _):
        for b in range(3):
            piece = x_ref[b, :, pl.ds(a, 2), :, lanes(info_ref[0], half)].reshape(count, half)
            total = jnp.dot(turned_ref[outs], piece, preferred_element_type=jnp.float32)
            piece = x_pair_ref[b, :, pl.ds(a, 2)].reshape(count, half)
            total += jnp.dot(turned_pair_ref[outs], piece, preferred_element_type=jnp.float32)
            keep(total, a, b)
        return 0

    lax.fori_loop(0, 3, spatial, 0)
    for k in range(3):
        piece = cot_ref[outs, (2 - k) * block : (4 - k) * block]
        total = jnp.dot(piece, hid_ref[...], preferred_element_type=jnp.float32)
        piece = cot_pair_ref[outs, (2 - k) * block : (4 - k) * block]
        total += jnp.dot(piece, hid_pair_ref[...], preferred_element_type=jnp.float32)
        keep(total, 3, k)
    for slot in range(2):
        for i in range(4):
            sent_ref[slot, i] = terms_ref[2 + slot, i].astype(jnp.bfloat16)


def weight_terms(upper, own, info, *operands):
    half = operands[-1].shape[-1]
    shape = (4, 4, 3, 2, own, half)
    return pl.pallas_call(
        functools.partial(weight_kernel, upper),
        out_shape=(
            jax.ShapeDtypeStruct(shape, jnp.float32),
            jax.ShapeDtypeStruct((2,) + shape[1:], jnp.bfloat16),
        ),
        in_specs=[SMEM] + [VMEM] * 8,
        out_specs=(VMEM, VMEM),
        compiler_params=PARAMS,
        cost_estimate=pl.CostEstimate(flops=2400000000, bytes_accessed=16000000, transcendentals=0),
    )(info, *operands)


def grad_kernel(f, info_ref, x_ref, cot_ref, mine_ref, other_ref, *refs):
    out_ref = refs[-1]
    block, chans = out_ref.shape[1:]
    half = chans // 2
    for kernel_ref, index in ((mine_ref, info_ref[0]), (other_ref, 1 - info_ref[0])):

        def convolve(a, _, kernel_ref=kernel_ref, index=index):
            total = out_ref[0, :, lanes(index, half)]
            for b in range(3):
                piece = x_ref[2 - b, f, pl.ds(2 - a, 2)].reshape(block, chans)
                kernel = kernel_ref[a, :, b].reshape(chans, half)
                total += jnp.dot(piece, kernel, preferred_element_type=jnp.float32)
            out_ref[0, :, lanes(index, half)] = total
            return 0

        out_ref[0, :, lanes(index, half)] = cot_ref[f, :, lanes(index, half)].astype(jnp.float32)
        lax.fori_loop(0, 3, convolve, 0)


def input_gradient(f, info, shifts, cotangent, k_mine, k_other, earlier=()):
    frames, rows, width, chans = cotangent.shape
    block = pl.BlockSpec((1, rows * width, chans), lambda i: (f, 0, 0))
    whole = [pl.BlockSpec(memory_space=pltpu.VMEM)] * 4
    return pl.pallas_call(
        functools.partial(grad_kernel, f),
        grid=(1,),
        out_shape=jax.ShapeDtypeStruct((frames, rows * width, chans), jnp.float32),
        in_specs=[SMEM] + whole + [ANY] * len(earlier),
        out_specs=block,
        input_output_aliases={5: 0} if earlier else {},
        compiler_params=PARAMS,
        cost_estimate=pl.CostEstimate(flops=1800000000, bytes_accessed=8000000, transcendentals=0),
    )(info, shifts, cotangent.reshape(frames, rows * width, chans), k_mine, k_other, *earlier)


def kernel_unit(spatial_kernel, temporal_kernel, half):
    both = jnp.concatenate(
        [spatial_kernel.transpose(1, 0, 2), temporal_kernel.transpose(1, 0, 2)], axis=0
    )
    start = (3 * lax.axis_index("x"), 0, lax.axis_index("core") * half)
    unit = lax.dynamic_slice(both, start, (3, both.shape[1], half))
    p = lax.axis_index("zh")
    slots = [unit]
    for k in range(1, 4):
        slots.append(lax.ppermute(unit, "zh", [(i, i ^ k) for i in range(4)]))
    slots = [jnp.where(p & 1, slots[k ^ 1], slots[k]) for k in range(4)]
    slots = [jnp.where(p & 2, slots[k ^ 2], slots[k]) for k in range(4)]
    return jnp.stack(slots[:2]), jnp.stack(slots[2:])


def kernel_parts(unit, waited):
    lower = jnp.concatenate(ring_gather(unit[0], "y"))
    upper = jnp.concatenate(ring_gather(unit[1], "x"))
    lower, lower_rest = ring_gather(lower, "x")
    upper, upper_rest = ring_gather(upper, "y")
    rest, waited = lax.optimization_barrier(((lower_rest, upper_rest), waited))
    mine = (lower, rest[0], upper, rest[1])
    return mine, tuple(swap(part) for part in mine), waited


def per_device(activations, cotangent, spatial_kernel, temporal_kernel):
    frames, rows, width, chans = activations.shape
    count = frames * rows * width
    half = chans // 2
    core = lax.axis_index("core").astype(jnp.int32).reshape(1)
    own = spatial_kernel.shape[0]
    infos = [
        jnp.concatenate([core ^ turn, slots_in("x", turn), slots_in("y", turn)])
        for turn in range(2)
    ]

    unit = kernel_unit(spatial_kernel, temporal_kernel, half)
    x_wide = widened(activations, edges_of(activations, SPACE, 1), SPACE, 1)
    cot_pad = widened(cotangent, edges_of(cotangent, TM, 0), TM, 0)
    x_pair = swap(lax.dynamic_slice_in_dim(x_wide, (1 - core[0]) * half, half, axis=3))
    shifts = column_shifts(x_wide)
    cot_turned = cot_pad.reshape((frames + 2) * rows * width, chans).T
    waited = (shifts, cot_pad, cot_turned, x_pair)
    parts, parts_other, waited = kernel_parts(unit, waited)
    shifts, cot_pad, cot_turned, x_pair = waited
    cot_turned_pair = swap(cot_turned)
    cot_turned_pair, parts_other = lax.optimization_barrier((cot_turned_pair, parts_other))

    k_mine, results = forward(infos, shifts, cot_pad, parts, parts_other)
    hid_mine, hid_other, slope_pre, turned, k_other = results
    turned_pair, hid_pair = swap(turned), swap(hid_other)
    x_pair, _ = lax.optimization_barrier((x_pair, turned))
    shifts_pair = column_shifts(x_pair)
    slope_maps = slope_pre.reshape(frames, rows, width, chans)
    slope_edges = edges_of(slope_maps, SPACE, 1)
    operands = (
        turned,
        turned_pair,
        shifts,
        shifts_pair,
        cot_turned,
        cot_turned_pair,
        hid_mine.reshape(count, half),
        hid_pair.reshape(count, half),
    )
    info = jnp.concatenate([core, slots_of("x"), slots_of("y")])
    lower, sent_lower = weight_terms(0, own, info, *operands)
    upper, sent_upper = weight_terms(1, own, info, *operands)
    came_lower = exchange(sent_lower, "x", 0)
    came_upper = exchange(sent_upper, "y", 0)
    passed_lower = (lower[1] + widen(came_lower[1])).astype(jnp.bfloat16)
    passed_upper = (upper[1] + widen(came_upper[1])).astype(jnp.bfloat16)
    last_lower, last_upper = exchange(passed_lower, "x", 1), exchange(passed_upper, "y", 1)

    def total(terms, came, last, slots):
        return terms[0, slots] + widen(came[0, slots]) + widen(last[slots])

    keep, send = slice(0, 2), slice(2, 4)
    sent_lower = total(lower, came_lower, last_lower, send)
    sent_upper = total(upper, came_upper, last_upper, send)
    lower = ring_scatter(total(lower, came_lower, last_lower, keep), sent_lower, "y")
    upper = ring_scatter(total(upper, came_upper, last_upper, keep), sent_upper, "x")
    terms = jnp.concatenate([lower, upper], axis=1)
    terms = terms.reshape(3, 4, 2, own // 2, half).transpose(1, 2, 0, 3, 4)
    terms = terms.reshape(8, 3, own // 2, half).astype(jnp.bfloat16)

    slope_edges, _ = lax.optimization_barrier((slope_edges, terms))
    slope_wide = widened(slope_maps, slope_edges, SPACE, 1)
    shifts_slope = column_shifts(slope_wide)
    grad = input_gradient(0, core, shifts_slope, cotangent, k_mine, k_other)
    terms = lax.all_to_all(terms, ("zh", "zl"), 0, 0, tiled=True)
    terms, grad = lax.optimization_barrier((terms, grad))
    pixels = count * lax.axis_size(TM) * lax.axis_size(SPACE)
    terms = jnp.sum(widen(terms), axis=0) * (1.0 / math.sqrt(pixels))
    info, _ = lax.optimization_barrier((core, terms))
    grad = input_gradient(1, info, shifts_slope, cotangent, k_mine, k_other, (grad,))
    terms = gathered(terms, ("x", "zl"))
    terms, grad = lax.optimization_barrier((terms, grad))
    came = swap(terms)
    terms = jnp.concatenate(
        [jnp.where(core[0] == 0, terms, came), jnp.where(core[0] == 0, came, terms)], axis=3
    )
    terms = terms.reshape(4, 2, 3, own // 2, chans).transpose(0, 2, 1, 3, 4)
    spatial = terms[:3].reshape(9, own, chans).transpose(1, 0, 2)
    temporal = terms[3].reshape(3, own, chans).transpose(1, 0, 2)
    return grad.reshape(frames, rows, width, chans), spatial, temporal


def solution(mesh):
    split = Mesh(mesh.devices.reshape(4, 2, 2, 4, 4), TM + SPACE)
    maps = P(TM, SPACE, None, None)
    kernels = P(SPACE, None, None)
    return jax.shard_map(
        per_device,
        mesh=split,
        in_specs=(maps, maps, kernels, kernels),
        out_specs=(maps, kernels, kernels),
        check_vma=False,
    )
```

```python
import functools
import math

import jax
import jax.numpy as jnp
from jax import lax
from jax.experimental import pallas as pl
from jax.experimental.pallas import tpu as pltpu
from jax.sharding import Mesh, PartitionSpec as P

TM = ("x", "zl", "core")
SPACE = ("zh", "y")
PAIR = [(0, 1), (1, 0)]
ORDER = ((1, 3), (3, 1))
VMEM = pl.BlockSpec(memory_space=pltpu.VMEM)
ANY = pl.BlockSpec(memory_space=pl.ANY)
SMEM = pl.BlockSpec(memory_space=pltpu.SMEM)
PARAMS = pltpu.CompilerParams(vmem_limit_bytes=24 * 1024 * 1024)


def swap(block):
    return lax.ppermute(block, "core", PAIR)


def exchange(block, axis, stage):
    if axis == "x":
        names, number = ("x", "core"), lambda core, p: 2 * p + core
    else:
        names, number = ("core", axis), lambda core, p: 4 * core + p
    pairs = [
        (number(core, p), number(core, p ^ ORDER[core][stage]))
        for core in range(2)
        for p in range(4)
    ]
    return lax.ppermute(block, names, pairs)


def positions(axis):
    p = lax.axis_index(axis)
    core = lax.axis_index("core")
    return p, p ^ (1 + 2 * core), p ^ (3 - 2 * core), p ^ 2


def slots_of(axis):
    own, first, second, far = positions(axis)
    q = jnp.arange(4, dtype=jnp.int32)
    return jnp.where(q == own, 0, jnp.where(q == second, 1, jnp.where(q == first, 2, 3)))


def slots_in(axis, turn):
    p = lax.axis_index(axis)
    core = lax.axis_index("core") ^ turn
    return jnp.stack([p, p ^ (1 + 2 * core), p ^ (3 - 2 * core), p ^ 2]).astype(jnp.int32)


def widen(block):
    return block.astype(jnp.float32)


def ring_scatter(terms, sent, axis):
    came = exchange(sent, axis, 0)
    passed = (terms[1] + widen(came[1])).astype(sent.dtype)
    return terms[0] + widen(came[0]) + widen(exchange(passed, axis, 1))


def ring_gather(block, axis):
    pair = jnp.stack([block, exchange(block, axis, 0)])
    return pair, exchange(pair, axis, 1)


def gathered(block, axis):
    spread = jnp.broadcast_to(block[None], (lax.axis_size(axis),) + block.shape)
    return lax.all_to_all(spread, axis, 0, 0, tiled=True)


def scattered(block, axis):
    return jnp.sum(lax.all_to_all(block, axis, 0, 0, tiled=True).astype(jnp.float32), axis=0)


def edges_of(block, axis, dim):
    count = lax.axis_size(axis)
    forward = [(i, (i + 1) % count) for i in range(count)]
    backward = [(target, source) for source, target in forward]
    size = block.shape[dim]
    low = lax.ppermute(lax.slice_in_dim(block, size - 1, size, axis=dim), axis, forward)
    high = lax.ppermute(lax.slice_in_dim(block, 0, 1, axis=dim), axis, backward)
    return low, high


def widened(block, edges, axis, dim):
    low, high = edges
    index = lax.axis_index(axis)
    low = jnp.where(index == 0, jnp.zeros_like(low), low)
    high = jnp.where(index == lax.axis_size(axis) - 1, jnp.zeros_like(high), high)
    return jnp.concatenate([low, block, high], axis=dim)


def column_shifts(maps):
    edge = jnp.zeros_like(maps[:, :, :1])
    return jnp.stack(
        [
            jnp.concatenate([edge, maps[:, :, :-1]], axis=2),
            maps,
            jnp.concatenate([maps[:, :, 1:], edge], axis=2),
        ]
    )


def lanes(index, half):
    return pl.ds(pl.multiple_of(index * half, half), half)


def assemble(info_ref, parts, kernel_ref, others, sems):
    copies = []
    for pair in range(2):
        for j in range(2):
            slot = 2 * pair + j
            for t in range(4):
                x, y = info_ref[1 + slot], info_ref[5 + t]
                target = kernel_ref.at[x, pl.ds(0, 2), :, y]
                copies.append((parts[pair].at[j, t], target))
                x, y = info_ref[1 + t], info_ref[5 + slot]
                target = kernel_ref.at[x, pl.ds(2, 2), :, y]
                copies.append((parts[2 + pair].at[j, t], target))
    copies = [
        pltpu.make_async_copy(source, target, sems.at[i])
        for i, (source, target) in enumerate(copies)
    ]
    copies += [
        pltpu.make_async_copy(source, target, sems.at[32 + i])
        for i, (source, target) in enumerate(others)
    ]
    for copy in copies:
        copy.start()
    for copy in copies:
        copy.wait()


def add_terms(index, x_ref, cot_ref, kernel_ref, pre_ref, slope_ref, start_ref):
    frames, block, chans = pre_ref.shape
    half = chans // 2

    def convolve(f, _, a):
        if a > 0:
            total = pre_ref[f]
        elif start_ref is not None:
            total = start_ref[f]
        else:
            total = jnp.zeros((block, chans), jnp.float32)
        for b in range(3):
            piece = x_ref[b, f, a : a + 2, :, lanes(index, half)].reshape(block, half)
            total += lax.dot_general(
                piece,
                kernel_ref[a, :, b].reshape(chans, half),
                (((1,), (1,)), ((), ())),
                preferred_element_type=jnp.float32,
            )
        pre_ref[f] = total
        return 0

    def blend(f, _):
        total = jnp.zeros((block, half), jnp.float32)
        for k in range(3):
            piece = cot_ref[2 - k + f].reshape(block, chans)
            kernel = kernel_ref[3, :, k].reshape(chans, half)
            total += jnp.dot(piece, kernel, preferred_element_type=jnp.float32)
        slope_ref[f] = total
        return 0

    for a in range(3):
        lax.fori_loop(0, frames, functools.partial(convolve, a=a), 0)
    lax.fori_loop(0, frames, blend, 0)


def first_kernel(info_ref, x_hbm, cot_hbm, *refs):
    parts, (pre_ref, slope_ref, kernel_ref, x_ref, cot_ref, sems) = refs[:4], refs[4:]
    assemble(info_ref, parts, kernel_ref, ((x_hbm, x_ref), (cot_hbm, cot_ref)), sems)
    add_terms(info_ref[0], x_ref, cot_ref, kernel_ref, pre_ref, slope_ref, None)


def second_kernel(info_ref, x_hbm, cot_hbm, *refs):
    parts, (start_ref, mine_ref), refs = refs[:4], refs[4:6], refs[6:]
    hid_mine_ref, hid_other_ref, slope_ref, turned_ref, kernel_ref = refs[:5]
    pre_ref, other_ref, work_ref, x_ref, cot_ref, sems = refs[5:]
    assemble(info_ref, parts, kernel_ref, ((x_hbm, x_ref), (cot_hbm, cot_ref)), sems)
    other = info_ref[0]
    add_terms(other, x_ref, cot_ref, kernel_ref, pre_ref, other_ref, start_ref)
    frames, block, chans = pre_ref.shape
    half = chans // 2
    part = 32
    for hid_ref, source_ref, index in (
        (hid_mine_ref, mine_ref, 1 - other),
        (hid_other_ref, other_ref, other),
    ):

        def finish(step, _, hid_ref=hid_ref, source_ref=source_ref, index=index):
            f, r = step // (block // part), step % (block // part)
            rows = pl.ds(pl.multiple_of(r * part, part), part)
            pre = pre_ref[f, rows, lanes(index, half)]
            sigma = 1.0 / (1.0 + jnp.exp(-pre))
            hid_ref[f, rows] = (pre * sigma).astype(jnp.bfloat16)
            slope = source_ref[f, rows] * sigma * (1.0 + pre * (1.0 - sigma))
            work_ref[f, rows, lanes(index, half)] = slope
            return 0

        lax.fori_loop(0, frames * (block // part), finish, 0)
    for f in range(frames):
        slope = work_ref[f].astype(jnp.bfloat16)
        slope_ref[f] = slope
        turned_ref[:, f * block : (f + 1) * block] = slope.T


def forward(infos, shifts, cot_pad, parts, parts_other):
    frames, _, width, chans = shifts.shape[1:]
    block = 2 * width
    half = chans // 2
    full = jax.ShapeDtypeStruct((frames, block, chans), jnp.float32)
    part = jax.ShapeDtypeStruct((frames, block, half), jnp.float32)
    hid = jax.ShapeDtypeStruct((frames, block, half), jnp.bfloat16)
    kernel = jax.ShapeDtypeStruct((4, 4, 3, 4) + parts[0].shape[-2:], parts[0].dtype)
    held = [
        pltpu.VMEM(shifts.shape, shifts.dtype),
        pltpu.VMEM(cot_pad.shape, cot_pad.dtype),
        pltpu.SemaphoreType.DMA((34,)),
    ]
    pre, mine, k_mine = pl.pallas_call(
        first_kernel,
        out_shape=(full, part, kernel),
        in_specs=[SMEM] + [ANY] * 6,
        out_specs=(VMEM,) * 3,
        scratch_shapes=held,
        compiler_params=PARAMS,
        cost_estimate=pl.CostEstimate(flops=3200000000, bytes_accessed=12000000, transcendentals=0),
    )(infos[0], shifts, cot_pad, *parts)
    results = pl.pallas_call(
        second_kernel,
        out_shape=(
            hid,
            hid,
            jax.ShapeDtypeStruct((frames, block, chans), jnp.bfloat16),
            jax.ShapeDtypeStruct((chans, frames * block), jnp.bfloat16),
            kernel,
        ),
        in_specs=[SMEM] + [ANY] * 6 + [VMEM] * 2,
        out_specs=(VMEM,) * 5,
        scratch_shapes=[
            pltpu.VMEM(full.shape, jnp.float32),
            pltpu.VMEM(part.shape, jnp.float32),
            pltpu.VMEM(full.shape, jnp.float32),
        ]
        + held,
        compiler_params=PARAMS,
        cost_estimate=pl.CostEstimate(flops=3200000000, bytes_accessed=15000000, transcendentals=0),
    )(infos[1], shifts, cot_pad, *parts_other, pre, mine)
    return k_mine, results


def weight_kernel(
    upper,
    info_ref,
    turned_ref,
    turned_pair_ref,
    x_ref,
    x_pair_ref,
    cot_ref,
    cot_pair_ref,
    hid_ref,
    hid_pair_ref,
    terms_ref,
    sent_ref,
):
    half = x_pair_ref.shape[-1]
    count = turned_ref.shape[1]
    block = count // 2
    own = terms_ref.shape[-2]
    outs = pl.ds(half * upper, half)

    def keep(total, group, b):
        for zh in range(2):
            for y in range(4):
                row = (4 * zh + y) * own
                slots = info_ref[1 + group], info_ref[5 + y]
                slots = slots[::-1] if upper else slots
                terms_ref[slots[0], slots[1], b, zh] = total[row : row + own]

    def spatial(a, _):
        for b in range(3):
            piece = x_ref[b, :, pl.ds(a, 2), :, lanes(info_ref[0], half)].reshape(count, half)
            total = jnp.dot(turned_ref[outs], piece, preferred_element_type=jnp.float32)
            piece = x_pair_ref[b, :, pl.ds(a, 2)].reshape(count, half)
            total += jnp.dot(turned_pair_ref[outs], piece, preferred_element_type=jnp.float32)
            keep(total, a, b)
        return 0

    lax.fori_loop(0, 3, spatial, 0)
    for k in range(3):
        piece = cot_ref[outs, (2 - k) * block : (4 - k) * block]
        total = jnp.dot(piece, hid_ref[...], preferred_element_type=jnp.float32)
        piece = cot_pair_ref[outs, (2 - k) * block : (4 - k) * block]
        total += jnp.dot(piece, hid_pair_ref[...], preferred_element_type=jnp.float32)
        keep(total, 3, k)
    for slot in range(2):
        for i in range(4):
            sent_ref[slot, i] = terms_ref[2 + slot, i].astype(jnp.bfloat16)


def weight_terms(upper, own, info, *operands):
    half = operands[-1].shape[-1]
    shape = (4, 4, 3, 2, own, half)
    return pl.pallas_call(
        functools.partial(weight_kernel, upper),
        out_shape=(
            jax.ShapeDtypeStruct(shape, jnp.float32),
            jax.ShapeDtypeStruct((2,) + shape[1:], jnp.bfloat16),
        ),
        in_specs=[SMEM] + [VMEM] * 8,
        out_specs=(VMEM, VMEM),
        compiler_params=PARAMS,
        cost_estimate=pl.CostEstimate(flops=2400000000, bytes_accessed=16000000, transcendentals=0),
    )(info, *operands)


def grad_kernel(f, info_ref, x_ref, cot_ref, mine_ref, other_ref, *refs):
    out_ref = refs[-1]
    block, chans = out_ref.shape[1:]
    half = chans // 2
    for kernel_ref, index in ((mine_ref, info_ref[0]), (other_ref, 1 - info_ref[0])):

        def convolve(a, _, kernel_ref=kernel_ref, index=index):
            total = out_ref[0, :, lanes(index, half)]
            for b in range(3):
                piece = x_ref[2 - b, f, pl.ds(2 - a, 2)].reshape(block, chans)
                kernel = kernel_ref[a, :, b].reshape(chans, half)
                total += jnp.dot(piece, kernel, preferred_element_type=jnp.float32)
            out_ref[0, :, lanes(index, half)] = total
            return 0

        out_ref[0, :, lanes(index, half)] = cot_ref[f, :, lanes(index, half)].astype(jnp.float32)
        lax.fori_loop(0, 3, convolve, 0)


def input_gradient(f, info, shifts, cotangent, k_mine, k_other, earlier=()):
    frames, rows, width, chans = cotangent.shape
    block = pl.BlockSpec((1, rows * width, chans), lambda i: (f, 0, 0))
    whole = [pl.BlockSpec(memory_space=pltpu.VMEM)] * 4
    return pl.pallas_call(
        functools.partial(grad_kernel, f),
        grid=(1,),
        out_shape=jax.ShapeDtypeStruct((frames, rows * width, chans), jnp.float32),
        in_specs=[SMEM] + whole + [ANY] * len(earlier),
        out_specs=block,
        input_output_aliases={5: 0} if earlier else {},
        compiler_params=PARAMS,
        cost_estimate=pl.CostEstimate(flops=1800000000, bytes_accessed=8000000, transcendentals=0),
    )(info, shifts, cotangent.reshape(frames, rows * width, chans), k_mine, k_other, *earlier)


def kernel_unit(spatial_kernel, temporal_kernel, half):
    both = jnp.concatenate(
        [spatial_kernel.transpose(1, 0, 2), temporal_kernel.transpose(1, 0, 2)], axis=0
    )
    start = (3 * lax.axis_index("x"), 0, lax.axis_index("core") * half)
    unit = lax.dynamic_slice(both, start, (3, both.shape[1], half))
    p = lax.axis_index("zh")
    slots = [unit]
    for k in range(1, 4):
        slots.append(lax.ppermute(unit, "zh", [(i, i ^ k) for i in range(4)]))
    slots = [jnp.where(p & 1, slots[k ^ 1], slots[k]) for k in range(4)]
    slots = [jnp.where(p & 2, slots[k ^ 2], slots[k]) for k in range(4)]
    return jnp.stack(slots[:2]), jnp.stack(slots[2:])


def kernel_parts(unit, waited):
    lower = jnp.concatenate(ring_gather(unit[0], "y"))
    upper = jnp.concatenate(ring_gather(unit[1], "x"))
    lower, lower_rest = ring_gather(lower, "x")
    upper, upper_rest = ring_gather(upper, "y")
    rest, waited = lax.optimization_barrier(((lower_rest, upper_rest), waited))
    mine = (lower, rest[0], upper, rest[1])
    return mine, tuple(swap(part) for part in mine), waited


def per_device(activations, cotangent, spatial_kernel, temporal_kernel):
    frames, rows, width, chans = activations.shape
    count = frames * rows * width
    half = chans // 2
    core = lax.axis_index("core").astype(jnp.int32).reshape(1)
    own = spatial_kernel.shape[0]
    infos = [
        jnp.concatenate([core ^ turn, slots_in("x", turn), slots_in("y", turn)])
        for turn in range(2)
    ]

    unit = kernel_unit(spatial_kernel, temporal_kernel, half)
    x_wide = widened(activations, edges_of(activations, SPACE, 1), SPACE, 1)
    cot_pad = widened(cotangent, edges_of(cotangent, TM, 0), TM, 0)
    x_pair = swap(lax.dynamic_slice_in_dim(x_wide, (1 - core[0]) * half, half, axis=3))
    shifts = column_shifts(x_wide)
    cot_turned = cot_pad.reshape((frames + 2) * rows * width, chans).T
    waited = (shifts, cot_pad, cot_turned, x_pair)
    parts, parts_other, waited = kernel_parts(unit, waited)
    shifts, cot_pad, cot_turned, x_pair = waited
    cot_turned_pair = swap(cot_turned)
    cot_turned_pair, parts_other = lax.optimization_barrier((cot_turned_pair, parts_other))

    k_mine, results = forward(infos, shifts, cot_pad, parts, parts_other)
    hid_mine, hid_other, slope_pre, turned, k_other = results
    turned_pair, hid_pair = swap(turned), swap(hid_other)
    x_pair, _ = lax.optimization_barrier((x_pair, turned))
    shifts_pair = column_shifts(x_pair)
    slope_maps = slope_pre.reshape(frames, rows, width, chans)
    slope_edges = edges_of(slope_maps, SPACE, 1)
    operands = (
        turned,
        turned_pair,
        shifts,
        shifts_pair,
        cot_turned,
        cot_turned_pair,
        hid_mine.reshape(count, half),
        hid_pair.reshape(count, half),
    )
    info = jnp.concatenate([core, slots_of("x"), slots_of("y")])
    lower, sent_lower = weight_terms(0, own, info, *operands)
    upper, sent_upper = weight_terms(1, own, info, *operands)
    slope_edges, _ = lax.optimization_barrier((slope_edges, (sent_lower, sent_upper)))
    slope_wide = widened(slope_maps, slope_edges, SPACE, 1)
    shifts_slope = column_shifts(slope_wide)

    came_lower = exchange(sent_lower, "x", 0)
    came_upper = exchange(sent_upper, "y", 0)
    passed = (lower[1] + widen(came_lower[1])).astype(jnp.bfloat16)
    last_lower = exchange(passed, "x", 1)
    info, _ = lax.optimization_barrier((core, passed))
    grad = input_gradient(0, info, shifts_slope, cotangent, k_mine, k_other)
    came_upper, grad = lax.optimization_barrier((came_upper, grad))
    passed = (upper[1] + widen(came_upper[1])).astype(jnp.bfloat16)
    last_upper = exchange(passed, "y", 1)
    info, _ = lax.optimization_barrier((core, passed))
    grad = input_gradient(1, info, shifts_slope, cotangent, k_mine, k_other, (grad,))
    last_lower, grad = lax.optimization_barrier((last_lower, grad))

    def total(terms, came, last, slots):
        return terms[0, slots] + widen(came[0, slots]) + widen(last[slots])

    keep, send = slice(0, 2), slice(2, 4)
    sent_lower = total(lower, came_lower, last_lower, send)
    sent_upper = total(upper, came_upper, last_upper, send)
    lower = ring_scatter(total(lower, came_lower, last_lower, keep), sent_lower, "y")
    upper = ring_scatter(total(upper, came_upper, last_upper, keep), sent_upper, "x")
    terms = jnp.concatenate([lower, upper], axis=1)
    terms = terms.reshape(3, 4, 2, own // 2, half).transpose(1, 2, 0, 3, 4)
    terms = terms.reshape(8, 3, own // 2, half).astype(jnp.bfloat16)

    terms = lax.all_to_all(terms, ("zh", "zl"), 0, 0, tiled=True)
    pixels = count * lax.axis_size(TM) * lax.axis_size(SPACE)
    terms = jnp.sum(widen(terms), axis=0) * (1.0 / math.sqrt(pixels))
    terms = gathered(terms, ("x", "zl"))
    came = swap(terms)
    terms = jnp.concatenate(
        [jnp.where(core[0] == 0, terms, came), jnp.where(core[0] == 0, came, terms)], axis=3
    )
    terms = terms.reshape(4, 2, 3, own // 2, chans).transpose(0, 2, 1, 3, 4)
    spatial = terms[:3].reshape(9, own, chans).transpose(1, 0, 2)
    temporal = terms[3].reshape(3, own, chans).transpose(1, 0, 2)
    return grad.reshape(frames, rows, width, chans), spatial, temporal


def solution(mesh):
    split = Mesh(mesh.devices.reshape(4, 2, 2, 4, 4), TM + SPACE)
    maps = P(TM, SPACE, None, None)
    kernels = P(SPACE, None, None)
    return jax.shard_map(
        per_device,
        mesh=split,
        in_specs=(maps, maps, kernels, kernels),
        out_specs=(maps, kernels, kernels),
        check_vma=False,
    )
```

```python
import functools
import math

import jax
import jax.numpy as jnp
from jax import lax
from jax.experimental import pallas as pl
from jax.experimental.pallas import tpu as pltpu
from jax.sharding import Mesh, PartitionSpec as P

TM = ("x", "zl", "core")
SPACE = ("zh", "y")
PAIR = [(0, 1), (1, 0)]
ORDER = ((1, 3), (3, 1))
VMEM = pl.BlockSpec(memory_space=pltpu.VMEM)
ANY = pl.BlockSpec(memory_space=pl.ANY)
SMEM = pl.BlockSpec(memory_space=pltpu.SMEM)
PARAMS = pltpu.CompilerParams(vmem_limit_bytes=24 * 1024 * 1024)


def swap(block):
    return lax.ppermute(block, "core", PAIR)


def exchange(block, axis, stage):
    if axis == "x":
        names, number = ("x", "core"), lambda core, p: 2 * p + core
    else:
        names, number = ("core", axis), lambda core, p: 4 * core + p
    pairs = [
        (number(core, p), number(core, p ^ ORDER[core][stage]))
        for core in range(2)
        for p in range(4)
    ]
    return lax.ppermute(block, names, pairs)


def positions(axis):
    p = lax.axis_index(axis)
    core = lax.axis_index("core")
    return p, p ^ (1 + 2 * core), p ^ (3 - 2 * core), p ^ 2


def slots_of(axis):
    own, first, second, far = positions(axis)
    q = jnp.arange(4, dtype=jnp.int32)
    return jnp.where(q == own, 0, jnp.where(q == second, 1, jnp.where(q == first, 2, 3)))


def slots_in(axis, turn):
    p = lax.axis_index(axis)
    core = lax.axis_index("core") ^ turn
    return jnp.stack([p, p ^ (1 + 2 * core), p ^ (3 - 2 * core), p ^ 2]).astype(jnp.int32)


def widen(block):
    return block.astype(jnp.float32)


def ring_scatter(terms, sent, axis):
    came = exchange(sent, axis, 0)
    passed = (terms[1] + widen(came[1])).astype(sent.dtype)
    return terms[0] + widen(came[0]) + widen(exchange(passed, axis, 1))


def ring_gather(block, axis):
    pair = jnp.stack(lax.optimization_barrier((block, exchange(block, axis, 0))))
    return pair, exchange(pair, axis, 1)


def gathered(block, axis):
    spread = jnp.broadcast_to(block[None], (lax.axis_size(axis),) + block.shape)
    return lax.all_to_all(spread, axis, 0, 0, tiled=True)


def scattered(block, axis):
    return jnp.sum(lax.all_to_all(block, axis, 0, 0, tiled=True).astype(jnp.float32), axis=0)


def edges_of(block, axis, dim):
    count = lax.axis_size(axis)
    forward = [(i, (i + 1) % count) for i in range(count)]
    backward = [(target, source) for source, target in forward]
    size = block.shape[dim]
    low = lax.ppermute(lax.slice_in_dim(block, size - 1, size, axis=dim), axis, forward)
    high = lax.ppermute(lax.slice_in_dim(block, 0, 1, axis=dim), axis, backward)
    return low, high


def widened(block, edges, axis, dim):
    low, high = edges
    index = lax.axis_index(axis)
    low = jnp.where(index == 0, jnp.zeros_like(low), low)
    high = jnp.where(index == lax.axis_size(axis) - 1, jnp.zeros_like(high), high)
    return jnp.concatenate([low, block, high], axis=dim)


def column_shifts(maps):
    edge = jnp.zeros_like(maps[:, :, :1])
    return jnp.stack(
        [
            jnp.concatenate([edge, maps[:, :, :-1]], axis=2),
            maps,
            jnp.concatenate([maps[:, :, 1:], edge], axis=2),
        ]
    )


def lanes(index, half):
    return pl.ds(pl.multiple_of(index * half, half), half)


def assemble(info_ref, parts, kernel_ref, others, sems):
    copies = []
    for pair in range(2):
        for j in range(2):
            slot = 2 * pair + j
            for t in range(4):
                x, y = info_ref[1 + slot], info_ref[5 + t]
                target = kernel_ref.at[x, pl.ds(0, 2), :, y]
                copies.append((parts[pair].at[j, t], target))
                x, y = info_ref[1 + t], info_ref[5 + slot]
                target = kernel_ref.at[x, pl.ds(2, 2), :, y]
                copies.append((parts[2 + pair].at[j, t], target))
    copies = [
        pltpu.make_async_copy(source, target, sems.at[i])
        for i, (source, target) in enumerate(copies)
    ]
    copies += [
        pltpu.make_async_copy(source, target, sems.at[32 + i])
        for i, (source, target) in enumerate(others)
    ]
    for copy in copies:
        copy.start()
    for copy in copies:
        copy.wait()


def add_terms(index, x_ref, cot_ref, kernel_ref, pre_ref, slope_ref, start_ref):
    frames, block, chans = pre_ref.shape
    half = chans // 2

    def convolve(f, _, a):
        if a > 0:
            total = pre_ref[f]
        elif start_ref is not None:
            total = start_ref[f]
        else:
            total = jnp.zeros((block, chans), jnp.float32)
        for b in range(3):
            piece = x_ref[b, f, a : a + 2, :, lanes(index, half)].reshape(block, half)
            total += lax.dot_general(
                piece,
                kernel_ref[a, :, b].reshape(chans, half),
                (((1,), (1,)), ((), ())),
                preferred_element_type=jnp.float32,
            )
        pre_ref[f] = total
        return 0

    def blend(f, _):
        total = jnp.zeros((block, half), jnp.float32)
        for k in range(3):
            piece = cot_ref[2 - k + f].reshape(block, chans)
            kernel = kernel_ref[3, :, k].reshape(chans, half)
            total += jnp.dot(piece, kernel, preferred_element_type=jnp.float32)
        slope_ref[f] = total
        return 0

    for a in range(3):
        lax.fori_loop(0, frames, functools.partial(convolve, a=a), 0)
    lax.fori_loop(0, frames, blend, 0)


def first_kernel(info_ref, x_hbm, cot_hbm, *refs):
    parts, (pre_ref, slope_ref, kernel_ref, x_ref, cot_ref, sems) = refs[:4], refs[4:]
    assemble(info_ref, parts, kernel_ref, ((x_hbm, x_ref), (cot_hbm, cot_ref)), sems)
    add_terms(info_ref[0], x_ref, cot_ref, kernel_ref, pre_ref, slope_ref, None)


def second_kernel(info_ref, x_hbm, cot_hbm, *refs):
    parts, (start_ref, mine_ref), refs = refs[:4], refs[4:6], refs[6:]
    hid_mine_ref, hid_other_ref, slope_ref, turned_ref, kernel_ref = refs[:5]
    pre_ref, other_ref, work_ref, x_ref, cot_ref, sems = refs[5:]
    assemble(info_ref, parts, kernel_ref, ((x_hbm, x_ref), (cot_hbm, cot_ref)), sems)
    other = info_ref[0]
    add_terms(other, x_ref, cot_ref, kernel_ref, pre_ref, other_ref, start_ref)
    frames, block, chans = pre_ref.shape
    half = chans // 2
    part = 96
    for hid_ref, source_ref, index in (
        (hid_mine_ref, mine_ref, 1 - other),
        (hid_other_ref, other_ref, other),
    ):

        def finish(step, _, hid_ref=hid_ref, source_ref=source_ref, index=index):
            f, r = step // (block // part), step % (block // part)
            rows = pl.ds(pl.multiple_of(r * part, part), part)
            pre = pre_ref[f, rows, lanes(index, half)]
            sigma = 1.0 / (1.0 + jnp.exp(-pre))
            hid_ref[f, rows] = (pre * sigma).astype(jnp.bfloat16)
            slope = source_ref[f, rows] * sigma * (1.0 + pre * (1.0 - sigma))
            work_ref[f, rows, lanes(index, half)] = slope
            return 0

        lax.fori_loop(0, frames * (block // part), finish, 0)
    for f in range(frames):
        slope = work_ref[f].astype(jnp.bfloat16)
        slope_ref[f] = slope
        turned_ref[:, f * block : (f + 1) * block] = slope.T


def forward(infos, shifts, cot_pad, parts, parts_other):
    frames, _, width, chans = shifts.shape[1:]
    block = 2 * width
    half = chans // 2
    full = jax.ShapeDtypeStruct((frames, block, chans), jnp.float32)
    part = jax.ShapeDtypeStruct((frames, block, half), jnp.float32)
    hid = jax.ShapeDtypeStruct((frames, block, half), jnp.bfloat16)
    kernel = jax.ShapeDtypeStruct((4, 4, 3, 4) + parts[0].shape[-2:], parts[0].dtype)
    held = [
        pltpu.VMEM(shifts.shape, shifts.dtype),
        pltpu.VMEM(cot_pad.shape, cot_pad.dtype),
        pltpu.SemaphoreType.DMA((34,)),
    ]
    pre, mine, k_mine = pl.pallas_call(
        first_kernel,
        out_shape=(full, part, kernel),
        in_specs=[SMEM] + [ANY] * 6,
        out_specs=(VMEM,) * 3,
        scratch_shapes=held,
        compiler_params=PARAMS,
        cost_estimate=pl.CostEstimate(flops=3200000000, bytes_accessed=12000000, transcendentals=0),
    )(infos[0], shifts, cot_pad, *parts)
    results = pl.pallas_call(
        second_kernel,
        out_shape=(
            hid,
            hid,
            jax.ShapeDtypeStruct((frames, block, chans), jnp.bfloat16),
            jax.ShapeDtypeStruct((chans, frames * block), jnp.bfloat16),
            kernel,
        ),
        in_specs=[SMEM] + [ANY] * 6 + [VMEM] * 2,
        out_specs=(VMEM,) * 5,
        scratch_shapes=[
            pltpu.VMEM(full.shape, jnp.float32),
            pltpu.VMEM(part.shape, jnp.float32),
            pltpu.VMEM(full.shape, jnp.float32),
        ]
        + held,
        compiler_params=PARAMS,
        cost_estimate=pl.CostEstimate(flops=3200000000, bytes_accessed=15000000, transcendentals=0),
    )(infos[1], shifts, cot_pad, *parts_other, pre, mine)
    return k_mine, results


def weight_kernel(
    upper,
    info_ref,
    turned_ref,
    turned_pair_ref,
    x_ref,
    x_pair_ref,
    cot_ref,
    cot_pair_ref,
    hid_ref,
    hid_pair_ref,
    terms_ref,
    sent_ref,
):
    half = x_pair_ref.shape[-1]
    count = turned_ref.shape[1]
    block = count // 2
    own = terms_ref.shape[-2]
    outs = pl.ds(half * upper, half)

    def keep(total, group, b):
        for zh in range(2):
            for y in range(4):
                row = (4 * zh + y) * own
                slots = info_ref[1 + group], info_ref[5 + y]
                slots = slots[::-1] if upper else slots
                terms_ref[slots[0], slots[1], b, zh] = total[row : row + own]

    def spatial(a, _):
        for b in range(3):
            piece = x_ref[b, :, pl.ds(a, 2), :, lanes(info_ref[0], half)].reshape(count, half)
            total = jnp.dot(turned_ref[outs], piece, preferred_element_type=jnp.float32)
            piece = x_pair_ref[b, :, pl.ds(a, 2)].reshape(count, half)
            total += jnp.dot(turned_pair_ref[outs], piece, preferred_element_type=jnp.float32)
            keep(total, a, b)
        return 0

    lax.fori_loop(0, 3, spatial, 0)
    for k in range(3):
        piece = cot_ref[outs, (2 - k) * block : (4 - k) * block]
        total = jnp.dot(piece, hid_ref[...], preferred_element_type=jnp.float32)
        piece = cot_pair_ref[outs, (2 - k) * block : (4 - k) * block]
        total += jnp.dot(piece, hid_pair_ref[...], preferred_element_type=jnp.float32)
        keep(total, 3, k)
    for slot in range(2):
        for i in range(4):
            sent_ref[slot, i] = terms_ref[2 + slot, i].astype(jnp.bfloat16)


def weight_terms(upper, own, info, *operands):
    half = operands[-1].shape[-1]
    shape = (4, 4, 3, 2, own, half)
    return pl.pallas_call(
        functools.partial(weight_kernel, upper),
        out_shape=(
            jax.ShapeDtypeStruct(shape, jnp.float32),
            jax.ShapeDtypeStruct((2,) + shape[1:], jnp.bfloat16),
        ),
        in_specs=[SMEM] + [VMEM] * 8,
        out_specs=(VMEM, VMEM),
        compiler_params=PARAMS,
        cost_estimate=pl.CostEstimate(flops=2400000000, bytes_accessed=16000000, transcendentals=0),
    )(info, *operands)


def grad_kernel(f, info_ref, x_ref, cot_ref, mine_ref, other_ref, *refs):
    out_ref = refs[-1]
    block, chans = out_ref.shape[1:]
    half = chans // 2
    for kernel_ref, index in ((mine_ref, info_ref[0]), (other_ref, 1 - info_ref[0])):

        def convolve(a, _, kernel_ref=kernel_ref, index=index):
            total = out_ref[0, :, lanes(index, half)]
            for b in range(3):
                piece = x_ref[2 - b, f, pl.ds(2 - a, 2)].reshape(block, chans)
                kernel = kernel_ref[a, :, b].reshape(chans, half)
                total += jnp.dot(piece, kernel, preferred_element_type=jnp.float32)
            out_ref[0, :, lanes(index, half)] = total
            return 0

        out_ref[0, :, lanes(index, half)] = cot_ref[f, :, lanes(index, half)].astype(jnp.float32)
        lax.fori_loop(0, 3, convolve, 0)


def input_gradient(f, info, shifts, cotangent, k_mine, k_other, earlier=()):
    frames, rows, width, chans = cotangent.shape
    block = pl.BlockSpec((1, rows * width, chans), lambda i: (f, 0, 0))
    whole = [pl.BlockSpec(memory_space=pltpu.VMEM)] * 4
    return pl.pallas_call(
        functools.partial(grad_kernel, f),
        grid=(1,),
        out_shape=jax.ShapeDtypeStruct((frames, rows * width, chans), jnp.float32),
        in_specs=[SMEM] + whole + [ANY] * len(earlier),
        out_specs=block,
        input_output_aliases={5: 0} if earlier else {},
        compiler_params=PARAMS,
        cost_estimate=pl.CostEstimate(flops=1800000000, bytes_accessed=8000000, transcendentals=0),
    )(info, shifts, cotangent.reshape(frames, rows * width, chans), k_mine, k_other, *earlier)


def kernel_unit(spatial_kernel, temporal_kernel, half):
    both = jnp.concatenate(
        [spatial_kernel.transpose(1, 0, 2), temporal_kernel.transpose(1, 0, 2)], axis=0
    )
    start = (3 * lax.axis_index("x"), 0, lax.axis_index("core") * half)
    unit = lax.dynamic_slice(both, start, (3, both.shape[1], half))
    p = lax.axis_index("zh")
    slots = [unit]
    for k in range(1, 4):
        slots.append(lax.ppermute(unit, "zh", [(i, i ^ k) for i in range(4)]))
    slots = [jnp.where(p & 1, slots[k ^ 1], slots[k]) for k in range(4)]
    slots = [jnp.where(p & 2, slots[k ^ 2], slots[k]) for k in range(4)]
    return jnp.stack(slots[:2]), jnp.stack(slots[2:])


def kernel_parts(unit, waited):
    lower = jnp.concatenate(ring_gather(unit[0], "y"))
    upper = jnp.concatenate(ring_gather(unit[1], "x"))
    lower, lower_rest = ring_gather(lower, "x")
    upper, upper_rest = ring_gather(upper, "y")
    rest, waited = lax.optimization_barrier(((lower_rest, upper_rest), waited))
    mine = (lower, rest[0], upper, rest[1])
    return mine, tuple(swap(part) for part in mine), waited


def per_device(activations, cotangent, spatial_kernel, temporal_kernel):
    frames, rows, width, chans = activations.shape
    count = frames * rows * width
    half = chans // 2
    core = lax.axis_index("core").astype(jnp.int32).reshape(1)
    own = spatial_kernel.shape[0]
    infos = [
        jnp.concatenate([core ^ turn, slots_in("x", turn), slots_in("y", turn)])
        for turn in range(2)
    ]

    unit = kernel_unit(spatial_kernel, temporal_kernel, half)
    x_wide = widened(activations, edges_of(activations, SPACE, 1), SPACE, 1)
    cot_pad = widened(cotangent, edges_of(cotangent, TM, 0), TM, 0)
    x_pair = swap(lax.dynamic_slice_in_dim(x_wide, (1 - core[0]) * half, half, axis=3))
    shifts = column_shifts(x_wide)
    cot_turned = cot_pad.reshape((frames + 2) * rows * width, chans).T
    waited = (shifts, cot_pad, cot_turned, x_pair)
    parts, parts_other, waited = kernel_parts(unit, waited)
    shifts, cot_pad, cot_turned, x_pair = waited
    cot_turned_pair = swap(cot_turned)
    cot_turned_pair, parts_other = lax.optimization_barrier((cot_turned_pair, parts_other))

    k_mine, results = forward(infos, shifts, cot_pad, parts, parts_other)
    hid_mine, hid_other, slope_pre, turned, k_other = results
    turned_pair, hid_pair = swap(turned), swap(hid_other)
    x_pair, _ = lax.optimization_barrier((x_pair, turned))
    shifts_pair = column_shifts(x_pair)
    slope_maps = slope_pre.reshape(frames, rows, width, chans)
    slope_edges = edges_of(slope_maps, SPACE, 1)
    operands = (
        turned,
        turned_pair,
        shifts,
        shifts_pair,
        cot_turned,
        cot_turned_pair,
        hid_mine.reshape(count, half),
        hid_pair.reshape(count, half),
    )
    info = jnp.concatenate([core, slots_of("x"), slots_of("y")])
    lower, sent_lower = weight_terms(0, own, info, *operands)
    upper, sent_upper = weight_terms(1, own, info, *operands)
    slope_edges, _ = lax.optimization_barrier((slope_edges, (sent_lower, sent_upper)))
    slope_wide = widened(slope_maps, slope_edges, SPACE, 1)
    shifts_slope = column_shifts(slope_wide)

    came_lower = exchange(sent_lower, "x", 0)
    came_upper = exchange(sent_upper, "y", 0)
    passed = (lower[1] + widen(came_lower[1])).astype(jnp.bfloat16)
    last_lower = exchange(passed, "x", 1)
    info, _ = lax.optimization_barrier((core, passed))
    grad = input_gradient(0, info, shifts_slope, cotangent, k_mine, k_other)
    came_upper, grad = lax.optimization_barrier((came_upper, grad))
    passed = (upper[1] + widen(came_upper[1])).astype(jnp.bfloat16)
    last_upper = exchange(passed, "y", 1)
    info, _ = lax.optimization_barrier((core, passed))
    grad = input_gradient(1, info, shifts_slope, cotangent, k_mine, k_other, (grad,))
    last_lower, grad = lax.optimization_barrier((last_lower, grad))

    def total(terms, came, last, slots):
        return terms[0, slots] + widen(came[0, slots]) + widen(last[slots])

    keep, send = slice(0, 2), slice(2, 4)
    sent_lower = total(lower, came_lower, last_lower, send)
    sent_upper = total(upper, came_upper, last_upper, send)
    lower = ring_scatter(total(lower, came_lower, last_lower, keep), sent_lower, "y")
    upper = ring_scatter(total(upper, came_upper, last_upper, keep), sent_upper, "x")
    terms = jnp.concatenate([lower, upper], axis=1)
    terms = terms.reshape(3, 4, 2, own // 2, half).transpose(1, 2, 0, 3, 4)
    terms = terms.reshape(8, 3, own // 2, half).astype(jnp.bfloat16)

    terms = lax.all_to_all(terms, ("zh", "zl"), 0, 0, tiled=True)
    pixels = count * lax.axis_size(TM) * lax.axis_size(SPACE)
    terms = jnp.sum(widen(terms), axis=0) * (1.0 / math.sqrt(pixels))
    terms = gathered(terms, ("x", "zl"))
    came = swap(terms)
    terms = jnp.concatenate(
        [jnp.where(core[0] == 0, terms, came), jnp.where(core[0] == 0, came, terms)], axis=3
    )
    terms = terms.reshape(4, 2, 3, own // 2, chans).transpose(0, 2, 1, 3, 4)
    spatial = terms[:3].reshape(9, own, chans).transpose(1, 0, 2)
    temporal = terms[3].reshape(3, own, chans).transpose(1, 0, 2)
    return grad.reshape(frames, rows, width, chans), spatial, temporal


def solution(mesh):
    split = Mesh(mesh.devices.reshape(4, 2, 2, 4, 4), TM + SPACE)
    maps = P(TM, SPACE, None, None)
    kernels = P(SPACE, None, None)
    return jax.shard_map(
        per_device,
        mesh=split,
        in_specs=(maps, maps, kernels, kernels),
        out_specs=(maps, kernels, kernels),
        check_vma=False,
    )
```

```python
import functools
import math

import jax
import jax.numpy as jnp
from jax import lax
from jax.experimental import pallas as pl
from jax.experimental.pallas import tpu as pltpu
from jax.sharding import Mesh, PartitionSpec as P

TM = ("x", "zl", "core")
SPACE = ("zh", "y")
PAIR = [(0, 1), (1, 0)]
ORDER = ((1, 3), (3, 1))
VMEM = pl.BlockSpec(memory_space=pltpu.VMEM)
ANY = pl.BlockSpec(memory_space=pl.ANY)
SMEM = pl.BlockSpec(memory_space=pltpu.SMEM)
PARAMS = pltpu.CompilerParams(vmem_limit_bytes=24 * 1024 * 1024)


def swap(block):
    return lax.ppermute(block, "core", PAIR)


def exchange(block, axis, stage):
    if axis == "x":
        names, number = ("x", "core"), lambda core, p: 2 * p + core
    else:
        names, number = ("core", axis), lambda core, p: 4 * core + p
    pairs = [
        (number(core, p), number(core, p ^ ORDER[core][stage]))
        for core in range(2)
        for p in range(4)
    ]
    return lax.ppermute(block, names, pairs)


def positions(axis):
    p = lax.axis_index(axis)
    core = lax.axis_index("core")
    return p, p ^ (1 + 2 * core), p ^ (3 - 2 * core), p ^ 2


def slots_of(axis):
    own, first, second, far = positions(axis)
    q = jnp.arange(4, dtype=jnp.int32)
    return jnp.where(q == own, 0, jnp.where(q == second, 1, jnp.where(q == first, 2, 3)))


def slots_in(axis, turn):
    p = lax.axis_index(axis)
    core = lax.axis_index("core") ^ turn
    return jnp.stack([p, p ^ (1 + 2 * core), p ^ (3 - 2 * core), p ^ 2]).astype(jnp.int32)


def widen(block):
    return block.astype(jnp.float32)


def ring_scatter(terms, sent, axis):
    came = exchange(sent, axis, 0)
    passed = (terms[1] + widen(came[1])).astype(sent.dtype)
    return terms[0] + widen(came[0]) + widen(exchange(passed, axis, 1))


def ring_gather(block, axis):
    pair = jnp.stack(lax.optimization_barrier((block, exchange(block, axis, 0))))
    return pair, exchange(pair, axis, 1)


def gathered(block, axis):
    spread = jnp.broadcast_to(block[None], (lax.axis_size(axis),) + block.shape)
    return lax.all_to_all(spread, axis, 0, 0, tiled=True)


def scattered(block, axis):
    return jnp.sum(lax.all_to_all(block, axis, 0, 0, tiled=True).astype(jnp.float32), axis=0)


def edges_of(block, axis, dim):
    count = lax.axis_size(axis)
    forward = [(i, (i + 1) % count) for i in range(count)]
    backward = [(target, source) for source, target in forward]
    size = block.shape[dim]
    low = lax.ppermute(lax.slice_in_dim(block, size - 1, size, axis=dim), axis, forward)
    high = lax.ppermute(lax.slice_in_dim(block, 0, 1, axis=dim), axis, backward)
    return low, high


def widened(block, edges, axis, dim):
    low, high = edges
    index = lax.axis_index(axis)
    low = jnp.where(index == 0, jnp.zeros_like(low), low)
    high = jnp.where(index == lax.axis_size(axis) - 1, jnp.zeros_like(high), high)
    return jnp.concatenate([low, block, high], axis=dim)


def column_shifts(maps):
    edge = jnp.zeros_like(maps[:, :, :1])
    return jnp.stack(
        [
            jnp.concatenate([edge, maps[:, :, :-1]], axis=2),
            maps,
            jnp.concatenate([maps[:, :, 1:], edge], axis=2),
        ]
    )


def lanes(index, half):
    return pl.ds(pl.multiple_of(index * half, half), half)


def assemble(info_ref, parts, kernel_ref, others, sems):
    copies = []
    for pair in range(2):
        for j in range(2):
            slot = 2 * pair + j
            for t in range(4):
                x, y = info_ref[1 + slot], info_ref[5 + t]
                target = kernel_ref.at[x, pl.ds(0, 2), :, y]
                copies.append((parts[pair].at[j, t], target))
                x, y = info_ref[1 + t], info_ref[5 + slot]
                target = kernel_ref.at[x, pl.ds(2, 2), :, y]
                copies.append((parts[2 + pair].at[j, t], target))
    copies = [
        pltpu.make_async_copy(source, target, sems.at[i])
        for i, (source, target) in enumerate(copies)
    ]
    copies += [
        pltpu.make_async_copy(source, target, sems.at[32 + i])
        for i, (source, target) in enumerate(others)
    ]
    for copy in copies:
        copy.start()
    for copy in copies:
        copy.wait()


def add_terms(index, x_ref, cot_ref, kernel_ref, pre_ref, slope_ref, start_ref):
    frames, block, chans = pre_ref.shape
    half = chans // 2

    def convolve(f, _, a):
        if a > 0:
            total = pre_ref[f]
        elif start_ref is not None:
            total = start_ref[f]
        else:
            total = jnp.zeros((block, chans), jnp.float32)
        for b in range(3):
            piece = x_ref[b, f, a : a + 2, :, lanes(index, half)].reshape(block, half)
            total += lax.dot_general(
                piece,
                kernel_ref[a, :, b].reshape(chans, half),
                (((1,), (1,)), ((), ())),
                preferred_element_type=jnp.float32,
            )
        pre_ref[f] = total
        return 0

    def blend(f, _):
        total = jnp.zeros((block, half), jnp.float32)
        for k in range(3):
            piece = cot_ref[2 - k + f].reshape(block, chans)
            kernel = kernel_ref[3, :, k].reshape(chans, half)
            total += jnp.dot(piece, kernel, preferred_element_type=jnp.float32)
        slope_ref[f] = total
        return 0

    for a in range(3):
        lax.fori_loop(0, frames, functools.partial(convolve, a=a), 0)
    lax.fori_loop(0, frames, blend, 0)


def first_kernel(info_ref, x_hbm, cot_hbm, *refs):
    parts, (pre_ref, slope_ref, kernel_ref, x_ref, cot_ref, sems) = refs[:4], refs[4:]
    assemble(info_ref, parts, kernel_ref, ((x_hbm, x_ref), (cot_hbm, cot_ref)), sems)
    add_terms(info_ref[0], x_ref, cot_ref, kernel_ref, pre_ref, slope_ref, None)


def second_kernel(info_ref, x_hbm, cot_hbm, *refs):
    parts, (start_ref, mine_ref), refs = refs[:4], refs[4:6], refs[6:]
    hid_mine_ref, hid_other_ref, slope_ref, turned_ref, kernel_ref = refs[:5]
    pre_ref, other_ref, work_ref, x_ref, cot_ref, sems = refs[5:]
    assemble(info_ref, parts, kernel_ref, ((x_hbm, x_ref), (cot_hbm, cot_ref)), sems)
    other = info_ref[0]
    add_terms(other, x_ref, cot_ref, kernel_ref, pre_ref, other_ref, start_ref)
    frames, block, chans = pre_ref.shape
    half = chans // 2
    part = 96
    for hid_ref, source_ref, index in (
        (hid_mine_ref, mine_ref, 1 - other),
        (hid_other_ref, other_ref, other),
    ):

        def finish(step, _, hid_ref=hid_ref, source_ref=source_ref, index=index):
            f, r = step // (block // part), step % (block // part)
            rows = pl.ds(pl.multiple_of(r * part, part), part)
            pre = pre_ref[f, rows, lanes(index, half)]
            sigma = 1.0 / (1.0 + jnp.exp(-pre))
            hid_ref[f, rows] = (pre * sigma).astype(jnp.bfloat16)
            slope = source_ref[f, rows] * sigma * (1.0 + pre * (1.0 - sigma))
            work_ref[f, rows, lanes(index, half)] = slope
            return 0

        lax.fori_loop(0, frames * (block // part), finish, 0)
    for f in range(frames):
        slope = work_ref[f].astype(jnp.bfloat16)
        slope_ref[f] = slope
        turned_ref[:, f * block : (f + 1) * block] = slope.T


def forward(infos, shifts, cot_pad, parts, parts_other):
    frames, _, width, chans = shifts.shape[1:]
    block = 2 * width
    half = chans // 2
    full = jax.ShapeDtypeStruct((frames, block, chans), jnp.float32)
    part = jax.ShapeDtypeStruct((frames, block, half), jnp.float32)
    hid = jax.ShapeDtypeStruct((frames, block, half), jnp.bfloat16)
    kernel = jax.ShapeDtypeStruct((4, 4, 3, 4) + parts[0].shape[-2:], parts[0].dtype)
    held = [
        pltpu.VMEM(shifts.shape, shifts.dtype),
        pltpu.VMEM(cot_pad.shape, cot_pad.dtype),
        pltpu.SemaphoreType.DMA((34,)),
    ]
    pre, mine, k_mine = pl.pallas_call(
        first_kernel,
        out_shape=(full, part, kernel),
        in_specs=[SMEM] + [ANY] * 6,
        out_specs=(VMEM,) * 3,
        scratch_shapes=held,
        compiler_params=PARAMS,
        cost_estimate=pl.CostEstimate(flops=3200000000, bytes_accessed=12000000, transcendentals=0),
    )(infos[0], shifts, cot_pad, *parts)
    results = pl.pallas_call(
        second_kernel,
        out_shape=(
            hid,
            hid,
            jax.ShapeDtypeStruct((frames, block, chans), jnp.bfloat16),
            jax.ShapeDtypeStruct((chans, frames * block), jnp.bfloat16),
            kernel,
        ),
        in_specs=[SMEM] + [ANY] * 6 + [VMEM] * 2,
        out_specs=(VMEM,) * 5,
        scratch_shapes=[
            pltpu.VMEM(full.shape, jnp.float32),
            pltpu.VMEM(part.shape, jnp.float32),
            pltpu.VMEM(full.shape, jnp.float32),
        ]
        + held,
        compiler_params=PARAMS,
        cost_estimate=pl.CostEstimate(flops=3200000000, bytes_accessed=15000000, transcendentals=0),
    )(infos[1], shifts, cot_pad, *parts_other, pre, mine)
    return k_mine, results


def weight_kernel(
    upper,
    info_ref,
    turned_ref,
    turned_pair_ref,
    x_ref,
    x_pair_ref,
    cot_ref,
    cot_pair_ref,
    hid_ref,
    hid_pair_ref,
    terms_ref,
    sent_ref,
):
    half = x_pair_ref.shape[-1]
    count = turned_ref.shape[1]
    block = count // 2
    own = terms_ref.shape[-2]
    outs = pl.ds(half * upper, half)

    def keep(total, group, b):
        for zh in range(2):
            for y in range(4):
                row = (4 * zh + y) * own
                slots = info_ref[1 + group], info_ref[5 + y]
                slots = slots[::-1] if upper else slots
                terms_ref[slots[0], slots[1], b, zh] = total[row : row + own]

    def spatial(a, _):
        for b in range(3):
            piece = x_ref[b, :, pl.ds(a, 2), :, lanes(info_ref[0], half)].reshape(count, half)
            total = jnp.dot(turned_ref[outs], piece, preferred_element_type=jnp.float32)
            piece = x_pair_ref[b, :, pl.ds(a, 2)].reshape(count, half)
            total += jnp.dot(turned_pair_ref[outs], piece, preferred_element_type=jnp.float32)
            keep(total, a, b)
        return 0

    lax.fori_loop(0, 3, spatial, 0)
    for k in range(3):
        piece = cot_ref[outs, (2 - k) * block : (4 - k) * block]
        total = jnp.dot(piece, hid_ref[...], preferred_element_type=jnp.float32)
        piece = cot_pair_ref[outs, (2 - k) * block : (4 - k) * block]
        total += jnp.dot(piece, hid_pair_ref[...], preferred_element_type=jnp.float32)
        keep(total, 3, k)
    for slot in range(2):
        for i in range(4):
            sent_ref[slot, i] = terms_ref[2 + slot, i].astype(jnp.bfloat16)


def weight_terms(upper, own, info, *operands):
    half = operands[-1].shape[-1]
    shape = (4, 4, 3, 2, own, half)
    return pl.pallas_call(
        functools.partial(weight_kernel, upper),
        out_shape=(
            jax.ShapeDtypeStruct(shape, jnp.float32),
            jax.ShapeDtypeStruct((2,) + shape[1:], jnp.bfloat16),
        ),
        in_specs=[SMEM] + [VMEM] * 8,
        out_specs=(VMEM, VMEM),
        compiler_params=PARAMS,
        cost_estimate=pl.CostEstimate(flops=2400000000, bytes_accessed=16000000, transcendentals=0),
    )(info, *operands)


def grad_kernel(f, info_ref, x_ref, cot_ref, mine_ref, other_ref, *refs):
    out_ref = refs[-1]
    block, chans = out_ref.shape[1:]
    half = chans // 2
    for kernel_ref, index in ((mine_ref, info_ref[0]), (other_ref, 1 - info_ref[0])):

        def convolve(a, _, kernel_ref=kernel_ref, index=index):
            total = out_ref[0, :, lanes(index, half)]
            for b in range(3):
                piece = x_ref[2 - b, f, pl.ds(2 - a, 2)].reshape(block, chans)
                kernel = kernel_ref[a, :, b].reshape(chans, half)
                total += jnp.dot(piece, kernel, preferred_element_type=jnp.float32)
            out_ref[0, :, lanes(index, half)] = total
            return 0

        out_ref[0, :, lanes(index, half)] = cot_ref[f, :, lanes(index, half)].astype(jnp.float32)
        lax.fori_loop(0, 3, convolve, 0)


def input_gradient(f, info, shifts, cotangent, k_mine, k_other, earlier=()):
    frames, rows, width, chans = cotangent.shape
    block = pl.BlockSpec((1, rows * width, chans), lambda i: (f, 0, 0))
    whole = [pl.BlockSpec(memory_space=pltpu.VMEM)] * 4
    return pl.pallas_call(
        functools.partial(grad_kernel, f),
        grid=(1,),
        out_shape=jax.ShapeDtypeStruct((frames, rows * width, chans), jnp.float32),
        in_specs=[SMEM] + whole + [ANY] * len(earlier),
        out_specs=block,
        input_output_aliases={5: 0} if earlier else {},
        compiler_params=PARAMS,
        cost_estimate=pl.CostEstimate(flops=1800000000, bytes_accessed=8000000, transcendentals=0),
    )(info, shifts, cotangent.reshape(frames, rows * width, chans), k_mine, k_other, *earlier)


def kernel_unit(spatial_kernel, temporal_kernel, half):
    both = jnp.concatenate(
        [spatial_kernel.transpose(1, 0, 2), temporal_kernel.transpose(1, 0, 2)], axis=0
    )
    start = (3 * lax.axis_index("x"), 0, lax.axis_index("core") * half)
    unit = lax.dynamic_slice(both, start, (3, both.shape[1], half))
    p = lax.axis_index("zh")
    slots = [unit]
    for k in range(1, 4):
        slots.append(lax.ppermute(unit, "zh", [(i, i ^ k) for i in range(4)]))
    slots = [jnp.where(p & 1, slots[k ^ 1], slots[k]) for k in range(4)]
    slots = [jnp.where(p & 2, slots[k ^ 2], slots[k]) for k in range(4)]
    return jnp.stack(slots[:2]), jnp.stack(slots[2:])


def kernel_parts(unit, waited):
    lower = jnp.concatenate(ring_gather(unit[0], "y"))
    upper = jnp.concatenate(ring_gather(unit[1], "x"))
    lower, lower_rest = ring_gather(lower, "x")
    upper, upper_rest = ring_gather(upper, "y")
    rest, waited = lax.optimization_barrier(((lower_rest, upper_rest), waited))
    mine = (lower, rest[0], upper, rest[1])
    return mine, tuple(swap(part) for part in mine), waited


def per_device(activations, cotangent, spatial_kernel, temporal_kernel):
    frames, rows, width, chans = activations.shape
    count = frames * rows * width
    half = chans // 2
    core = lax.axis_index("core").astype(jnp.int32).reshape(1)
    own = spatial_kernel.shape[0]
    infos = [
        jnp.concatenate([core ^ turn, slots_in("x", turn), slots_in("y", turn)])
        for turn in range(2)
    ]

    unit = kernel_unit(spatial_kernel, temporal_kernel, half)
    x_wide = widened(activations, edges_of(activations, SPACE, 1), SPACE, 1)
    cot_pad = widened(cotangent, edges_of(cotangent, TM, 0), TM, 0)
    x_pair = swap(lax.dynamic_slice_in_dim(x_wide, (1 - core[0]) * half, half, axis=3))
    shifts = column_shifts(x_wide)
    cot_turned = cot_pad.reshape((frames + 2) * rows * width, chans).T
    waited = (shifts, cot_pad, cot_turned, x_pair)
    parts, parts_other, waited = kernel_parts(unit, waited)
    shifts, cot_pad, cot_turned, x_pair = waited
    cot_turned_pair = swap(cot_turned)
    cot_turned_pair, parts_other = lax.optimization_barrier((cot_turned_pair, parts_other))

    k_mine, results = forward(infos, shifts, cot_pad, parts, parts_other)
    hid_mine, hid_other, slope_pre, turned, k_other = results
    turned_pair, hid_pair = swap(turned), swap(hid_other)
    x_pair, _ = lax.optimization_barrier((x_pair, turned))
    shifts_pair = column_shifts(x_pair)
    slope_maps = slope_pre.reshape(frames, rows, width, chans)
    operands = (
        turned,
        turned_pair,
        shifts,
        shifts_pair,
        cot_turned,
        cot_turned_pair,
        hid_mine.reshape(count, half),
        hid_pair.reshape(count, half),
    )
    info = jnp.concatenate([core, slots_of("x"), slots_of("y")])
    lower, sent_lower = weight_terms(0, own, info, *operands)
    upper, sent_upper = weight_terms(1, own, info, *operands)

    came_lower = exchange(sent_lower, "x", 0)
    came_upper = exchange(sent_upper, "y", 0)
    passed = (lower[1] + widen(came_lower[1])).astype(jnp.bfloat16)
    last_lower = exchange(passed, "x", 1)
    slope_maps, _ = lax.optimization_barrier((slope_maps, passed))
    slope_edges = edges_of(slope_maps, SPACE, 1)
    slope_wide = widened(slope_maps, slope_edges, SPACE, 1)
    shifts_slope = column_shifts(slope_wide)
    passed = (upper[1] + widen(came_upper[1])).astype(jnp.bfloat16)
    last_upper = exchange(passed, "y", 1)
    info, _ = lax.optimization_barrier((core, passed))
    grad = input_gradient(0, info, shifts_slope, cotangent, k_mine, k_other)
    grad = input_gradient(1, info, shifts_slope, cotangent, k_mine, k_other, (grad,))
    last_lower, grad = lax.optimization_barrier((last_lower, grad))

    def total(terms, came, last, slots):
        return terms[0, slots] + widen(came[0, slots]) + widen(last[slots])

    keep, send = slice(0, 2), slice(2, 4)
    sent_lower = total(lower, came_lower, last_lower, send)
    sent_upper = total(upper, came_upper, last_upper, send)
    lower = ring_scatter(total(lower, came_lower, last_lower, keep), sent_lower, "y")
    upper = ring_scatter(total(upper, came_upper, last_upper, keep), sent_upper, "x")
    terms = jnp.concatenate([lower, upper], axis=1)
    terms = terms.reshape(3, 4, 2, own // 2, half).transpose(1, 2, 0, 3, 4)
    terms = terms.reshape(8, 3, own // 2, half).astype(jnp.bfloat16)

    terms = lax.all_to_all(terms, ("zh", "zl"), 0, 0, tiled=True)
    pixels = count * lax.axis_size(TM) * lax.axis_size(SPACE)
    terms = jnp.sum(widen(terms), axis=0) * (1.0 / math.sqrt(pixels))
    terms = gathered(terms, ("x", "zl"))
    came = swap(terms)
    terms = jnp.concatenate(
        [jnp.where(core[0] == 0, terms, came), jnp.where(core[0] == 0, came, terms)], axis=3
    )
    terms = terms.reshape(4, 2, 3, own // 2, chans).transpose(0, 2, 1, 3, 4)
    spatial = terms[:3].reshape(9, own, chans).transpose(1, 0, 2)
    temporal = terms[3].reshape(3, own, chans).transpose(1, 0, 2)
    return grad.reshape(frames, rows, width, chans), spatial, temporal


def solution(mesh):
    split = Mesh(mesh.devices.reshape(4, 2, 2, 4, 4), TM + SPACE)
    maps = P(TM, SPACE, None, None)
    kernels = P(SPACE, None, None)
    return jax.shard_map(
        per_device,
        mesh=split,
        in_specs=(maps, maps, kernels, kernels),
        out_specs=(maps, kernels, kernels),
        check_vma=False,
    )
```
